32 devices in a mesh: space: 8 (over z, y), tm: 4 (over x, core).
Axes of the slice: x: 2, y: 2, z: 4, core: 2. Of those that a mesh axis runs over, the one named last changes fastest.
Arguments:
- velocity: float32 [4, 3, 3, 128, 128, 128], P('tm', None, None, 'space'), may hold values from -6 to 6
Outputs:
- new_velocity: float32 [4, 3, 3, 128, 128, 128], P('tm', None, None, 'space')
- new_rhs: bfloat16 [4, 3, 3, 128, 128, 128], P('tm', None, None, 'space')
The draws below stay inside these ranges and needn't reach their ends.
All inputs are finite; a program needn't handle non-finite values.
Results may differ from the reference program's by a relative error of at most 0.001.
Values sent between devices are 32-bit elements; how exact they have to be, the bound alone decides.
No kernel may reach another device: no remote copies, remote signals or barrier semaphores. Data moves between devices by JAX's collectives and lax.ppermute only.
A program may use at most 192 MiB of HBM per device.

```python
import math
import jax
import jax.numpy as jnp

NX = 128
FY = 128
FZ = 128
INTERVALS = 4


def level_of(key, shape, shards, least, top_value):
    def one(dim, blocks):
        draws = jax.random.uniform(jax.random.fold_in(jax.random.fold_in(key, 6), dim), (blocks,), jnp.float32, least / len(shards), top_value / len(shards))
        return jnp.repeat(jnp.exp(draws), shape[dim] // blocks).reshape((-1,) + (1,) * (len(shape) - dim - 1))

    loudness = one(*shards[0])
    for cut in shards[1:]:
        loudness = loudness * one(*cut)
    return loudness


def normal_values(stream_key, shape, width, reach, cuts=(), kind=jnp.bfloat16):
    array = jax.random.normal(stream_key, shape, jnp.float32) * width
    if len(cuts) > 0:
        array = level_of(stream_key, shape, cuts, -0.22, 0.18) * array
    return jnp.clip(array, min=-reach, max=reach).astype(kind)


def setup_inputs(seed: int = 0) -> dict:
    arg_keys = jax.random.split(jax.random.key(seed), 2)
    return {
        "velocity": normal_values(arg_keys[0], (INTERVALS, 3, 3, NX, FY, FZ), 1.0, 6.0, ((0, 4), (3, 8)), jnp.float32),
    }


viscosity = 1.0
coarse_viscosity = 10.0
time_step = 0.3
weights_first = (5.0 / 24.0, 1.0 / 3.0, -1.0 / 24.0)
weights_second = (-1.0 / 24.0, 1.0 / 3.0, 5.0 / 24.0)


def advection_laplace(stacked, spacing):
    advect = jnp.zeros_like(stacked)
    laplace = -6.0 * stacked
    for direction in range(3):
        axis_pos = stacked.ndim - 3 + direction
        forward_cell = jnp.roll(stacked, -1, axis_pos)
        backward_cell = jnp.roll(stacked, 1, axis_pos)
        advect = advect - stacked[:, direction:direction + 1] * ((forward_cell - backward_cell) / (2.0 * spacing))
        laplace = laplace + forward_cell + backward_cell
    return advect, laplace / (spacing * spacing)


def fine_rhs(stacked):
    advect, laplace = advection_laplace(stacked, 1.0)
    return advect + viscosity * laplace


def integrate(stacked, weights):
    return time_step * (weights[0] * stacked[0] + weights[1] * stacked[1] + weights[2] * stacked[2])


def restrict(stacked):
    dims = stacked.shape
    blocks = stacked.reshape(dims[:-3] + (dims[-3] // 2, 2, dims[-2] // 2, 2, dims[-1] // 2, 2))
    return jnp.mean(blocks, axis=(-5, -3, -1))


def refine_axis(coarse, axis_pos, following):
    middle = 0.5 * (coarse + following)
    paired = jnp.stack([coarse, middle], axis=axis_pos + 1)
    dims = list(coarse.shape)
    dims[axis_pos] = 2 * dims[axis_pos]
    return paired.reshape(tuple(dims))


def refine(coarse):
    result = coarse
    for direction in range(3):
        axis_pos = coarse.ndim - 3 + direction
        result = refine_axis(result, axis_pos, jnp.roll(result, -1, axis_pos))
    return result


def spectral_denominator(size_x, size_y, size_z):
    wave_x = jnp.sin(jnp.arange(size_x) * (math.pi / size_x)) ** 2
    wave_y = jnp.sin(jnp.arange(size_y) * (math.pi / size_y)) ** 2
    wave_z = jnp.sin(jnp.arange(size_z) * (math.pi / size_z)) ** 2
    total = wave_x[:, None, None] + wave_y[None, :, None] + wave_z[None, None, :]
    return 1.0 + 0.5 * time_step * coarse_viscosity * (4.0 / (2.0 * 2.0)) * total


def reference(velocity):
    count = velocity.shape[0]
    half_step = 0.5 * time_step
    denominator = spectral_denominator(velocity.shape[3] // 2, velocity.shape[4] // 2, velocity.shape[5] // 2)
    new_list = []
    rhs_list = []
    carried_fine = velocity[0, 0]
    carried_coarse = None
    for interval in range(count):
        nodes = velocity[interval]
        old_rhs = fine_rhs(nodes)
        sweep_first = nodes[0] + integrate(old_rhs, weights_first)
        rhs_first = fine_rhs(sweep_first[None])[0]
        sweep_last = sweep_first + half_step * (rhs_first - old_rhs[1]) + integrate(old_rhs, weights_second)
        rhs_last = fine_rhs(sweep_last[None])[0]
        swept = jnp.stack([nodes[0], sweep_first, sweep_last])
        fresh_rhs = jnp.stack([old_rhs[0], rhs_first, rhs_last])
        coarse = restrict(swept)
        coarse_lap = advection_laplace(coarse[1:], 2.0)[1]
        sources = restrict(jnp.stack([integrate(fresh_rhs, weights_first), integrate(fresh_rhs, weights_second)])) - half_step * coarse_viscosity * coarse_lap
        source_hat = jnp.fft.fftn(sources, axes=(2, 3, 4))
        if interval == 0:
            start_hat = jnp.fft.fftn(coarse[0], axes=(1, 2, 3))
        else:
            start_hat = carried_coarse
        middle_hat = (start_hat + source_hat[0]) / denominator
        last_hat = (middle_hat + source_hat[1]) / denominator
        carried_coarse = last_hat
        physical = jnp.fft.ifftn(jnp.stack([middle_hat, last_hat]), axes=(2, 3, 4)).real
        refined = refine(physical - coarse[1:])
        corrected = swept[1:] + refined
        if interval == 0:
            first_node = nodes[0]
        else:
            first_node = carried_fine
        carried_fine = corrected[1]
        new_nodes = jnp.stack([first_node, corrected[0], corrected[1]])
        new_list.append(new_nodes)
        rhs_list.append(fine_rhs(new_nodes).astype(jnp.bfloat16))
    return jnp.stack(new_list), jnp.stack(rhs_list)
```

```python
import functools

import jax
import jax.numpy as jnp
import ml_dtypes
import numpy as np
from jax import lax
from jax.experimental import pallas as pl
from jax.experimental.pallas import tpu as pltpu
from jax.sharding import PartitionSpec as P

viscosity = 1.0
coarse_viscosity = 10.0
time_step = 0.3
weights_first = (5.0 / 24.0, 1.0 / 3.0, -1.0 / 24.0)
weights_second = (-1.0 / 24.0, 1.0 / 3.0, 5.0 / 24.0)
half_step = 0.5 * time_step
first = tuple(time_step * w for w in weights_first)
second = tuple(time_step * w for w in weights_second)
lanes = 128
pad = 8
rows_at_once = 32
params = pltpu.CompilerParams(vmem_limit_bytes=50 * 1024 * 1024)
f32 = jnp.float32
bf16 = jnp.bfloat16


def round_up(value, multiple):
    return -(-value // multiple) * multiple


def frequencies(length):
    index = np.arange(length)
    return np.where(index <= length // 2, index, index - length // 2)


def basis(length):
    index = np.arange(length)
    waves = frequencies(length)
    angles = 2.0 * np.pi * (waves[:, None] * index[None, :] % length) / length
    table = np.where(index[:, None] <= length // 2, np.cos(angles), np.sin(angles))
    edge = (waves == 0) | (2 * waves == length)
    return table * np.sqrt(np.where(edge, 1.0, 2.0) / length)[:, None]


def wave_squares(length):
    return np.sin(np.pi * frequencies(length) / length) ** 2


def refine_matrix(length):
    table = np.zeros((2 * length, length))
    for i in range(length):
        table[2 * i, i] += 1.0
        table[2 * i + 1, i] += 0.5
        table[2 * i + 1, (i + 1) % length] += 0.5
    return table


def pair_matrix(length):
    return np.repeat(np.eye(length), 2, axis=0)


def split(table):
    high = table.astype(np.float32).astype(ml_dtypes.bfloat16)
    low = (table - high.astype(np.float64)).astype(np.float32).astype(ml_dtypes.bfloat16)
    return high, low


def left_table(table):
    high, low = split(table)
    return np.concatenate([high, low, high], axis=1)


def right_table(table):
    high, low = split(table)
    return np.concatenate([high, low, high], axis=0)


def split_value(value):
    high = value.astype(bf16)
    return high, (value - high.astype(f32)).astype(bf16)


def left_dot(table, value):
    high, low = split_value(value)
    return jnp.dot(table, jnp.concatenate([high, high, low], axis=0), preferred_element_type=f32)


def right_dot(value, table):
    high, low = split_value(value)
    return jnp.dot(
        jnp.concatenate([high, high, low], axis=1), table, preferred_element_type=f32
    )


def wrap_rows(ref, plane, count):
    size = ref.shape[2] - 2 * pad
    for field in range(count):
        ref[field, plane, pad - 1 : pad, :] = ref[field, plane, pad + size - 1 : pad + size, :]
        ref[field, plane, pad + size : pad + size + 1, :] = ref[field, plane, pad : pad + 1, :]


def rhs_rows(ref, base, plane, start):
    stop = start + rows_at_once
    center = [ref[base + c, plane, start:stop, :] for c in range(3)]
    size = ref.shape[3]
    results = []
    for c in range(3):
        x_up = ref[base + c, plane + 1, start:stop, :]
        x_down = ref[base + c, plane - 1, start:stop, :]
        y_up = ref[base + c, plane, start + 1 : stop + 1, :]
        y_down = ref[base + c, plane, start - 1 : stop - 1, :]
        z_up = pltpu.roll(center[c], size - 1, 1)
        z_down = pltpu.roll(center[c], 1, 1)
        advect = (
            center[0] * (x_up - x_down) + center[1] * (y_up - y_down) + center[2] * (z_up - z_down)
        )
        laplace = (x_up + x_down) + (y_up + y_down) + (z_up + z_down) - 6.0 * center[c]
        results.append(viscosity * laplace - 0.5 * advect)
    return center, results


def planes_in(source, low, high, held, sems):
    length = source.shape[1]
    size = source.shape[2]
    rows = pl.ds(pad, size)

    def inner(plane):
        return pltpu.make_async_copy(
            source.at[:, plane], held.at[:, plane + 1, rows, :], sems.at[plane]
        )

    below = pltpu.make_async_copy(low, held.at[:, 0, rows, :], sems.at[length])
    above = pltpu.make_async_copy(high, held.at[:, length + 1, rows, :], sems.at[length + 1])
    return inner, below, above


def arrive(step, source, low, high, held, sems):
    length = source.shape[1]
    count = source.shape[0]
    inner, below, above = planes_in(source, low, high, held, sems)

    @pl.when(step == 0)
    def _():
        below.start()

        def launch(plane, carry):
            inner(plane).start()
            return carry

        lax.fori_loop(0, length, launch, 0)
        above.start()
        below.wait()
        inner(0).wait()
        wrap_rows(held, 1, count)

    inner(2 * step + 1).wait()
    wrap_rows(held, 2 * step + 2, count)

    @pl.when(2 * step + 2 < length)
    def _():
        inner(2 * step + 2).wait()
        wrap_rows(held, 2 * step + 3, count)

    @pl.when(2 * step + 2 >= length)
    def _():
        above.wait()


def chunks(size):
    return range(0, size, rows_at_once)


def spectral(pairs, z_table, y_table, count):
    size = pairs.shape[1]
    half = size // 2
    summed = [
        pairs[k, pl.ds(0, half, 2), :] + pairs[k, pl.ds(1, half, 2), :] for k in range(count)
    ]
    couples = []
    for k in range(0, count, 2):
        other = summed[min(k + 1, count - 1)]
        couples.append(jnp.concatenate([summed[k], other], axis=1))
    in_z = right_dot(jnp.concatenate(couples, axis=0), z_table)
    in_z = [in_z[k * half : (k + 1) * half] for k in range(len(couples))]
    in_y = left_dot(y_table, jnp.concatenate(in_z, axis=1))
    blocks = half // 2
    lane = lax.broadcasted_iota(jnp.int32, (blocks, lanes), 1)
    results = []
    for k in range(count):
        both = in_y[:, (k // 2) * lanes : (k // 2 + 1) * lanes]
        upper, lower = both[:blocks], both[blocks:]
        if k % 2 == 0:
            results.append(jnp.where(lane < lanes // 2, upper, pltpu.roll(lower, lanes // 2, 1)))
        else:
            results.append(jnp.where(lane < lanes // 2, pltpu.roll(upper, lanes // 2, 1), lower))
    return results


def sweep_one_kernel(is_first, source, low, high, s1, w, u, v, held, sems):
    step = pl.program_id(0)
    size = source.shape[2]
    arrive(step, source, low, high, held, sems)
    for row in chunks(size):
        rows = slice(row, row + rows_at_once)
        for part in range(2):
            plane = 2 * step + part + 1
            total_first, total_second, start, initial = None, None, None, None
            for node in range(3):
                center, old = rhs_rows(held, 3 * node, plane, pad + row)
                a, b = first[node], second[node] - (half_step if node == 1 else 0.0)
                if node == 0:
                    start, initial = center, old
                    total_first = [start[c] + a * old[c] for c in range(3)]
                    total_second = [b * old[c] for c in range(3)]
                else:
                    total_first = [total_first[c] + a * old[c] for c in range(3)]
                    total_second = [total_second[c] + b * old[c] for c in range(3)]
                if node == 0:
                    for c in range(3):
                        mine = first[0] * old[c] + is_first[0] * start[c]
                        other = second[0] * old[c]
                        if part == 1:
                            mine = mine + u[c, 0, rows, :]
                            other = other + v[c, 0, rows, :]
                        u[c, 0, rows, :] = mine
                        v[c, 0, rows, :] = other
            for c in range(3):
                s1[c, part, rows, :] = total_first[c]
                w[c, part, rows, :] = total_first[c] + total_second[c]
                u[c, 0, rows, :] = u[c, 0, rows, :] - total_first[c]
                v[c, 0, rows, :] = v[c, 0, rows, :] + total_first[c]


def sweep_two_kernel(
    group, source, low, high, w, u, v, z_table, y_table, s2, u_out, v_out, g, held, pairs, sems
):
    step = pl.program_id(0)
    size = source.shape[2]
    arrive(step, source, low, high, held, sems)
    for row in chunks(size):
        rows = slice(row, row + rows_at_once)
        fresh_sum, sweep_sum = None, None
        for part in range(2):
            _, fresh = rhs_rows(held, 0, 2 * step + part + 1, pad + row)
            swept = [w[c, part, rows, :] + half_step * fresh[c] for c in range(3)]
            for c in range(3):
                s2[c, part, rows, :] = swept[c]
            if part == 0:
                fresh_sum, sweep_sum = fresh, swept
            else:
                fresh_sum = [fresh_sum[c] + fresh[c] for c in range(3)]
                sweep_sum = [sweep_sum[c] + swept[c] for c in range(3)]
        for c in range(3):
            u_out[c, 0, rows, :] = u[c, 0, rows, :] + first[1] * fresh_sum[c]
            v_out[c, 0, rows, :] = v[c, 0, rows, :] + second[1] * fresh_sum[c] - sweep_sum[c]
            pairs[c, rows, :] = sweep_sum[c]
    planes = source.shape[1] // 2
    blocks = g.shape[0] // group
    for c, value in enumerate(spectral(pairs, z_table[...], y_table[...], 3)):
        g[pl.ds(c * planes + step, blocks, group), :] = value


def source_kernel(
    group, g_group, source, low, high, u, v, g, z_table, y_table, out, held, pairs, sems
):
    step = pl.program_id(0)
    size = source.shape[2]
    arrive(step, source, low, high, held, sems)
    for row in chunks(size):
        rows = slice(row, row + rows_at_once)
        _, fresh = rhs_rows(held, 0, 2 * step + 1, pad + row)
        _, other = rhs_rows(held, 0, 2 * step + 2, pad + row)
        for c in range(3):
            total = fresh[c] + other[c]
            pairs[c, rows, :] = u[c, 0, rows, :] + first[2] * total
            pairs[3 + c, rows, :] = v[c, 0, rows, :] + second[2] * total
    planes = source.shape[1] // 2
    blocks = out.shape[0] // group
    for k, value in enumerate(spectral(pairs, z_table[...], y_table[...], 6)):
        if k < 3:
            value = value + g[pl.ds(k * planes + step, blocks, g_group), :]
        out[pl.ds(k * planes + step, blocks, group), :] = value


def solve_kernel(peers, intervals, planes, group, back, values, inverse, forward, backward, out):
    start = [None] * 3
    for interval in range(intervals):
        loaded = []
        for field in range(6):
            parts = [
                values[
                    pl.ds(interval * group + field * planes + p, peers, intervals * group), :
                ]
                for p in range(planes)
            ]
            loaded.append(jnp.concatenate(parts, axis=0))
        spectra = left_dot(forward[...], jnp.concatenate(loaded, axis=1))
        rates = inverse[...]
        wanted = []
        for field in range(6):
            c = field % 3
            value = spectra[:, field * lanes : (field + 1) * lanes]
            if start[c] is not None:
                value = value + start[c]
            start[c] = value * rates
            wanted.append(start[c])
        physical = left_dot(backward[...], jnp.concatenate(wanted, axis=1))
        for field in range(6):
            base = (field // 3) * (back // 2) + (field % 3) * (planes + 2)
            for e in range(planes + 2):
                out[pl.ds(interval * back + base + e, peers, intervals * back), :] = physical[
                    e * peers : (e + 1) * peers, field * lanes : (field + 1) * lanes
                ]


def corrected_kernel(
    nodes, group, *refs
):
    count = 3 * len(nodes)
    spectra, z_table, y_table = refs[:3]
    fields = [refs[3 + 3 * k : 6 + 3 * k] for k in range(len(nodes))]
    new_velocity, new_rhs, held, coarse, result, sems, out_sems, rhs_sems = refs[-8:]
    length = fields[0][0].shape[1]
    size = fields[0][0].shape[2]
    planes = length // 2
    rows_all = pl.ds(pad, size)
    inner_copies, edge_copies = [], []
    for k, (source, low, high) in enumerate(fields):
        place = held.at[3 * k : 3 * k + 3]
        edge_copies.append(
            pltpu.make_async_copy(low, place.at[:, 0, rows_all, :], sems.at[k, length])
        )
        edge_copies.append(
            pltpu.make_async_copy(high, place.at[:, length + 1, rows_all, :], sems.at[k, length + 1])
        )
        for plane in range(length):
            inner_copies.append(
                pltpu.make_async_copy(
                    source.at[:, plane], place.at[:, plane + 1, rows_all, :], sems.at[k, plane]
                )
            )
    for copy in edge_copies + inner_copies:
        copy.start()
    blocks = spectra.shape[0] // group
    for k in range(len(nodes)):
        for c in range(3):
            base = k * (group // len(nodes)) + c * (planes + 2)
            parts = [spectra[pl.ds(base + e, blocks, group), :] for e in range(planes + 2)]
            in_z = right_dot(jnp.concatenate(parts, axis=0), z_table[...])
            for e in range(planes + 2):
                mine = in_z[e * blocks : (e + 1) * blocks]
                stacked = jnp.concatenate([mine[:, :size], mine[:, size:]], axis=0)
                coarse[3 * k + c, e] = left_dot(y_table[...], stacked)
    for copy in edge_copies + inner_copies:
        copy.wait()

    def out_copy(k, plane):
        return pltpu.make_async_copy(
            held.at[3 * k : 3 * k + 3, plane + 1, rows_all, :],
            new_velocity.at[nodes[k], :, plane],
            out_sems.at[k, plane],
        )

    def rhs_copy(k, plane):
        return pltpu.make_async_copy(
            result.at[3 * k : 3 * k + 3, plane],
            new_rhs.at[nodes[k], :, plane],
            rhs_sems.at[k, plane],
        )

    def correct(plane, cell, odd):
        for field in range(count):
            for row in chunks(size):
                rows = slice(row, row + rows_at_once)
                held_rows = slice(pad + row, pad + row + rows_at_once)
                value = coarse[field, cell, rows, :]
                if odd:
                    value = 0.5 * (value + coarse[field, cell + 1, rows, :])
                held[field, plane, held_rows, :] = held[field, plane, held_rows, :] + value
        wrap_rows(held, plane, count)

    correct(0, 0, True)
    correct(1, 1, False)
    for k in range(len(nodes)):
        out_copy(k, 0).start()

    def body(q, carry):
        correct(2 * q + 2, q + 1, True)
        correct(2 * q + 3, q + 2, False)
        for k in range(len(nodes)):
            out_copy(k, 2 * q + 1).start()

            @pl.when(2 * q + 2 < length)
            def _():
                out_copy(k, 2 * q + 2).start()

        for part in range(2):
            plane = 2 * q + part
            for k in range(len(nodes)):
                for row in chunks(size):
                    _, fresh = rhs_rows(held, 3 * k, plane + 1, pad + row)
                    for c in range(3):
                        result[3 * k + c, plane, row : row + rows_at_once, :] = fresh[c].astype(bf16)
                rhs_copy(k, plane).start()
        return carry

    lax.fori_loop(0, planes, body, 0)

    def finish(plane, carry):
        for k in range(len(nodes)):
            out_copy(k, plane).wait()
            rhs_copy(k, plane).wait()
        return carry

    lax.fori_loop(0, length, finish, 0)


anywhere = pl.BlockSpec(memory_space=pl.ANY)


def whole(shape):
    return pl.BlockSpec(shape, lambda *index: (0,) * len(shape))


def struct(shape, dtype=f32):
    return jax.ShapeDtypeStruct(shape, dtype)


def slab(shape):
    return pl.BlockSpec(shape, lambda q: (0, q, 0, 0))


def held_planes(count, length, size_y, size_z):
    return pltpu.VMEM((count, length + 2, size_y + 2 * pad, size_z), f32)


def neighbours(low_plane, high_plane):
    count = lax.axis_size("space")
    up = [(i, (i + 1) % count) for i in range(count)]
    down = [(j, i) for i, j in up]
    return lax.ppermute(high_plane, "space", up), lax.ppermute(low_plane, "space", down)


def later_interval(value):
    count = lax.axis_size("tm")
    return lax.ppermute(value, "tm", [(i, i + 1) for i in range(count - 1)])


def corrected(nodes, spectra, tables, fields, outs):
    length, size_y, size_z = fields[0][0].shape[1:]
    count = 3 * len(nodes)
    planes = length // 2
    group = spectra.shape[1]
    operands = [spectra.reshape(-1, lanes), *tables]
    for field in fields:
        operands.extend(field)
    specs = [whole(o.shape) for o in operands[:3]] + [anywhere] * (len(operands) - 3)
    shape = (3, 3, length, size_y, size_z)
    aliases = {}
    if outs is not None:
        aliases = {len(operands): 0, len(operands) + 1: 1}
        operands.extend(outs)
        specs += [anywhere] * 2
    return pl.pallas_call(
        functools.partial(corrected_kernel, nodes, group),
        out_shape=(struct(shape), struct(shape, bf16)),
        in_specs=specs,
        out_specs=(anywhere, anywhere),
        input_output_aliases=aliases,
        scratch_shapes=[
            held_planes(count, length, size_y, size_z),
            pltpu.VMEM((count, planes + 2, size_y, size_z), f32),
            pltpu.VMEM((count, length, size_y, size_z), bf16),
            pltpu.SemaphoreType.DMA((len(nodes), length + 2)),
            pltpu.SemaphoreType.DMA((len(nodes), length)),
            pltpu.SemaphoreType.DMA((len(nodes), length)),
        ],
        compiler_params=params,
        name="corrected",
    )(*operands)


def per_device(velocity):
    length, size_y, size_z = velocity.shape[3:]
    planes = length // 2
    peers, intervals = lax.axis_size("space"), lax.axis_size("tm")
    devices = peers * intervals
    coarse_x, coarse_y, coarse_z = peers * planes, size_y // 2, size_z // 2
    blocks = coarse_y * coarse_z // lanes
    per_block = devices // blocks
    columns = lanes // per_block
    device = lax.axis_index("space") * intervals + lax.axis_index("tm")
    tm_first = lax.axis_index("tm") == 0
    fields = velocity.reshape(9, length, size_y, size_z)

    x_basis, y_basis, z_basis = basis(coarse_x), basis(coarse_y), basis(coarse_z)
    z_forward = 0.25 * pair_matrix(coarse_z) @ z_basis.T
    z_table = right_table(np.kron(np.eye(2), z_forward))
    y_table = left_table(0.5 * y_basis)
    order = np.arange(coarse_x).reshape(peers, planes).T.reshape(-1)
    x_forward = left_table(x_basis[:, order])
    wanted_x = np.arange(peers)[None, :] * planes + np.arange(-1, planes + 1)[:, None]
    x_backward = left_table(x_basis.T[wanted_x.reshape(-1) % coarse_x])
    z_back = (refine_matrix(coarse_z) @ z_basis.T).T
    z_back_table = right_table(np.kron(np.eye(2), z_back))
    y_back_table = left_table(refine_matrix(coarse_y) @ y_basis.T)
    y_of = np.arange(2)[:, None] * blocks + np.arange(blocks)[None, :]
    waves = wave_squares(coarse_y)[y_of.T][:, :, None] + wave_squares(coarse_z)[None, None, :]
    waves = waves.reshape(devices, columns)
    waves = np.pad(waves, ((0, 0), (0, lanes - columns)))
    mine = lax.dynamic_slice_in_dim(jnp.asarray(waves, f32), device, 1, axis=0)
    total = jnp.asarray(wave_squares(coarse_x), f32)[:, None] + mine
    rates = 1.0 / (1.0 + half_step * coarse_viscosity * (4.0 / (2.0 * 2.0)) * total)

    low, high = neighbours(fields[:, 0], fields[:, length - 1])
    fine = (3, length, size_y, size_z)
    halved = (3, planes, size_y, size_z)
    two = (3, 2, size_y, size_z)
    one = (3, 1, size_y, size_z)
    in_sems = pltpu.SemaphoreType.DMA((length + 2,))
    swept_1, w, u, v = pl.pallas_call(
        sweep_one_kernel,
        grid=(planes,),
        out_shape=(struct(fine), struct(fine), struct(halved), struct(halved)),
        in_specs=[pl.BlockSpec(memory_space=pltpu.SMEM), anywhere, anywhere, anywhere],
        out_specs=(slab(two), slab(two), slab(one), slab(one)),
        scratch_shapes=[held_planes(9, length, size_y, size_z), in_sems],
        compiler_params=params,
        name="sweep_one",
    )(tm_first.astype(f32).reshape(1), fields, low, high)
    low_1, high_1 = neighbours(swept_1[:, 0], swept_1[:, length - 1])

    g_group = round_up(3 * planes, 8)
    swept_2, u, v, g = pl.pallas_call(
        functools.partial(sweep_two_kernel, g_group),
        grid=(planes,),
        out_shape=(struct(fine), struct(halved), struct(halved), struct((blocks * g_group, lanes))),
        in_specs=[anywhere, anywhere, anywhere, slab(two), slab(one), slab(one)]
        + [whole(z_table.shape), whole(y_table.shape)],
        out_specs=(slab(two), slab(one), slab(one), whole((blocks * g_group, lanes))),
        scratch_shapes=[
            held_planes(3, length, size_y, size_z),
            pltpu.VMEM((3, size_y, size_z), f32),
            in_sems,
        ],
        compiler_params=params,
        name="sweep_two",
    )(swept_1, low_1, high_1, w, u, v, z_table, y_table)
    low_2, high_2 = neighbours(swept_2[:, 0], swept_2[:, length - 1])
    g = later_interval(g)

    group = round_up(6 * planes, 8)
    sources = pl.pallas_call(
        functools.partial(source_kernel, group, g_group),
        grid=(planes,),
        out_shape=struct((blocks * group, lanes)),
        in_specs=[anywhere, anywhere, anywhere, slab(one), slab(one), whole(g.shape)]
        + [whole(z_table.shape), whole(y_table.shape)],
        out_specs=whole((blocks * group, lanes)),
        scratch_shapes=[
            held_planes(3, length, size_y, size_z),
            pltpu.VMEM((6, size_y, size_z), f32),
            in_sems,
        ],
        compiler_params=params,
        name="sources",
    )(swept_2, low_2, high_2, u, v, g, z_table, y_table)
    carried = later_interval(swept_2)
    carried_low = later_interval(low_2)
    carried_high = later_interval(high_2)

    both = ("space", "tm")

    def to_columns(value, rows):
        if per_block > 1:
            value = value.reshape(blocks, rows, per_block, columns).swapaxes(1, 2)
        value = value.reshape(devices, rows, columns)
        value = lax.all_to_all(value, both, split_axis=0, concat_axis=0, tiled=True)
        value = jnp.pad(value, ((0, 0), (0, 0), (0, lanes - columns)))
        return value.reshape(devices * rows, lanes)

    def to_planes(value, rows):
        value = value.reshape(devices, rows, lanes)[:, :, :columns]
        value = lax.all_to_all(value, both, split_axis=0, concat_axis=0, tiled=True)
        if per_block > 1:
            value = value.reshape(blocks, per_block, rows, columns).swapaxes(1, 2)
        return value.reshape(blocks, rows, lanes)

    back = 2 * round_up(3 * (planes + 2), 8)
    solved = pl.pallas_call(
        functools.partial(solve_kernel, peers, intervals, planes, group, back),
        out_shape=struct((devices * back, lanes)),
        compiler_params=params,
        name="solve",
    )(to_columns(sources, group), rates, x_forward, x_backward)
    spectra = to_planes(solved, back)
    carried_spectra = later_interval(spectra[:, back // 2 :])

    outs = corrected(
        (1, 2),
        spectra,
        (z_back_table, y_back_table),
        ((swept_1, low_1, high_1), (swept_2, low_2, high_2)),
        None,
    )
    new_velocity, new_rhs = corrected(
        (0,),
        carried_spectra,
        (z_back_table, y_back_table),
        (
            (
                jnp.where(tm_first, fields[:3], carried),
                jnp.where(tm_first, low[:3], carried_low),
                jnp.where(tm_first, high[:3], carried_high),
            ),
        ),
        outs,
    )
    return (new_velocity[None], new_rhs[None])


def solution(mesh):
    placed = P("tm", None, None, "space", None, None)
    return jax.shard_map(
        per_device,
        mesh=mesh,
        in_specs=(placed,),
        out_specs=(placed, placed),
        check_vma=False,
    )
```

```python
import functools

import jax
import jax.numpy as jnp
import ml_dtypes
import numpy as np
from jax import lax
from jax.experimental import pallas as pl
from jax.experimental.pallas import tpu as pltpu
from jax.sharding import PartitionSpec as P

viscosity = 1.0
coarse_viscosity = 10.0
time_step = 0.3
weights_first = (5.0 / 24.0, 1.0 / 3.0, -1.0 / 24.0)
weights_second = (-1.0 / 24.0, 1.0 / 3.0, 5.0 / 24.0)
half_step = 0.5 * time_step
first = tuple(time_step * w for w in weights_first)
second = tuple(time_step * w for w in weights_second)
lanes = 128
pad = 8
rows_at_once = 32
params = pltpu.CompilerParams(vmem_limit_bytes=50 * 1024 * 1024)
f32 = jnp.float32
bf16 = jnp.bfloat16


def round_up(value, multiple):
    return -(-value // multiple) * multiple


def frequencies(length):
    index = np.arange(length)
    return np.where(index <= length // 2, index, index - length // 2)


def basis(length):
    index = np.arange(length)
    waves = frequencies(length)
    angles = 2.0 * np.pi * (waves[:, None] * index[None, :] % length) / length
    table = np.where(index[:, None] <= length // 2, np.cos(angles), np.sin(angles))
    edge = (waves == 0) | (2 * waves == length)
    return table * np.sqrt(np.where(edge, 1.0, 2.0) / length)[:, None]


def wave_squares(length):
    return np.sin(np.pi * frequencies(length) / length) ** 2


def refine_matrix(length):
    table = np.zeros((2 * length, length))
    for i in range(length):
        table[2 * i, i] += 1.0
        table[2 * i + 1, i] += 0.5
        table[2 * i + 1, (i + 1) % length] += 0.5
    return table


def pair_matrix(length):
    return np.repeat(np.eye(length), 2, axis=0)


def split(table):
    high = table.astype(np.float32).astype(ml_dtypes.bfloat16)
    low = (table - high.astype(np.float64)).astype(np.float32).astype(ml_dtypes.bfloat16)
    return high, low


def left_table(table):
    high, low = split(table)
    return np.concatenate([high, low, high], axis=1)


def right_table(table):
    high, low = split(table)
    return np.concatenate([high, low, high], axis=0)


def split_value(value):
    high = value.astype(bf16)
    return high, (value - high.astype(f32)).astype(bf16)


def left_dot(table, value):
    high, low = split_value(value)
    return jnp.dot(table, jnp.concatenate([high, high, low], axis=0), preferred_element_type=f32)


def right_dot(value, table):
    high, low = split_value(value)
    return jnp.dot(
        jnp.concatenate([high, high, low], axis=1), table, preferred_element_type=f32
    )


def wrap_rows(ref, plane, count):
    size = ref.shape[2] - 2 * pad
    for field in range(count):
        ref[field, plane, pad - 1 : pad, :] = ref[field, plane, pad + size - 1 : pad + size, :]
        ref[field, plane, pad + size : pad + size + 1, :] = ref[field, plane, pad : pad + 1, :]


def rhs_rows(ref, base, plane, start):
    stop = start + rows_at_once
    center = [ref[base + c, plane, start:stop, :] for c in range(3)]
    size = ref.shape[3]
    results = []
    for c in range(3):
        x_up = ref[base + c, plane + 1, start:stop, :]
        x_down = ref[base + c, plane - 1, start:stop, :]
        y_up = ref[base + c, plane, start + 1 : stop + 1, :]
        y_down = ref[base + c, plane, start - 1 : stop - 1, :]
        z_up = pltpu.roll(center[c], size - 1, 1)
        z_down = pltpu.roll(center[c], 1, 1)
        advect = (
            center[0] * (x_up - x_down) + center[1] * (y_up - y_down) + center[2] * (z_up - z_down)
        )
        laplace = (x_up + x_down) + (y_up + y_down) + (z_up + z_down) - 6.0 * center[c]
        results.append(viscosity * laplace - 0.5 * advect)
    return center, results


def planes_in(source, low, high, held, sems):
    length = source.shape[1]
    size = source.shape[2]
    rows = pl.ds(pad, size)

    def inner(plane):
        return pltpu.make_async_copy(
            source.at[:, plane], held.at[:, plane + 1, rows, :], sems.at[plane]
        )

    below = pltpu.make_async_copy(low, held.at[:, 0, rows, :], sems.at[length])
    above = pltpu.make_async_copy(high, held.at[:, length + 1, rows, :], sems.at[length + 1])
    return inner, below, above


def arrive(step, source, low, high, held, sems):
    length = source.shape[1]
    count = source.shape[0]
    inner, below, above = planes_in(source, low, high, held, sems)

    @pl.when(step == 0)
    def _():
        below.start()

        def launch(plane, carry):
            inner(plane).start()
            return carry

        lax.fori_loop(0, length, launch, 0)
        above.start()
        below.wait()
        inner(0).wait()
        wrap_rows(held, 1, count)

    inner(2 * step + 1).wait()
    wrap_rows(held, 2 * step + 2, count)

    @pl.when(2 * step + 2 < length)
    def _():
        inner(2 * step + 2).wait()
        wrap_rows(held, 2 * step + 3, count)

    @pl.when(2 * step + 2 >= length)
    def _():
        above.wait()


def chunks(size):
    return range(0, size, rows_at_once)


def transform(summed, z_table, y_table):
    count, half = len(summed), summed[0].shape[0]
    couples = []
    for k in range(0, count, 2):
        couples.append(jnp.concatenate([summed[k], summed[min(k + 1, count - 1)]], axis=1))
    in_z = right_dot(jnp.concatenate(couples, axis=0), z_table[...])
    in_z = [in_z[k * half : (k + 1) * half] for k in range(len(couples))]
    in_y = left_dot(y_table[...], jnp.concatenate(in_z, axis=1))
    blocks = half // 2
    lane = lax.broadcasted_iota(jnp.int32, (blocks, lanes), 1)
    results = []
    for k in range(count):
        both = in_y[:, (k // 2) * lanes : (k // 2 + 1) * lanes]
        upper, lower = both[:blocks], both[blocks:]
        if k % 2 == 0:
            results.append(jnp.where(lane < lanes // 2, upper, pltpu.roll(lower, lanes // 2, 1)))
        else:
            results.append(jnp.where(lane < lanes // 2, pltpu.roll(upper, lanes // 2, 1), lower))
    return results


def spectral(pairs, z_table, y_table, count):
    half = pairs.shape[1] // 2
    summed = [
        pairs[k, pl.ds(0, half, 2), :] + pairs[k, pl.ds(1, half, 2), :] for k in range(count)
    ]
    return transform(summed, z_table, y_table)


def sweep_one_kernel(is_first, source, low, high, s1, w, u, v, held, sems):
    step = pl.program_id(0)
    size = source.shape[2]
    arrive(step, source, low, high, held, sems)
    for row in chunks(size):
        rows = slice(row, row + rows_at_once)
        for part in range(2):
            plane = 2 * step + part + 1
            total_first, total_second, start, initial = None, None, None, None
            for node in range(3):
                center, old = rhs_rows(held, 3 * node, plane, pad + row)
                a, b = first[node], second[node] - (half_step if node == 1 else 0.0)
                if node == 0:
                    start, initial = center, old
                    total_first = [start[c] + a * old[c] for c in range(3)]
                    total_second = [b * old[c] for c in range(3)]
                else:
                    total_first = [total_first[c] + a * old[c] for c in range(3)]
                    total_second = [total_second[c] + b * old[c] for c in range(3)]
                if node == 0:
                    for c in range(3):
                        mine = first[0] * old[c] + is_first[0] * start[c]
                        other = second[0] * old[c]
                        if part == 1:
                            mine = mine + u[c, 0, rows, :]
                            other = other + v[c, 0, rows, :]
                        u[c, 0, rows, :] = mine
                        v[c, 0, rows, :] = other
            for c in range(3):
                s1[c, part, rows, :] = total_first[c]
                w[c, part, rows, :] = total_first[c] + total_second[c]
                u[c, 0, rows, :] = u[c, 0, rows, :] - total_first[c]
                v[c, 0, rows, :] = v[c, 0, rows, :] + total_first[c]


def sweep_two_kernel(
    group, source, low, high, w, u, v, z_table, y_table, s2, u_out, v_out, g, held, pairs, sems
):
    step = pl.program_id(0)
    size = source.shape[2]
    arrive(step, source, low, high, held, sems)
    for row in chunks(size):
        rows = slice(row, row + rows_at_once)
        fresh_sum, sweep_sum = None, None
        for part in range(2):
            _, fresh = rhs_rows(held, 0, 2 * step + part + 1, pad + row)
            swept = [w[c, part, rows, :] + half_step * fresh[c] for c in range(3)]
            for c in range(3):
                s2[c, part, rows, :] = swept[c]
            if part == 0:
                fresh_sum, sweep_sum = fresh, swept
            else:
                fresh_sum = [fresh_sum[c] + fresh[c] for c in range(3)]
                sweep_sum = [sweep_sum[c] + swept[c] for c in range(3)]
        for c in range(3):
            u_out[c, 0, rows, :] = u[c, 0, rows, :] + first[1] * fresh_sum[c]
            v_out[c, 0, rows, :] = v[c, 0, rows, :] + second[1] * fresh_sum[c] - sweep_sum[c]
            pairs[c, rows, :] = sweep_sum[c]
    planes = source.shape[1] // 2
    blocks = g.shape[0] // group
    for c, value in enumerate(spectral(pairs, z_table, y_table, 3)):
        g[pl.ds(c * planes + step, blocks, group), :] = value


def source_kernel(
    group, g_group, source, low, high, u, v, g, z_table, y_table, out, held, pairs, sems
):
    step = pl.program_id(0)
    size = source.shape[2]
    arrive(step, source, low, high, held, sems)
    for row in chunks(size):
        rows = slice(row, row + rows_at_once)
        _, fresh = rhs_rows(held, 0, 2 * step + 1, pad + row)
        _, other = rhs_rows(held, 0, 2 * step + 2, pad + row)
        for c in range(3):
            total = fresh[c] + other[c]
            pairs[c, rows, :] = u[c, 0, rows, :] + first[2] * total
            pairs[3 + c, rows, :] = v[c, 0, rows, :] + second[2] * total
    planes = source.shape[1] // 2
    blocks = out.shape[0] // group
    for k, value in enumerate(spectral(pairs, z_table, y_table, 6)):
        if k < 3:
            value = value + g[pl.ds(k * planes + step, blocks, g_group), :]
        out[pl.ds(k * planes + step, blocks, group), :] = value


def solve_kernel(
    peers, intervals, planes, group, back, values, inverse, forward, backward, out_1, out_2
):
    start = [None] * 3
    for interval in range(intervals):
        loaded = []
        for field in range(6):
            parts = [
                values[
                    pl.ds(interval * group + field * planes + p, peers, intervals * group), :
                ]
                for p in range(planes)
            ]
            loaded.append(jnp.concatenate(parts, axis=0))
        spectra = left_dot(forward[...], jnp.concatenate(loaded, axis=1))
        rates = inverse[...]
        wanted = []
        for field in range(6):
            c = field % 3
            value = spectra[:, field * lanes : (field + 1) * lanes]
            if start[c] is not None:
                value = value + start[c]
            start[c] = value * rates
            wanted.append(start[c])
        physical = left_dot(backward[...], jnp.concatenate(wanted, axis=1))
        for field in range(6):
            out = (out_1, out_2)[field // 3]
            base = (field % 3) * (planes + 2)
            for e in range(planes + 2):
                out[pl.ds(interval * back + base + e, peers, intervals * back), :] = physical[
                    e * peers : (e + 1) * peers, field * lanes : (field + 1) * lanes
                ]


def edges_kernel(source, low, high, sems):
    length = source.shape[1]
    copies = [
        pltpu.make_async_copy(source.at[:, 0], low, sems.at[0]),
        pltpu.make_async_copy(source.at[:, length - 1], high, sems.at[1]),
    ]
    for copy in copies:
        copy.start()
    for copy in copies:
        copy.wait()


def sweep_one_plane(is_first, held, slot, put_s1, put_w, uv, cell):
    size = held.shape[2] - 2 * pad
    for row in chunks(size):
        rows = slice(row, row + rows_at_once)
        total_first, total_second = [], []
        for node in range(3):
            start, old = rhs_rows(held, 3 * node, slot, pad + row)
            a, b = first[node], second[node] - (half_step if node == 1 else 0.0)
            if node == 0:
                for c in range(3):
                    uv[c, cell, rows, :] += first[0] * old[c] + is_first[0] * start[c]
                    uv[3 + c, cell, rows, :] += second[0] * old[c]
                total_first = [start[c] + a * old[c] for c in range(3)]
                total_second = [b * old[c] for c in range(3)]
            else:
                total_first = [total_first[c] + a * old[c] for c in range(3)]
                total_second = [total_second[c] + b * old[c] for c in range(3)]
        for c in range(3):
            put_s1(c, row, total_first[c])
            put_w(c, row, total_first[c] + total_second[c])
            uv[c, cell, rows, :] -= total_first[c]
            uv[3 + c, cell, rows, :] += total_first[c]


def sweep_two_plane(held, slot, get_w, put_s2, uv, cell):
    size = held.shape[2] - 2 * pad
    for row in chunks(size):
        rows = slice(row, row + rows_at_once)
        _, fresh = rhs_rows(held, 0, slot, pad + row)
        for c in range(3):
            swept = get_w(c, row) + half_step * fresh[c]
            put_s2(c, row, swept)
            uv[c, cell, rows, :] += first[1] * fresh[c]
            uv[3 + c, cell, rows, :] += second[1] * fresh[c] - swept


def last_rhs_pair(held, slot, uv, cell):
    size = held.shape[2] - 2 * pad
    for row in chunks(size):
        rows = slice(row, row + rows_at_once)
        _, fresh = rhs_rows(held, 0, slot, pad + row)
        _, other = rhs_rows(held, 0, slot + 1, pad + row)
        for c in range(3):
            total = fresh[c] + other[c]
            uv[c, cell, rows, :] += first[2] * total
            uv[3 + c, cell, rows, :] += second[2] * total


def uv_halves(uv, k, cell):
    half = uv.shape[2] // 2
    return uv[k, cell, pl.ds(0, half, 2), :] + uv[k, cell, pl.ds(1, half, 2), :]


def held_halves(held, c, slot):
    half = (held.shape[2] - 2 * pad) // 2
    total = held[c, slot, pl.ds(pad, half, 2), :] + held[c, slot, pl.ds(pad + 1, half, 2), :]
    total = total + held[c, slot + 1, pl.ds(pad, half, 2), :]
    return total + held[c, slot + 1, pl.ds(pad + 1, half, 2), :]


def interior_kernel(
    group, g_group, is_first, source, z_table, y_table,
    s1_out, s2_out, w_out, uv_end, uv_next, out, g,
    held, held_1, held_2, w, uv, sems, out_sems
):
    length, size = source.shape[1], source.shape[2]
    planes = length // 2
    blocks = out.shape[0] // group
    rows_all = pl.ds(pad, size)

    def arriving(plane):
        return pltpu.make_async_copy(
            source.at[:, plane], held.at[:, plane, rows_all, :], sems.at[plane]
        )

    def launch(plane, carry):
        arriving(plane).start()
        return carry

    lax.fori_loop(0, length, launch, 0)
    uv[...] = jnp.zeros(uv.shape, f32)
    arriving(0).wait()
    arriving(1).wait()
    wrap_rows(held, 1, 9)

    def s1_copy(plane):
        return pltpu.make_async_copy(
            held_1.at[:, plane, rows_all, :], s1_out.at[:, plane - 1], out_sems.at[0, plane]
        )

    def s2_copy(plane):
        return pltpu.make_async_copy(
            held_2.at[:, plane, rows_all, :], s2_out.at[:, plane - 2], out_sems.at[1, plane]
        )

    def phase_one(plane, carry):
        arriving(plane + 1).wait()
        wrap_rows(held, plane + 1, 9)

        def put_s1(c, row, value):
            held_1[c, plane, pad + row : pad + row + rows_at_once, :] = value

        def put_w(c, row, value):
            w[c, plane, row : row + rows_at_once, :] = value

        sweep_one_plane(is_first, held, plane, put_s1, put_w, uv, plane // 2)
        wrap_rows(held_1, plane, 3)
        s1_copy(plane).start()
        return carry

    lax.fori_loop(1, length - 1, phase_one, 0)

    def phase_two(plane, carry):
        def get_w(c, row):
            return w[c, plane, row : row + rows_at_once, :]

        def put_s2(c, row, value):
            held_2[c, plane, pad + row : pad + row + rows_at_once, :] = value

        sweep_two_plane(held_1, plane, get_w, put_s2, uv, plane // 2)
        wrap_rows(held_2, plane, 3)
        s2_copy(plane).start()
        return carry

    lax.fori_loop(2, length - 2, phase_two, 0)
    tails = []
    for k, plane in enumerate((1, length - 2)):
        tails.append(pltpu.make_async_copy(w.at[:, plane], w_out.at[:, k], out_sems.at[2, k]))
    for k, cell in enumerate((0, planes - 1)):
        tails.append(pltpu.make_async_copy(uv.at[:, cell], uv_end.at[:, k], out_sems.at[2, 2 + k]))
    for k, cell in enumerate((1, planes - 2)):
        tails.append(pltpu.make_async_copy(uv.at[:, cell], uv_next.at[:, k], out_sems.at[2, 4 + k]))
    for copy in tails:
        copy.start()

    def phase_three(cell, carry):
        last_rhs_pair(held_2, 2 * cell, uv, cell)
        return carry

    lax.fori_loop(2, planes - 2, phase_three, 0)
    for start in range(2, planes - 2, 2):
        cells = range(start, min(start + 2, planes - 2))
        entries = [(k, cell) for cell in cells for k in range(6)]
        values = transform([uv_halves(uv, k, cell) for k, cell in entries], z_table, y_table)
        for (k, cell), value in zip(entries, values):
            out[pl.ds(k * planes + cell, blocks, group), :] = value
    for start in range(1, planes - 1, 4):
        cells = range(start, min(start + 4, planes - 1))
        entries = [(c, cell) for cell in cells for c in range(3)]
        values = transform([held_halves(held_2, c, 2 * cell) for c, cell in entries], z_table, y_table)
        for (c, cell), value in zip(entries, values):
            g[pl.ds(c * planes + cell, blocks, g_group), :] = value

    def finish_one(plane, carry):
        s1_copy(plane).wait()
        return carry

    def finish_two(plane, carry):
        s2_copy(plane).wait()
        return carry

    lax.fori_loop(1, length - 1, finish_one, 0)
    lax.fori_loop(2, length - 2, finish_two, 0)
    for copy in tails:
        copy.wait()


def start_all(copies):
    for copy in copies:
        copy.start()
    for copy in copies:
        copy.wait()


def end_one_kernel(
    is_first, source, low, high, uv_in, low_out, high_out, w_out, uv, held, sems
):
    length, size = source.shape[1], source.shape[2]
    rows_all = pl.ds(pad, size)
    sources = [low, source.at[:, 0], source.at[:, 1]]
    sources += [source.at[:, length - 2], source.at[:, length - 1], high]
    start_all([
        pltpu.make_async_copy(ref, held.at[:, slot, rows_all, :], sems.at[slot])
        for slot, ref in enumerate(sources)
    ])
    uv[...] = uv_in[...]
    for k, (slot, ref) in enumerate(((1, low_out), (4, high_out))):
        wrap_rows(held, slot, 9)

        def put_s1(c, row, value):
            ref[c, row : row + rows_at_once, :] = value

        def put_w(c, row, value):
            w_out[c, k, row : row + rows_at_once, :] = value

        sweep_one_plane(is_first, held, slot, put_s1, put_w, uv, k)


def end_two_kernel(
    g_group, swept, low, low_end, high_end, high, w_end, w_next, uv_in, g_in, z_table, y_table,
    low_out, high_out, next_out, uv, g, held, held_2, sems
):
    count, size = swept.shape[1], swept.shape[2]
    rows_all = pl.ds(pad, size)
    planes = (count + 2) // 2
    sources = [low, low_end, swept.at[:, 0], swept.at[:, 1]]
    sources += [swept.at[:, count - 2], swept.at[:, count - 1], high_end, high]
    start_all([
        pltpu.make_async_copy(ref, held.at[:, slot, rows_all, :], sems.at[slot])
        for slot, ref in enumerate(sources)
    ])
    uv[...] = uv_in[...]
    g[...] = g_in[...]
    places = ((1, 0, w_end, 0), (2, 0, w_next, 0), (5, 1, w_next, 1), (6, 1, w_end, 1))
    for index, (slot, cell, w, k) in enumerate(places):
        wrap_rows(held, slot, 3)

        def get_w(c, row):
            return w[c, k, row : row + rows_at_once, :]

        def put_s2(c, row, value):
            rows = slice(row, row + rows_at_once)
            if slot == 1:
                low_out[c, rows, :] = value
            elif slot == 6:
                high_out[c, rows, :] = value
            else:
                next_out[c, k, rows, :] = value
            held_2[c, index, pad + row : pad + row + rows_at_once, :] = value

        sweep_two_plane(held, slot, get_w, put_s2, uv, cell)
    blocks = g.shape[0] // g_group
    entries = [(c, k) for k in range(2) for c in range(3)]
    values = transform([held_halves(held_2, c, 2 * k) for c, k in entries], z_table, y_table)
    for (c, k), value in zip(entries, values):
        g[pl.ds(c * planes + k * (planes - 1), blocks, g_group), :] = value


def end_three_kernel(
    group, g_group, swept, low, low_end, nexts, high_end, high, uv_end, uv_next, f, g,
    z_table, y_table, pack, out, held, uv, sems, out_sems
):
    count, size = swept.shape[1], swept.shape[2]
    rows_all = pl.ds(pad, size)
    planes = (count + 4) // 2
    sources = [low, low_end, nexts.at[:, 0], swept.at[:, 0], swept.at[:, 1], swept.at[:, 2]]
    sources += [swept.at[:, count - 3], swept.at[:, count - 2], swept.at[:, count - 1]]
    sources += [nexts.at[:, 1], high_end, high]
    start_all([
        pltpu.make_async_copy(ref, held.at[:, slot, rows_all, :], sems.at[slot])
        for slot, ref in enumerate(sources)
    ])
    packing = [
        pltpu.make_async_copy(held.at[:, slot, rows_all, :], pack.at[:, k], out_sems.at[k])
        for k, slot in enumerate((0, 1, 2, 9, 10, 11))
    ]
    for k in range(2):
        uv[:, 3 * k] = uv_end[:, k]
        uv[:, 1 + k] = uv_next[:, k]
    out[...] = f[...]
    for slot in (1, 2, 3, 4, 7, 8, 9, 10):
        wrap_rows(held, slot, 3)
    for copy in packing:
        copy.start()
    for index, slot in enumerate((1, 3, 7, 9)):
        last_rhs_pair(held, slot, uv, index)
    blocks = out.shape[0] // group
    cells = (0, 1, planes - 2, planes - 1)
    for half in range(2):
        entries = [(k, index) for index in (2 * half, 2 * half + 1) for k in range(6)]
        values = transform([uv_halves(uv, k, index) for k, index in entries], z_table, y_table)
        for (k, index), value in zip(entries, values):
            out[pl.ds(k * planes + cells[index], blocks, group), :] = value
    for block in range(blocks):
        out[block * group : block * group + 3 * planes, :] += g[
            block * g_group : block * g_group + 3 * planes, :
        ]
    for copy in packing:
        copy.wait()


def corrected_kernel(node, group, layouts, counts, *refs):
    if len(layouts) > 1:
        is_first, refs = refs[0], refs[1:]
    spectra, z_table, y_table = refs[:3]
    fields = refs[3 : 3 + counts]
    new_velocity, new_rhs, held, coarse, result, sems, out_sems, rhs_sems = refs[-8:]
    length, size = held.shape[1] - 2, held.shape[2] - 2 * pad
    planes = length // 2
    rows_all = pl.ds(pad, size)

    def arriving(layout, slot):
        number, index = layout[slot]
        ref = fields[number]
        ref = ref.at[0:3, index] if index is not None else ref.at[0:3]
        return pltpu.make_async_copy(ref, held.at[:, slot, rows_all, :], sems.at[slot])

    def launch(layout):
        for slot in range(length + 2):
            arriving(layout, slot).start()

    if len(layouts) > 1:

        @pl.when(is_first[0] > 0)
        def _():
            launch(layouts[0])

        @pl.when(is_first[0] <= 0)
        def _():
            launch(layouts[1])
    else:
        launch(layouts[0])
    blocks = spectra.shape[0] // group
    for c in range(3):
        base = c * (planes + 2)
        parts = [spectra[pl.ds(base + e, blocks, group), :] for e in range(planes + 2)]
        in_z = right_dot(jnp.concatenate(parts, axis=0), z_table[...])
        for e in range(planes + 2):
            mine = in_z[e * blocks : (e + 1) * blocks]
            stacked = jnp.concatenate([mine[:, :size], mine[:, size:]], axis=0)
            coarse[c, e] = left_dot(y_table[...], stacked)
    for slot in range(length + 2):
        arriving(layouts[0], slot).wait()

    def out_copy(plane):
        return pltpu.make_async_copy(
            held.at[:, plane + 1, rows_all, :], new_velocity.at[node, :, plane], out_sems.at[plane]
        )

    def rhs_copy(plane):
        return pltpu.make_async_copy(
            result.at[:, plane], new_rhs.at[node, :, plane], rhs_sems.at[plane]
        )

    def correct(plane, cell, odd):
        for field in range(3):
            for row in chunks(size):
                rows = slice(row, row + rows_at_once)
                held_rows = slice(pad + row, pad + row + rows_at_once)
                value = coarse[field, cell, rows, :]
                if odd:
                    value = 0.5 * (value + coarse[field, cell + 1, rows, :])
                held[field, plane, held_rows, :] += value
        wrap_rows(held, plane, 3)

    correct(0, 0, True)
    correct(1, 1, False)
    out_copy(0).start()

    def body(q, carry):
        correct(2 * q + 2, q + 1, True)
        correct(2 * q + 3, q + 2, False)
        out_copy(2 * q + 1).start()

        @pl.when(2 * q + 2 < length)
        def _():
            out_copy(2 * q + 2).start()

        for part in range(2):
            plane = 2 * q + part
            for row in chunks(size):
                _, fresh = rhs_rows(held, 0, plane + 1, pad + row)
                for c in range(3):
                    result[c, plane, row : row + rows_at_once, :] = fresh[c].astype(bf16)
            rhs_copy(plane).start()
        return carry

    lax.fori_loop(0, planes, body, 0)

    def finish(plane, carry):
        out_copy(plane).wait()
        rhs_copy(plane).wait()
        return carry

    lax.fori_loop(0, length, finish, 0)


anywhere = pl.BlockSpec(memory_space=pl.ANY)
scalar = pl.BlockSpec(memory_space=pltpu.SMEM)
vmem = pl.BlockSpec(memory_space=pltpu.VMEM)


def whole(shape):
    return pl.BlockSpec(shape, lambda *index: (0,) * len(shape))


def struct(shape, dtype=f32):
    return jax.ShapeDtypeStruct(shape, dtype)


def slab(shape):
    return pl.BlockSpec(shape, lambda q: (0, q, 0, 0))


def held_planes(count, length, size_y, size_z):
    return pltpu.VMEM((count, length + 2, size_y + 2 * pad, size_z), f32)


def neighbours(low_plane, high_plane):
    count = lax.axis_size("space")
    up = [(i, (i + 1) % count) for i in range(count)]
    down = [(j, i) for i, j in up]
    return lax.ppermute(high_plane, "space", up), lax.ppermute(low_plane, "space", down)


def later_interval(value):
    count = lax.axis_size("tm")
    return lax.ppermute(value, "tm", [(i, i + 1) for i in range(count - 1)])


def corrected(node, spectra, tables, fields, layouts, outs, is_first=None):
    length = len(layouts[0]) - 2
    size_y, size_z = fields[0].shape[-2:]
    planes = length // 2
    group = spectra.shape[1]
    operands = [spectra.reshape(-1, lanes), *tables]
    specs = [whole(o.shape) for o in operands]
    if is_first is not None:
        operands, specs = [is_first, *operands], [scalar, *specs]
    operands, specs = [*operands, *fields], specs + [anywhere] * len(fields)
    shape = (3, 3, length, size_y, size_z)
    aliases = {}
    if outs is not None:
        aliases = {len(operands): 0, len(operands) + 1: 1}
        operands, specs = [*operands, *outs], specs + [anywhere] * 2
    return pl.pallas_call(
        functools.partial(corrected_kernel, node, group, layouts, len(fields)),
        out_shape=(struct(shape), struct(shape, bf16)),
        in_specs=specs,
        out_specs=(anywhere, anywhere),
        input_output_aliases=aliases,
        scratch_shapes=[
            held_planes(3, length, size_y, size_z),
            pltpu.VMEM((3, planes + 2, size_y, size_z), f32),
            pltpu.VMEM((3, length, size_y, size_z), bf16),
            pltpu.SemaphoreType.DMA((length + 2,)),
            pltpu.SemaphoreType.DMA((length,)),
            pltpu.SemaphoreType.DMA((length,)),
        ],
        compiler_params=params,
        name=f"corrected_{node}",
    )(*operands)


def sweep_whole(fields, is_first, z_table, y_table, blocks):
    length, size_y, size_z = fields.shape[1:]
    planes = length // 2
    low, high = neighbours(fields[:, 0], fields[:, length - 1])
    fine = (3, length, size_y, size_z)
    halved = (3, planes, size_y, size_z)
    two = (3, 2, size_y, size_z)
    one = (3, 1, size_y, size_z)
    in_sems = pltpu.SemaphoreType.DMA((length + 2,))
    swept_1, w, u, v = pl.pallas_call(
        sweep_one_kernel,
        grid=(planes,),
        out_shape=(struct(fine), struct(fine), struct(halved), struct(halved)),
        in_specs=[scalar, anywhere, anywhere, anywhere],
        out_specs=(slab(two), slab(two), slab(one), slab(one)),
        scratch_shapes=[held_planes(9, length, size_y, size_z), in_sems],
        compiler_params=params,
        name="sweep_one",
    )(is_first, fields, low, high)
    low_1, high_1 = neighbours(swept_1[:, 0], swept_1[:, length - 1])

    g_group = round_up(3 * planes, 8)
    swept_2, u, v, g = pl.pallas_call(
        functools.partial(sweep_two_kernel, g_group),
        grid=(planes,),
        out_shape=(struct(fine), struct(halved), struct(halved), struct((blocks * g_group, lanes))),
        in_specs=[anywhere, anywhere, anywhere, slab(two), slab(one), slab(one)]
        + [whole(z_table.shape), whole(y_table.shape)],
        out_specs=(slab(two), slab(one), slab(one), whole((blocks * g_group, lanes))),
        scratch_shapes=[
            held_planes(3, length, size_y, size_z),
            pltpu.VMEM((3, size_y, size_z), f32),
            in_sems,
        ],
        compiler_params=params,
        name="sweep_two",
    )(swept_1, low_1, high_1, w, u, v, z_table, y_table)
    low_2, high_2 = neighbours(swept_2[:, 0], swept_2[:, length - 1])
    g = later_interval(g)

    group = round_up(6 * planes, 8)
    sources = pl.pallas_call(
        functools.partial(source_kernel, group, g_group),
        grid=(planes,),
        out_shape=struct((blocks * group, lanes)),
        in_specs=[anywhere, anywhere, anywhere, slab(one), slab(one), whole(g.shape)]
        + [whole(z_table.shape), whole(y_table.shape)],
        out_specs=whole((blocks * group, lanes)),
        scratch_shapes=[
            held_planes(3, length, size_y, size_z),
            pltpu.VMEM((6, size_y, size_z), f32),
            in_sems,
        ],
        compiler_params=params,
        name="sources",
    )(swept_2, low_2, high_2, u, v, g, z_table, y_table)
    layout = tuple([(0, None)] + [(1, p) for p in range(length)] + [(2, None)])
    carried = [later_interval(value) for value in (low_2, swept_2, high_2)]
    later = tuple((3 + number, index) for number, index in layout)
    return (
        sources,
        ((low_1, swept_1, high_1), (layout,)),
        ((low_2, swept_2, high_2), (layout,)),
        ((low, fields, high, *carried), (layout, later)),
    )


def sweep_split(fields, is_first, z_table, y_table, blocks):
    length, size_y, size_z = fields.shape[1:]
    planes = length // 2
    plane, g_group, group = (size_y, size_z), round_up(3 * planes, 8), round_up(6 * planes, 8)

    def held(count, slots):
        return pltpu.VMEM((count, slots, size_y + 2 * pad, size_z), f32)

    def sems(*shape):
        return pltpu.SemaphoreType.DMA(shape)

    low, high = pl.pallas_call(
        edges_kernel,
        out_shape=(struct((9, *plane)),) * 2,
        in_specs=[anywhere],
        out_specs=(anywhere,) * 2,
        scratch_shapes=[sems(2)],
        name="edges",
    )(fields)
    low, high = neighbours(low, high)
    swept_1, swept_2, w_next, uv_end, uv_next, f, g = pl.pallas_call(
        functools.partial(interior_kernel, group, g_group),
        out_shape=(
            struct((3, length - 2, *plane)),
            struct((3, length - 4, *plane)),
            struct((3, 2, *plane)),
            struct((6, 2, *plane)),
            struct((6, 2, *plane)),
            struct((blocks * group, lanes)),
            struct((blocks * g_group, lanes)),
        ),
        in_specs=[scalar, anywhere, vmem, vmem],
        out_specs=(anywhere,) * 5 + (vmem,) * 2,
        scratch_shapes=[
            held(9, length),
            held(3, length),
            held(3, length),
            pltpu.VMEM((3, length, *plane), f32),
            pltpu.VMEM((6, planes, *plane), f32),
            sems(length),
            sems(3, max(length, 6)),
        ],
        compiler_params=params,
        cost_estimate=pl.CostEstimate(flops=4 * 10**9, bytes_accessed=6 * 10**7, transcendentals=0),
        name="interior",
    )(is_first, fields, z_table, y_table)
    low_end_1, high_end_1, w_end, uv_end = pl.pallas_call(
        end_one_kernel,
        out_shape=(
            struct((3, *plane)),
            struct((3, *plane)),
            struct((3, 2, *plane)),
            struct((6, 2, *plane)),
        ),
        in_specs=[scalar, anywhere, anywhere, anywhere, vmem],
        out_specs=(vmem,) * 4,
        scratch_shapes=[held(9, 6), sems(6)],
        compiler_params=params,
        name="end_one",
    )(is_first, fields, low, high, uv_end)
    low_1, high_1 = neighbours(low_end_1, high_end_1)
    low_end_2, high_end_2, next_2, uv_end, g = pl.pallas_call(
        functools.partial(end_two_kernel, g_group),
        out_shape=(
            struct((3, *plane)),
            struct((3, *plane)),
            struct((3, 2, *plane)),
            struct((6, 2, *plane)),
            struct((blocks * g_group, lanes)),
        ),
        in_specs=[anywhere] * 5 + [vmem] * 6,
        out_specs=(vmem,) * 5,
        scratch_shapes=[held(3, 8), held(3, 4), sems(8)],
        compiler_params=params,
        name="end_two",
    )(swept_1, low_1, low_end_1, high_end_1, high_1, w_end, w_next, uv_end, g, z_table, y_table)
    low_2, high_2 = neighbours(low_end_2, high_end_2)
    pack, sources = pl.pallas_call(
        functools.partial(end_three_kernel, group, g_group),
        out_shape=(struct((3, 6, *plane)), struct((blocks * group, lanes))),
        in_specs=[anywhere] * 6 + [vmem] * 6,
        out_specs=(anywhere, vmem),
        scratch_shapes=[held(3, 12), pltpu.VMEM((6, 4, *plane), f32), sems(12), sems(6)],
        compiler_params=params,
        name="end_three",
    )(
        swept_2, low_2, low_end_2, next_2, high_end_2, high_2, uv_end, uv_next, f,
        later_interval(g), z_table, y_table
    )
    layout_1 = [(0, None), (1, None)] + [(2, p) for p in range(length - 2)] + [(3, None), (4, None)]
    layout_2 = [(0, None), (1, None), (2, 0)] + [(3, p) for p in range(length - 4)]
    layout_2 += [(2, 1), (4, None), (5, None)]
    layout_0 = [(0, None)] + [(1, p) for p in range(length)] + [(2, None)]
    later = [(3, 0), (3, 1), (3, 2)] + [(4, p) for p in range(length - 4)] + [(3, 3), (3, 4), (3, 5)]
    return (
        sources,
        ((low_1, low_end_1, swept_1, high_end_1, high_1), (tuple(layout_1),)),
        ((low_2, low_end_2, next_2, swept_2, high_end_2, high_2), (tuple(layout_2),)),
        (
            (low, fields, high, later_interval(pack), later_interval(swept_2)),
            (tuple(layout_0), tuple(later)),
        ),
    )


def per_device(velocity):
    length, size_y, size_z = velocity.shape[3:]
    planes = length // 2
    peers, intervals = lax.axis_size("space"), lax.axis_size("tm")
    devices = peers * intervals
    coarse_x, coarse_y, coarse_z = peers * planes, size_y // 2, size_z // 2
    blocks = coarse_y * coarse_z // lanes
    per_block = devices // blocks
    columns = lanes // per_block
    device = lax.axis_index("space") * intervals + lax.axis_index("tm")
    tm_first = lax.axis_index("tm") == 0
    fields = velocity.reshape(9, length, size_y, size_z)

    x_basis, y_basis, z_basis = basis(coarse_x), basis(coarse_y), basis(coarse_z)
    z_forward = 0.25 * pair_matrix(coarse_z) @ z_basis.T
    z_table = right_table(np.kron(np.eye(2), z_forward))
    y_table = left_table(0.5 * y_basis)
    order = np.arange(coarse_x).reshape(peers, planes).T.reshape(-1)
    x_forward = left_table(x_basis[:, order])
    wanted_x = np.arange(peers)[None, :] * planes + np.arange(-1, planes + 1)[:, None]
    x_backward = left_table(x_basis.T[wanted_x.reshape(-1) % coarse_x])
    z_back = (refine_matrix(coarse_z) @ z_basis.T).T
    z_back_table = right_table(np.kron(np.eye(2), z_back))
    y_back_table = left_table(refine_matrix(coarse_y) @ y_basis.T)
    y_of = np.arange(2)[:, None] * blocks + np.arange(blocks)[None, :]
    waves = wave_squares(coarse_y)[y_of.T][:, :, None] + wave_squares(coarse_z)[None, None, :]
    waves = waves.reshape(devices, columns)
    waves = np.pad(waves, ((0, 0), (0, lanes - columns)))
    mine = lax.dynamic_slice_in_dim(jnp.asarray(waves, f32), device, 1, axis=0)
    total = jnp.asarray(wave_squares(coarse_x), f32)[:, None] + mine
    rates = 1.0 / (1.0 + half_step * coarse_viscosity * (4.0 / (2.0 * 2.0)) * total)

    is_first = tm_first.astype(f32).reshape(1)
    sweep = sweep_split if length >= 10 else sweep_whole
    sources, one, two, zero = sweep(fields, is_first, z_table, y_table, blocks)
    group = round_up(6 * planes, 8)

    both = ("space", "tm")

    def to_columns(value, rows):
        if per_block > 1:
            value = value.reshape(blocks, rows, per_block, columns).swapaxes(1, 2)
        value = value.reshape(devices, rows, columns)
        value = lax.all_to_all(value, both, split_axis=0, concat_axis=0, tiled=True)
        value = jnp.pad(value, ((0, 0), (0, 0), (0, lanes - columns)))
        return value.reshape(devices * rows, lanes)

    def to_planes(value, rows):
        value = value.reshape(devices, rows, lanes)[:, :, :columns]
        value = lax.all_to_all(value, both, split_axis=0, concat_axis=0, tiled=True)
        if per_block > 1:
            value = value.reshape(blocks, per_block, rows, columns).swapaxes(1, 2)
        return value.reshape(blocks, rows, lanes)

    back = round_up(3 * (planes + 2), 8)
    columned = to_columns(sources, group)
    solved_1, solved_2 = pl.pallas_call(
        functools.partial(solve_kernel, peers, intervals, planes, group, back),
        out_shape=(struct((devices * back, lanes)),) * 2,
        compiler_params=params,
        name="solve",
    )(columned, rates, x_forward, x_backward)
    spectra_2 = to_planes(solved_2, back)
    spectra_1 = to_planes(solved_1, back)
    tables = (z_back_table, y_back_table)
    outs = corrected(2, spectra_2, tables, *two, None)
    outs = corrected(1, spectra_1, tables, *one, outs)
    new_velocity, new_rhs = corrected(0, later_interval(spectra_2), tables, *zero, outs, is_first)
    return (new_velocity[None], new_rhs[None])


def solution(mesh):
    placed = P("tm", None, None, "space", None, None)
    return jax.shard_map(
        per_device,
        mesh=mesh,
        in_specs=(placed,),
        out_specs=(placed, placed),
        check_vma=False,
    )
```

```python
import functools

import jax
import jax.numpy as jnp
import ml_dtypes
import numpy as np
from jax import lax
from jax.experimental import pallas as pl
from jax.experimental.pallas import tpu as pltpu
from jax.sharding import PartitionSpec as P

viscosity = 1.0
coarse_viscosity = 10.0
time_step = 0.3
weights_first = (5.0 / 24.0, 1.0 / 3.0, -1.0 / 24.0)
weights_second = (-1.0 / 24.0, 1.0 / 3.0, 5.0 / 24.0)
half_step = 0.5 * time_step
first = tuple(time_step * w for w in weights_first)
second = tuple(time_step * w for w in weights_second)
lanes = 128
pad = 8
rows_at_once = 32


def params(kibibytes):
    return pltpu.CompilerParams(vmem_limit_bytes=kibibytes * 1024)


def params_but(kibibytes):
    return params(64 * 1024 - kibibytes)


f32 = jnp.float32
bf16 = jnp.bfloat16


def round_up(value, multiple):
    return -(-value // multiple) * multiple


def frequencies(length):
    index = np.arange(length)
    return np.where(index <= length // 2, index, index - length // 2)


def basis(length):
    index = np.arange(length)
    waves = frequencies(length)
    angles = 2.0 * np.pi * (waves[:, None] * index[None, :] % length) / length
    table = np.where(index[:, None] <= length // 2, np.cos(angles), np.sin(angles))
    edge = (waves == 0) | (2 * waves == length)
    return table * np.sqrt(np.where(edge, 1.0, 2.0) / length)[:, None]


def wave_squares(length):
    return np.sin(np.pi * frequencies(length) / length) ** 2


def refine_matrix(length):
    table = np.zeros((2 * length, length))
    for i in range(length):
        table[2 * i, i] += 1.0
        table[2 * i + 1, i] += 0.5
        table[2 * i + 1, (i + 1) % length] += 0.5
    return table


def pair_matrix(length):
    return np.repeat(np.eye(length), 2, axis=0)


def split(table):
    high = table.astype(np.float32).astype(ml_dtypes.bfloat16)
    low = (table - high.astype(np.float64)).astype(np.float32).astype(ml_dtypes.bfloat16)
    return high, low


def left_table(table):
    high, low = split(table)
    return np.concatenate([high, low, high], axis=1)


def right_table(table):
    high, low = split(table)
    return np.concatenate([high, low, high], axis=0)


def split_value(value):
    high = value.astype(bf16)
    return high, (value - high.astype(f32)).astype(bf16)


def left_dot(table, value):
    high, low = split_value(value)
    return jnp.dot(table, jnp.concatenate([high, high, low], axis=0), preferred_element_type=f32)


def right_dot(value, table):
    high, low = split_value(value)
    return jnp.dot(
        jnp.concatenate([high, high, low], axis=1), table, preferred_element_type=f32
    )


def start_all(copies):
    for copy in copies:
        copy.start()
    for copy in copies:
        copy.wait()


def wrap_rows(ref, plane, count):
    size = ref.shape[2] - 2 * pad
    for field in range(count):
        ref[field, plane, pad - 1 : pad, :] = ref[field, plane, pad + size - 1 : pad + size, :]
        ref[field, plane, pad + size : pad + size + 1, :] = ref[field, plane, pad : pad + 1, :]


def rhs_rows(ref, base, plane, start):
    stop = start + rows_at_once
    center = [ref[base + c, plane, start:stop, :] for c in range(3)]
    size = ref.shape[3]
    results = []
    for c in range(3):
        x_up = ref[base + c, plane + 1, start:stop, :]
        x_down = ref[base + c, plane - 1, start:stop, :]
        y_up = ref[base + c, plane, start + 1 : stop + 1, :]
        y_down = ref[base + c, plane, start - 1 : stop - 1, :]
        z_up = pltpu.roll(center[c], size - 1, 1)
        z_down = pltpu.roll(center[c], 1, 1)
        advect = (
            center[0] * (x_up - x_down) + center[1] * (y_up - y_down) + center[2] * (z_up - z_down)
        )
        laplace = (x_up + x_down) + (y_up + y_down) + (z_up + z_down) - 6.0 * center[c]
        results.append(viscosity * laplace - 0.5 * advect)
    return center, results


def planes_in(source, low, high, held, sems):
    length = source.shape[1]
    size = source.shape[2]
    rows = pl.ds(pad, size)

    def inner(plane):
        return pltpu.make_async_copy(
            source.at[:, plane], held.at[:, plane + 1, rows, :], sems.at[plane]
        )

    below = pltpu.make_async_copy(low, held.at[:, 0, rows, :], sems.at[length])
    above = pltpu.make_async_copy(high, held.at[:, length + 1, rows, :], sems.at[length + 1])
    return inner, below, above


def arrive(step, source, low, high, held, sems):
    length = source.shape[1]
    count = source.shape[0]
    inner, below, above = planes_in(source, low, high, held, sems)

    @pl.when(step == 0)
    def _():
        below.start()

        def launch(plane, carry):
            inner(plane).start()
            return carry

        lax.fori_loop(0, length, launch, 0)
        above.start()
        below.wait()
        inner(0).wait()
        wrap_rows(held, 1, count)

    inner(2 * step + 1).wait()
    wrap_rows(held, 2 * step + 2, count)

    @pl.when(2 * step + 2 < length)
    def _():
        inner(2 * step + 2).wait()
        wrap_rows(held, 2 * step + 3, count)

    @pl.when(2 * step + 2 >= length)
    def _():
        above.wait()


def chunks(size):
    return range(0, size, rows_at_once)


def transform(summed, z_table, y_table):
    count, half = len(summed), summed[0].shape[0]
    couples = []
    for k in range(0, count, 2):
        couples.append(jnp.concatenate([summed[k], summed[min(k + 1, count - 1)]], axis=1))
    in_z = right_dot(jnp.concatenate(couples, axis=0), z_table[...])
    in_z = [in_z[k * half : (k + 1) * half] for k in range(len(couples))]
    in_y = left_dot(y_table[...], jnp.concatenate(in_z, axis=1))
    blocks = half // 2
    lane = lax.broadcasted_iota(jnp.int32, (blocks, lanes), 1)
    results = []
    for k in range(count):
        both = in_y[:, (k // 2) * lanes : (k // 2 + 1) * lanes]
        upper, lower = both[:blocks], both[blocks:]
        if k % 2 == 0:
            results.append(jnp.where(lane < lanes // 2, upper, pltpu.roll(lower, lanes // 2, 1)))
        else:
            results.append(jnp.where(lane < lanes // 2, pltpu.roll(upper, lanes // 2, 1), lower))
    return results


def spectral(pairs, z_table, y_table, count):
    half = pairs.shape[1] // 2
    summed = [
        pairs[k, pl.ds(0, half, 2), :] + pairs[k, pl.ds(1, half, 2), :] for k in range(count)
    ]
    return transform(summed, z_table, y_table)


def sweep_one_kernel(is_first, source, low, high, s1, w, u, v, held, sems):
    step = pl.program_id(0)
    size = source.shape[2]
    arrive(step, source, low, high, held, sems)
    for row in chunks(size):
        rows = slice(row, row + rows_at_once)
        for part in range(2):
            plane = 2 * step + part + 1
            total_first, total_second, start, initial = None, None, None, None
            for node in range(3):
                center, old = rhs_rows(held, 3 * node, plane, pad + row)
                a, b = first[node], second[node] - (half_step if node == 1 else 0.0)
                if node == 0:
                    start, initial = center, old
                    total_first = [start[c] + a * old[c] for c in range(3)]
                    total_second = [b * old[c] for c in range(3)]
                else:
                    total_first = [total_first[c] + a * old[c] for c in range(3)]
                    total_second = [total_second[c] + b * old[c] for c in range(3)]
                if node == 0:
                    for c in range(3):
                        mine = first[0] * old[c] + is_first[0] * start[c]
                        other = second[0] * old[c]
                        if part == 1:
                            mine = mine + u[c, 0, rows, :]
                            other = other + v[c, 0, rows, :]
                        u[c, 0, rows, :] = mine
                        v[c, 0, rows, :] = other
            for c in range(3):
                s1[c, part, rows, :] = total_first[c]
                w[c, part, rows, :] = total_first[c] + total_second[c]
                u[c, 0, rows, :] = u[c, 0, rows, :] - total_first[c]
                v[c, 0, rows, :] = v[c, 0, rows, :] + total_first[c]


def sweep_two_kernel(
    group, source, low, high, w, u, v, z_table, y_table, s2, u_out, v_out, g, held, pairs, sems
):
    step = pl.program_id(0)
    size = source.shape[2]
    arrive(step, source, low, high, held, sems)
    for row in chunks(size):
        rows = slice(row, row + rows_at_once)
        fresh_sum, sweep_sum = None, None
        for part in range(2):
            _, fresh = rhs_rows(held, 0, 2 * step + part + 1, pad + row)
            swept = [w[c, part, rows, :] + half_step * fresh[c] for c in range(3)]
            for c in range(3):
                s2[c, part, rows, :] = swept[c]
            if part == 0:
                fresh_sum, sweep_sum = fresh, swept
            else:
                fresh_sum = [fresh_sum[c] + fresh[c] for c in range(3)]
                sweep_sum = [sweep_sum[c] + swept[c] for c in range(3)]
        for c in range(3):
            u_out[c, 0, rows, :] = u[c, 0, rows, :] + first[1] * fresh_sum[c]
            v_out[c, 0, rows, :] = v[c, 0, rows, :] + second[1] * fresh_sum[c] - sweep_sum[c]
            pairs[c, rows, :] = sweep_sum[c]
    planes = source.shape[1] // 2
    blocks = g.shape[0] // group
    for c, value in enumerate(spectral(pairs, z_table, y_table, 3)):
        g[pl.ds(c * planes + step, blocks, group), :] = value


def source_kernel(
    group, g_group, source, low, high, u, v, g, z_table, y_table, out, held, pairs, sems
):
    step = pl.program_id(0)
    size = source.shape[2]
    arrive(step, source, low, high, held, sems)
    for row in chunks(size):
        rows = slice(row, row + rows_at_once)
        _, fresh = rhs_rows(held, 0, 2 * step + 1, pad + row)
        _, other = rhs_rows(held, 0, 2 * step + 2, pad + row)
        for c in range(3):
            total = fresh[c] + other[c]
            pairs[c, rows, :] = u[c, 0, rows, :] + first[2] * total
            pairs[3 + c, rows, :] = v[c, 0, rows, :] + second[2] * total
    planes = source.shape[1] // 2
    blocks = out.shape[0] // group
    for k, value in enumerate(spectral(pairs, z_table, y_table, 6)):
        if k < 3:
            value = value + g[pl.ds(k * planes + step, blocks, g_group), :]
        out[pl.ds(k * planes + step, blocks, group), :] = value


def solve_kernel(
    peers, intervals, planes, group, back, values, inverse_in, table_in,
    sent_1, sent_2, inverse, table, out_1, out_2, sems, out_sems
):
    start_all([
        pltpu.make_async_copy(table_in, table, sems.at[0]),
        pltpu.make_async_copy(inverse_in, inverse, sems.at[1]),
    ])
    sending = []
    rows_x = peers * planes
    start = [None] * 3
    for interval in range(intervals):
        loaded = []
        for field in range(6):
            parts = [
                values[
                    pl.ds(interval * group + field * planes + p, peers, intervals * group), :
                ]
                for p in range(planes)
            ]
            loaded.append(jnp.concatenate(parts, axis=0))
        spectra = left_dot(table[:rows_x, :], jnp.concatenate(loaded, axis=1))
        rates = inverse[...]
        wanted = []
        for field in range(6):
            c = field % 3
            value = spectra[:, field * lanes : (field + 1) * lanes]
            if start[c] is not None:
                value = value + start[c]
            start[c] = value * rates
            wanted.append(start[c])
        physical = left_dot(table[rows_x:, :], jnp.concatenate(wanted, axis=1))
        for field in range(6):
            out = (out_1, out_2)[field // 3]
            base = (field % 3) * (planes + 2)
            for e in range(planes + 2):
                out[pl.ds(interval * back + base + e, peers, intervals * back), :] = physical[
                    e * peers : (e + 1) * peers, field * lanes : (field + 1) * lanes
                ]
        for peer in range(peers):
            rows = pl.ds((peer * intervals + interval) * back, back)
            for k, (out, sent) in enumerate(((out_1, sent_1), (out_2, sent_2))):
                sem = out_sems.at[k, peer * intervals + interval]
                sending.append(pltpu.make_async_copy(out.at[rows], sent.at[rows], sem))
                sending[-1].start()
    for copy in sending:
        copy.wait()


def edges_kernel(source, low, high, sems):
    length = source.shape[1]
    start_all([
        pltpu.make_async_copy(source.at[:, 0], low, sems.at[0]),
        pltpu.make_async_copy(source.at[:, length - 1], high, sems.at[1]),
    ])


def sweep_one_plane(is_first, held, slot, put_s1, put_w, uv, cell):
    size = held.shape[2] - 2 * pad
    for row in chunks(size):
        rows = slice(row, row + rows_at_once)
        total_first, total_second = [], []
        for node in range(3):
            start, old = rhs_rows(held, 3 * node, slot, pad + row)
            a, b = first[node], second[node] - (half_step if node == 1 else 0.0)
            if node == 0:
                for c in range(3):
                    uv[c, cell, rows, :] += first[0] * old[c] + is_first[0] * start[c]
                    uv[3 + c, cell, rows, :] += second[0] * old[c]
                total_first = [start[c] + a * old[c] for c in range(3)]
                total_second = [b * old[c] for c in range(3)]
            else:
                total_first = [total_first[c] + a * old[c] for c in range(3)]
                total_second = [total_second[c] + b * old[c] for c in range(3)]
        for c in range(3):
            put_s1(c, row, total_first[c])
            put_w(c, row, total_first[c] + total_second[c])
            uv[c, cell, rows, :] -= total_first[c]
            uv[3 + c, cell, rows, :] += total_first[c]


def sweep_two_plane(held, slot, get_w, put_s2, uv, cell):
    size = held.shape[2] - 2 * pad
    for row in chunks(size):
        rows = slice(row, row + rows_at_once)
        _, fresh = rhs_rows(held, 0, slot, pad + row)
        for c in range(3):
            swept = get_w(c, row) + half_step * fresh[c]
            put_s2(c, row, swept)
            uv[c, cell, rows, :] += first[1] * fresh[c]
            uv[3 + c, cell, rows, :] += second[1] * fresh[c] - swept


def last_rhs_pair(held, slot, uv, cell):
    size = held.shape[2] - 2 * pad
    for row in chunks(size):
        rows = slice(row, row + rows_at_once)
        _, fresh = rhs_rows(held, 0, slot, pad + row)
        _, other = rhs_rows(held, 0, slot + 1, pad + row)
        for c in range(3):
            total = fresh[c] + other[c]
            uv[c, cell, rows, :] += first[2] * total
            uv[3 + c, cell, rows, :] += second[2] * total


def uv_halves(uv, k, cell):
    half = uv.shape[2] // 2
    return uv[k, cell, pl.ds(0, half, 2), :] + uv[k, cell, pl.ds(1, half, 2), :]


def held_halves(held, c, slot):
    half = (held.shape[2] - 2 * pad) // 2
    total = held[c, slot, pl.ds(pad, half, 2), :] + held[c, slot, pl.ds(pad + 1, half, 2), :]
    total = total + held[c, slot + 1, pl.ds(pad, half, 2), :]
    return total + held[c, slot + 1, pl.ds(pad + 1, half, 2), :]


def interior_kernel(
    group, g_group, is_first, source, z_table, y_table,
    near, s1_out, s2_out, w_out, uv_end, uv_next, out, g,
    held, held_1, held_2, w, uv, sems, out_sems
):
    length, size = source.shape[1], source.shape[2]
    planes = length // 2
    blocks = out.shape[0] // group
    rows_all = pl.ds(pad, size)

    def arriving(plane):
        return pltpu.make_async_copy(
            source.at[:, plane], held.at[:, plane, rows_all, :], sems.at[plane]
        )

    def launch(plane, carry):
        arriving(plane).start()
        return carry

    lax.fori_loop(0, length, launch, 0)
    uv[...] = jnp.zeros(uv.shape, f32)
    arriving(0).wait()
    arriving(1).wait()
    wrap_rows(held, 1, 9)

    def s1_copy(plane):
        return pltpu.make_async_copy(
            held_1.at[:, plane, rows_all, :], s1_out.at[:, plane - 1], out_sems.at[0, plane]
        )

    def s2_copy(plane):
        return pltpu.make_async_copy(
            held_2.at[:, plane, rows_all, :], s2_out.at[:, plane - 2], out_sems.at[1, plane]
        )

    def phase_one(plane, carry):
        arriving(plane + 1).wait()
        wrap_rows(held, plane + 1, 9)

        def put_s1(c, row, value):
            held_1[c, plane, pad + row : pad + row + rows_at_once, :] = value

        def put_w(c, row, value):
            w[c, plane, row : row + rows_at_once, :] = value

        sweep_one_plane(is_first, held, plane, put_s1, put_w, uv, plane // 2)
        wrap_rows(held_1, plane, 3)
        s1_copy(plane).start()
        return carry

    lax.fori_loop(1, length - 1, phase_one, 0)

    def phase_two(plane, carry):
        def get_w(c, row):
            return w[c, plane, row : row + rows_at_once, :]

        def put_s2(c, row, value):
            held_2[c, plane, pad + row : pad + row + rows_at_once, :] = value

        sweep_two_plane(held_1, plane, get_w, put_s2, uv, plane // 2)
        wrap_rows(held_2, plane, 3)
        s2_copy(plane).start()
        return carry

    lax.fori_loop(2, length - 2, phase_two, 0)
    tails = []
    for k, plane in enumerate((0, 1, length - 2, length - 1)):
        tails.append(
            pltpu.make_async_copy(held.at[:, plane, rows_all, :], near.at[:, k], out_sems.at[2, 6 + k])
        )
    for k, plane in enumerate((1, length - 2)):
        tails.append(pltpu.make_async_copy(w.at[:, plane], w_out.at[:, k], out_sems.at[2, k]))
    for k, cell in enumerate((0, planes - 1)):
        tails.append(pltpu.make_async_copy(uv.at[:, cell], uv_end.at[:, k], out_sems.at[2, 2 + k]))
    for k, cell in enumerate((1, planes - 2)):
        tails.append(pltpu.make_async_copy(uv.at[:, cell], uv_next.at[:, k], out_sems.at[2, 4 + k]))
    for copy in tails:
        copy.start()

    def phase_three(cell, carry):
        last_rhs_pair(held_2, 2 * cell, uv, cell)
        return carry

    lax.fori_loop(2, planes - 2, phase_three, 0)
    for start in range(2, planes - 2, 2):
        cells = range(start, min(start + 2, planes - 2))
        entries = [(k, cell) for cell in cells for k in range(6)]
        values = transform([uv_halves(uv, k, cell) for k, cell in entries], z_table, y_table)
        for (k, cell), value in zip(entries, values):
            out[pl.ds(k * planes + cell, blocks, group), :] = value
    for start in range(1, planes - 1, 4):
        cells = range(start, min(start + 4, planes - 1))
        entries = [(c, cell) for cell in cells for c in range(3)]
        values = transform([held_halves(held_2, c, 2 * cell) for c, cell in entries], z_table, y_table)
        for (c, cell), value in zip(entries, values):
            g[pl.ds(c * planes + cell, blocks, g_group), :] = value

    def finish_one(plane, carry):
        s1_copy(plane).wait()
        return carry

    def finish_two(plane, carry):
        s2_copy(plane).wait()
        return carry

    lax.fori_loop(1, length - 1, finish_one, 0)
    lax.fori_loop(2, length - 2, finish_two, 0)
    for copy in tails:
        copy.wait()


def end_one_kernel(
    is_first, near, low, high, uv_in, pack, low_out, high_out, w_out, uv, held, sems, out_sems
):
    size = near.shape[2]
    rows_all = pl.ds(pad, size)
    sources = [low, *[near.at[:, k] for k in range(4)], high]
    start_all([
        pltpu.make_async_copy(ref, held.at[:, slot, rows_all, :], sems.at[slot])
        for slot, ref in enumerate(sources)
    ])
    packing = [
        pltpu.make_async_copy(held.at[0:3, slot, rows_all, :], pack.at[:, k], out_sems.at[k])
        for k, slot in enumerate((0, 5))
    ]
    for copy in packing:
        copy.start()
    uv[...] = uv_in[...]
    for k, (slot, ref) in enumerate(((1, low_out), (4, high_out))):
        wrap_rows(held, slot, 9)

        def put_s1(c, row, value):
            ref[c, row : row + rows_at_once, :] = value

        def put_w(c, row, value):
            w_out[c, k, row : row + rows_at_once, :] = value

        sweep_one_plane(is_first, held, slot, put_s1, put_w, uv, k)
    for copy in packing:
        copy.wait()


def end_two_kernel(
    g_group, swept, low, low_end, high_end, high, w_end, w_next, uv_in, z_table, y_table,
    pack, low_out, high_out, next_out, uv, g, held, held_2, sems, out_sems
):
    count, size = swept.shape[1], swept.shape[2]
    rows_all = pl.ds(pad, size)
    sources = [low, low_end, swept.at[:, 0], swept.at[:, 1]]
    sources += [swept.at[:, count - 2], swept.at[:, count - 1], high_end, high]
    start_all([
        pltpu.make_async_copy(ref, held.at[:, slot, rows_all, :], sems.at[slot])
        for slot, ref in enumerate(sources)
    ])
    packing = [
        pltpu.make_async_copy(held.at[:, slot, rows_all, :], pack.at[:, k], out_sems.at[k])
        for k, slot in enumerate((0, 1, 6, 7))
    ]
    for copy in packing:
        copy.start()
    uv[...] = uv_in[...]
    places = ((1, 0, w_end, 0), (2, 0, w_next, 0), (5, 1, w_next, 1), (6, 1, w_end, 1))
    for index, (slot, cell, w, k) in enumerate(places):
        wrap_rows(held, slot, 3)

        def get_w(c, row):
            return w[c, k, row : row + rows_at_once, :]

        def put_s2(c, row, value):
            rows = slice(row, row + rows_at_once)
            if slot == 1:
                low_out[c, rows, :] = value
            elif slot == 6:
                high_out[c, rows, :] = value
            else:
                next_out[c, k, rows, :] = value
            held_2[c, index, pad + row : pad + row + rows_at_once, :] = value

        sweep_two_plane(held, slot, get_w, put_s2, uv, cell)
    blocks = g.shape[0] // g_group
    entries = [(c, k) for k in range(2) for c in range(3)]
    values = transform([held_halves(held_2, c, 2 * k) for c, k in entries], z_table, y_table)
    for (c, k), value in zip(entries, values):
        g[pl.ds(2 * c + k, blocks, g_group), :] = value
    for copy in packing:
        copy.wait()


def end_three_kernel(
    group, g_group, end_group, swept, low, low_end, nexts, high_end, high, uv_end, uv_next, f, g, g_end,
    z_table, y_table, pack, sent, out, held, uv, sems, out_sems
):
    count, size = swept.shape[1], swept.shape[2]
    rows_all = pl.ds(pad, size)
    planes = (count + 4) // 2
    sources = [low, low_end, nexts.at[:, 0], swept.at[:, 0], swept.at[:, 1], swept.at[:, 2]]
    sources += [swept.at[:, count - 3], swept.at[:, count - 2], swept.at[:, count - 1]]
    sources += [nexts.at[:, 1], high_end, high]
    start_all([
        pltpu.make_async_copy(ref, held.at[:, slot, rows_all, :], sems.at[slot])
        for slot, ref in enumerate(sources)
    ])
    packing = [
        pltpu.make_async_copy(held.at[:, slot, rows_all, :], pack.at[:, k], out_sems.at[k])
        for k, slot in enumerate((0, 1, 2, 9, 10, 11))
    ]
    for k in range(2):
        uv[:, 3 * k] = uv_end[:, k]
        uv[:, 1 + k] = uv_next[:, k]
    out[...] = f[...]
    for slot in (1, 2, 3, 4, 7, 8, 9, 10):
        wrap_rows(held, slot, 3)
    for copy in packing:
        copy.start()
    for index, slot in enumerate((1, 3, 7, 9)):
        last_rhs_pair(held, slot, uv, index)
    blocks = out.shape[0] // group
    cells = (0, 1, planes - 2, planes - 1)
    for half in range(2):
        entries = [(k, index) for index in (2 * half, 2 * half + 1) for k in range(6)]
        values = transform([uv_halves(uv, k, index) for k, index in entries], z_table, y_table)
        for (k, index), value in zip(entries, values):
            if k < 3:
                if index % 3 == 0:
                    value = value + g_end[pl.ds(2 * k + index // 3, blocks, end_group), :]
                else:
                    value = value + g[pl.ds(k * planes + cells[index], blocks, g_group), :]
            out[pl.ds(k * planes + cells[index], blocks, group), :] = value
    for k in range(3):
        for cell in range(2, planes - 2):
            out[pl.ds(k * planes + cell, blocks, group), :] += g[
                pl.ds(k * planes + cell, blocks, g_group), :
            ]
    start_all([pltpu.make_async_copy(out, sent, out_sems.at[6])])
    for copy in packing:
        copy.wait()


def stage_kernel(layouts, counts, *refs):
    if len(layouts) > 1:
        is_first, refs = refs[0], refs[1:]
    fields, sems = refs[:counts], refs[-1]
    extras = (len(refs) - counts - 2) // 2
    staged = refs[counts + extras]
    rest = [
        pltpu.make_async_copy(refs[counts + k], refs[counts + extras + 1 + k], sems.at[k])
        for k in range(extras)
    ]
    for copy in rest:
        copy.start()

    def arriving(layout, slot):
        number, index = layout[slot]
        ref = fields[number]
        ref = ref.at[0:3, index] if index is not None else ref.at[0:3]
        return pltpu.make_async_copy(ref, staged.at[:, slot], sems.at[extras + slot])

    def launch(layout):
        for slot in range(len(layout)):
            arriving(layout, slot).start()

    if len(layouts) > 1:

        @pl.when(is_first[0] > 0)
        def _():
            launch(layouts[0])

        @pl.when(is_first[0] <= 0)
        def _():
            launch(layouts[1])
    else:
        launch(layouts[0])
    for slot in range(len(layouts[0])):
        arriving(layouts[0], slot).wait()
    for copy in rest:
        copy.wait()


def corrected_kernel(node, group, spectra, table, staged, *refs):
    new_velocity, new_rhs, held, coarse, result, out_sems, rhs_sems = refs[-7:]
    length, size = staged.shape[1] - 2, staged.shape[2]
    planes = length // 2
    rows_all = pl.ds(pad, size)
    z_rows = 3 * lanes
    y_rows, y_columns = size, 3 * size // 2
    blocks = spectra.shape[0] // group
    for c in range(3):
        base = c * (planes + 2)
        parts = [spectra[pl.ds(base + e, blocks, group), :] for e in range(planes + 2)]
        in_z = right_dot(jnp.concatenate(parts, axis=0), table[:z_rows, :])
        for e in range(planes + 2):
            mine = in_z[e * blocks : (e + 1) * blocks]
            stacked = jnp.concatenate([mine[:, :size], mine[:, size:]], axis=0)
            coarse[c, e] = left_dot(table[z_rows : z_rows + y_rows, :y_columns], stacked)

    def out_copy(plane):
        return pltpu.make_async_copy(
            held.at[:, plane + 1, rows_all, :], new_velocity.at[node, :, plane], out_sems.at[plane]
        )

    def rhs_copy(plane):
        return pltpu.make_async_copy(
            result.at[:, plane], new_rhs.at[node, :, plane], rhs_sems.at[plane]
        )

    def correct(plane, cell, odd):
        for field in range(3):
            for row in chunks(size):
                rows = slice(row, row + rows_at_once)
                held_rows = slice(pad + row, pad + row + rows_at_once)
                value = coarse[field, cell, rows, :]
                if odd:
                    value = 0.5 * (value + coarse[field, cell + 1, rows, :])
                held[field, plane, held_rows, :] = staged[field, plane, rows, :] + value
        wrap_rows(held, plane, 3)

    correct(0, 0, True)
    correct(1, 1, False)
    out_copy(0).start()

    def body(q, carry):
        correct(2 * q + 2, q + 1, True)
        correct(2 * q + 3, q + 2, False)
        out_copy(2 * q + 1).start()

        @pl.when(2 * q + 2 < length)
        def _():
            out_copy(2 * q + 2).start()

        for part in range(2):
            plane = 2 * q + part
            for row in chunks(size):
                _, fresh = rhs_rows(held, 0, plane + 1, pad + row)
                for c in range(3):
                    result[c, plane, row : row + rows_at_once, :] = fresh[c].astype(bf16)
            rhs_copy(plane).start()
        return carry

    lax.fori_loop(0, planes, body, 0)

    def finish(plane, carry):
        out_copy(plane).wait()
        rhs_copy(plane).wait()
        return carry

    lax.fori_loop(0, length, finish, 0)


anywhere = pl.BlockSpec(memory_space=pl.ANY)
scalar = pl.BlockSpec(memory_space=pltpu.SMEM)
vmem = pl.BlockSpec(memory_space=pltpu.VMEM)
hbm = pl.BlockSpec(memory_space=pltpu.HBM)


def whole(shape):
    return pl.BlockSpec(shape, lambda *index: (0,) * len(shape))


def struct(shape, dtype=f32):
    return jax.ShapeDtypeStruct(shape, dtype)


def slab(shape):
    return pl.BlockSpec(shape, lambda q: (0, q, 0, 0))


def held_planes(count, length, size_y, size_z):
    return pltpu.VMEM((count, length + 2, size_y + 2 * pad, size_z), f32)


def neighbours(low_plane, high_plane):
    count = lax.axis_size("space")
    up = [(i, (i + 1) % count) for i in range(count)]
    down = [(j, i) for i, j in up]
    return lax.ppermute(high_plane, "space", up), lax.ppermute(low_plane, "space", down)


def later_interval(value):
    count = lax.axis_size("tm")
    return lax.ppermute(value, "tm", [(i, i + 1) for i in range(count - 1)])


def stage(fields, layouts, is_first, extras=()):
    size_y, size_z = fields[0].shape[-2:]
    slots = len(layouts[0])
    operands, specs = [*fields, *extras], [anywhere] * (len(fields) + len(extras))
    if len(layouts) > 1:
        operands, specs = [is_first, *operands], [scalar, *specs]
    return pl.pallas_call(
        functools.partial(stage_kernel, layouts, len(fields)),
        out_shape=(struct((3, slots, size_y, size_z)), *[struct(e.shape, e.dtype) for e in extras]),
        in_specs=specs,
        out_specs=(vmem,) * (1 + len(extras)),
        scratch_shapes=[pltpu.SemaphoreType.DMA((slots + len(extras),))],
        compiler_params=params(8192 if len(layouts) == 1 else 57344),
        name="stage",
    )(*operands)


def corrected(node, spectra, table, staged, outs):
    length = staged.shape[1] - 2
    size_y, size_z = staged.shape[-2:]
    planes = length // 2
    group = spectra.shape[1]
    operands, specs = [spectra.reshape(-1, lanes), table, staged], [vmem] * 3
    shape = (3, 3, length, size_y, size_z)
    aliases = {}
    if outs is not None:
        aliases = {3: 0, 4: 1}
        operands, specs = [*operands, *outs], specs + [hbm] * 2
    return pl.pallas_call(
        functools.partial(corrected_kernel, node, group),
        out_shape=(struct(shape), struct(shape, bf16)),
        in_specs=specs,
        out_specs=(hbm, hbm),
        input_output_aliases=aliases,
        scratch_shapes=[
            held_planes(3, length, size_y, size_z),
            pltpu.VMEM((3, planes + 2, size_y, size_z), f32),
            pltpu.VMEM((3, length, size_y, size_z), bf16),
            pltpu.SemaphoreType.DMA((length,)),
            pltpu.SemaphoreType.DMA((length,)),
        ],
        compiler_params=params(16384),
        name=f"corrected_{node}",
    )(*operands)


def sweep_whole(fields, is_first, z_table, y_table, blocks):
    length, size_y, size_z = fields.shape[1:]
    planes = length // 2
    low, high = neighbours(fields[:, 0], fields[:, length - 1])
    fine = (3, length, size_y, size_z)
    halved = (3, planes, size_y, size_z)
    two = (3, 2, size_y, size_z)
    one = (3, 1, size_y, size_z)
    in_sems = pltpu.SemaphoreType.DMA((length + 2,))
    swept_1, w, u, v = pl.pallas_call(
        sweep_one_kernel,
        grid=(planes,),
        out_shape=(struct(fine), struct(fine), struct(halved), struct(halved)),
        in_specs=[scalar, anywhere, anywhere, anywhere],
        out_specs=(slab(two), slab(two), slab(one), slab(one)),
        scratch_shapes=[held_planes(9, length, size_y, size_z), in_sems],
        compiler_params=params(40960),
        name="sweep_one",
    )(is_first, fields, low, high)
    low_1, high_1 = neighbours(swept_1[:, 0], swept_1[:, length - 1])

    g_group = round_up(3 * planes, 8)
    swept_2, u, v, g = pl.pallas_call(
        functools.partial(sweep_two_kernel, g_group),
        grid=(planes,),
        out_shape=(struct(fine), struct(halved), struct(halved), struct((blocks * g_group, lanes))),
        in_specs=[anywhere, anywhere, anywhere, slab(two), slab(one), slab(one)]
        + [whole(z_table.shape), whole(y_table.shape)],
        out_specs=(slab(two), slab(one), slab(one), whole((blocks * g_group, lanes))),
        scratch_shapes=[
            held_planes(3, length, size_y, size_z),
            pltpu.VMEM((3, size_y, size_z), f32),
            in_sems,
        ],
        compiler_params=params(40960),
        name="sweep_two",
    )(swept_1, low_1, high_1, w, u, v, z_table, y_table)
    low_2, high_2 = neighbours(swept_2[:, 0], swept_2[:, length - 1])
    g = later_interval(g)

    group = round_up(6 * planes, 8)
    sources = pl.pallas_call(
        functools.partial(source_kernel, group, g_group),
        grid=(planes,),
        out_shape=struct((blocks * group, lanes)),
        in_specs=[anywhere, anywhere, anywhere, slab(one), slab(one), whole(g.shape)]
        + [whole(z_table.shape), whole(y_table.shape)],
        out_specs=whole((blocks * group, lanes)),
        scratch_shapes=[
            held_planes(3, length, size_y, size_z),
            pltpu.VMEM((6, size_y, size_z), f32),
            in_sems,
        ],
        compiler_params=params(40960),
        name="sources",
    )(swept_2, low_2, high_2, u, v, g, z_table, y_table)
    layout = tuple([(0, None)] + [(1, p) for p in range(length)] + [(2, None)])
    carried = [later_interval(value) for value in (low_2, swept_2, high_2)]
    later = tuple((3 + number, index) for number, index in layout)
    return (
        sources,
        ((low_1, swept_1, high_1), (layout,)),
        ((low_2, swept_2, high_2), (layout,)),
        ((low, fields, high, *carried), (layout, later)),
    )


def sweep_split(fields, is_first, z_table, y_table, blocks):
    length, size_y, size_z = fields.shape[1:]
    planes = length // 2
    plane, g_group, group = (size_y, size_z), round_up(3 * planes, 8), round_up(6 * planes, 8)

    def held(count, slots):
        return pltpu.VMEM((count, slots, size_y + 2 * pad, size_z), f32)

    def sems(*shape):
        return pltpu.SemaphoreType.DMA(shape)

    low, high = pl.pallas_call(
        edges_kernel,
        out_shape=(struct((9, *plane)),) * 2,
        in_specs=[hbm],
        out_specs=(vmem,) * 2,
        scratch_shapes=[sems(2)],
        compiler_params=params_but(300),
        name="edges",
    )(fields)
    low, high = neighbours(low, high)
    near, swept_1, swept_2, w_next, uv_end, uv_next, f, g = pl.pallas_call(
        functools.partial(interior_kernel, group, g_group),
        out_shape=(
            struct((9, 4, *plane)),
            struct((3, length - 2, *plane)),
            struct((3, length - 4, *plane)),
            struct((3, 2, *plane)),
            struct((6, 2, *plane)),
            struct((6, 2, *plane)),
            struct((blocks * group, lanes)),
            struct((blocks * g_group, lanes)),
        ),
        in_specs=[scalar, hbm, vmem, vmem],
        out_specs=(hbm,) * 6 + (vmem,) * 2,
        scratch_shapes=[
            held(9, length),
            held(3, length),
            held(3, length),
            pltpu.VMEM((3, length, *plane), f32),
            pltpu.VMEM((6, planes, *plane), f32),
            sems(length),
            sems(3, max(length, 10)),
        ],
        compiler_params=params(40960),
        cost_estimate=pl.CostEstimate(flops=4 * 10**9, bytes_accessed=6 * 10**7, transcendentals=0),
        name="interior",
    )(is_first, fields, z_table, y_table)
    g_moved = later_interval(g)
    pack_0, low_end_1, high_end_1, w_end, uv_end = pl.pallas_call(
        end_one_kernel,
        out_shape=(
            struct((3, 2, *plane)),
            struct((3, *plane)),
            struct((3, *plane)),
            struct((3, 2, *plane)),
            struct((6, 2, *plane)),
        ),
        in_specs=[scalar, anywhere, anywhere, anywhere, vmem],
        out_specs=(hbm,) + (vmem,) * 4,
        scratch_shapes=[held(9, 6), sems(6), sems(2)],
        compiler_params=params(16384),
        name="end_one",
    )(is_first, near, low, high, uv_end)
    low_1, high_1 = neighbours(low_end_1, high_end_1)
    end_group = 8
    pack_1, low_end_2, high_end_2, next_2, uv_end, g_end = pl.pallas_call(
        functools.partial(end_two_kernel, end_group),
        out_shape=(
            struct((3, 4, *plane)),
            struct((3, *plane)),
            struct((3, *plane)),
            struct((3, 2, *plane)),
            struct((6, 2, *plane)),
            struct((blocks * end_group, lanes)),
        ),
        in_specs=[hbm] + [anywhere] * 4 + [vmem] * 5,
        out_specs=(hbm,) + (vmem,) * 5,
        scratch_shapes=[held(3, 8), held(3, 4), sems(8), sems(4)],
        compiler_params=params(16384),
        name="end_two",
    )(swept_1, low_1, low_end_1, high_end_1, high_1, w_end, w_next, uv_end, z_table, y_table)
    low_2, high_2 = neighbours(low_end_2, high_end_2)
    pack, sources = pl.pallas_call(
        functools.partial(end_three_kernel, group, g_group, end_group),
        out_shape=(struct((3, 6, *plane)), struct((blocks * group, lanes))),
        in_specs=[hbm] + [anywhere] * 5 + [vmem] * 7,
        out_specs=(hbm, hbm),
        scratch_shapes=[
            pltpu.VMEM((blocks * group, lanes), f32),
            held(3, 12),
            pltpu.VMEM((6, 4, *plane), f32),
            sems(12),
            sems(7),
        ],
        compiler_params=params(16384),
        name="end_three",
    )(
        swept_2, low_2, low_end_2, next_2, high_end_2, high_2, uv_end, uv_next, f,
        g_moved, later_interval(g_end), z_table, y_table
    )
    inner_1 = [(1, p) for p in range(length - 2)]
    inner_2 = [(1, p) for p in range(length - 4)]
    layout_1 = [(0, 0), (0, 1)] + inner_1 + [(0, 2), (0, 3)]
    layout_2 = [(0, 0), (0, 1), (0, 2)] + inner_2 + [(0, 3), (0, 4), (0, 5)]
    layout_0 = [(2, 0)] + [(3, p) for p in range(length)] + [(2, 1)]
    return (
        sources,
        ((pack_1, swept_1), (tuple(layout_1),)),
        ((pack, swept_2), (tuple(layout_2),)),
        (
            (later_interval(pack), later_interval(swept_2), pack_0, fields),
            (tuple(layout_0), tuple(layout_2)),
        ),
    )


def per_device(velocity):
    length, size_y, size_z = velocity.shape[3:]
    planes = length // 2
    peers, intervals = lax.axis_size("space"), lax.axis_size("tm")
    devices = peers * intervals
    coarse_x, coarse_y, coarse_z = peers * planes, size_y // 2, size_z // 2
    blocks = coarse_y * coarse_z // lanes
    per_block = devices // blocks
    columns = lanes // per_block
    device = lax.axis_index("space") * intervals + lax.axis_index("tm")
    tm_first = lax.axis_index("tm") == 0
    fields = velocity.reshape(9, length, size_y, size_z)

    x_basis, y_basis, z_basis = basis(coarse_x), basis(coarse_y), basis(coarse_z)
    z_forward = 0.25 * pair_matrix(coarse_z) @ z_basis.T
    z_table = right_table(np.kron(np.eye(2), z_forward))
    y_table = left_table(0.5 * y_basis)
    order = np.arange(coarse_x).reshape(peers, planes).T.reshape(-1)
    x_forward = left_table(x_basis[:, order])
    wanted_x = np.arange(peers)[None, :] * planes + np.arange(-1, planes + 1)[:, None]
    x_backward = left_table(x_basis.T[wanted_x.reshape(-1) % coarse_x])
    z_back = (refine_matrix(coarse_z) @ z_basis.T).T
    z_back_table = right_table(np.kron(np.eye(2), z_back))
    y_back_table = left_table(refine_matrix(coarse_y) @ y_basis.T)
    y_of = np.arange(2)[:, None] * blocks + np.arange(blocks)[None, :]
    waves = wave_squares(coarse_y)[y_of.T][:, :, None] + wave_squares(coarse_z)[None, None, :]
    waves = waves.reshape(devices, columns)
    waves = np.pad(waves, ((0, 0), (0, lanes - columns)))
    mine = lax.dynamic_slice_in_dim(jnp.asarray(waves, f32), device, 1, axis=0)
    total = jnp.asarray(wave_squares(coarse_x), f32)[:, None] + mine
    rates = 1.0 / (1.0 + half_step * coarse_viscosity * (4.0 / (2.0 * 2.0)) * total)

    is_first = tm_first.astype(f32).reshape(1)
    sweep = sweep_split if length >= 10 else sweep_whole
    carried_at = 1 if length >= 10 else 4
    sources, one, two, zero = sweep(fields, is_first, z_table, y_table, blocks)
    group = round_up(6 * planes, 8)

    both = ("space", "tm")

    def to_columns(value, rows):
        if per_block > 1:
            value = value.reshape(blocks, rows, per_block, columns).swapaxes(1, 2)
        value = value.reshape(devices, rows, columns)
        value = lax.all_to_all(value, both, split_axis=0, concat_axis=0, tiled=True)
        value = jnp.pad(value, ((0, 0), (0, 0), (0, lanes - columns)))
        return value.reshape(devices * rows, lanes)

    def to_planes(value, rows):
        value = value.reshape(devices, rows, lanes)[:, :, :columns]
        value = lax.all_to_all(value, both, split_axis=0, concat_axis=0, tiled=True)
        if per_block > 1:
            value = value.reshape(blocks, per_block, rows, columns).swapaxes(1, 2)
        return value.reshape(blocks, rows, lanes)

    back = round_up(3 * (planes + 2), 8)
    x_table = np.concatenate([x_forward, x_backward], axis=0)
    y_back_table = np.pad(y_back_table, ((0, 0), (0, z_back_table.shape[1] - y_back_table.shape[1])))
    table = np.concatenate([z_back_table, y_back_table], axis=0)
    columned = to_columns(sources, group)
    columned, moved = lax.optimization_barrier((columned, zero[0][carried_at]))
    carried_fields = zero[0][:carried_at] + (moved,) + zero[0][carried_at + 1 :]
    solved_1, solved_2 = pl.pallas_call(
        functools.partial(solve_kernel, peers, intervals, planes, group, back),
        out_shape=(struct((devices * back, lanes)),) * 2,
        in_specs=[vmem, hbm, hbm],
        out_specs=(hbm, hbm),
        scratch_shapes=[
            pltpu.VMEM(rates.shape, f32),
            pltpu.VMEM(x_table.shape, bf16),
            pltpu.VMEM((devices * back, lanes), f32),
            pltpu.VMEM((devices * back, lanes), f32),
            pltpu.SemaphoreType.DMA((2,)),
            pltpu.SemaphoreType.DMA((2, devices)),
        ],
        compiler_params=params_but(790),
        name="solve",
    )(columned, rates, x_table)
    fields_1, fields_2, solved_2, solved_1 = lax.optimization_barrier(
        (one[0], two[0], solved_2, solved_1)
    )
    spectra_2 = to_planes(solved_2, back)
    staged_2, table = stage(fields_2, two[1], None, (jnp.asarray(table),))
    (staged_1,) = stage(fields_1, one[1], None)
    solved_1, staged_2, staged_1 = lax.optimization_barrier((solved_1, staged_2, staged_1))
    spectra_1 = to_planes(solved_1, back)
    (staged_0,) = stage(carried_fields, zero[1], is_first)
    outs = corrected(2, spectra_2, table, staged_2, None)
    outs = corrected(0, later_interval(spectra_2), table, staged_0, outs)
    new_velocity, new_rhs = corrected(1, spectra_1, table, staged_1, outs)
    return (new_velocity[None], new_rhs[None])


def solution(mesh):
    placed = P("tm", None, None, "space", None, None)
    return jax.shard_map(
        per_device,
        mesh=mesh,
        in_specs=(placed,),
        out_specs=(placed, placed),
        check_vma=False,
    )
```

```python
import functools

import jax
import jax.numpy as jnp
import ml_dtypes
import numpy as np
from jax import lax
from jax.experimental import pallas as pl
from jax.experimental.pallas import tpu as pltpu
from jax.sharding import PartitionSpec as P

viscosity = 1.0
coarse_viscosity = 10.0
time_step = 0.3
weights_first = (5.0 / 24.0, 1.0 / 3.0, -1.0 / 24.0)
weights_second = (-1.0 / 24.0, 1.0 / 3.0, 5.0 / 24.0)
half_step = 0.5 * time_step
first = tuple(time_step * w for w in weights_first)
second = tuple(time_step * w for w in weights_second)
lanes = 128
pad = 8
rows_at_once = 32


def params(kibibytes):
    return pltpu.CompilerParams(vmem_limit_bytes=kibibytes * 1024)


def params_but(kibibytes):
    return params(64 * 1024 - kibibytes)


f32 = jnp.float32
bf16 = jnp.bfloat16


def round_up(value, multiple):
    return -(-value // multiple) * multiple


def frequencies(length):
    index = np.arange(length)
    return np.where(index <= length // 2, index, index - length // 2)


def basis(length):
    index = np.arange(length)
    waves = frequencies(length)
    angles = 2.0 * np.pi * (waves[:, None] * index[None, :] % length) / length
    table = np.where(index[:, None] <= length // 2, np.cos(angles), np.sin(angles))
    edge = (waves == 0) | (2 * waves == length)
    return table * np.sqrt(np.where(edge, 1.0, 2.0) / length)[:, None]


def wave_squares(length):
    return np.sin(np.pi * frequencies(length) / length) ** 2


def refine_matrix(length):
    table = np.zeros((2 * length, length))
    for i in range(length):
        table[2 * i, i] += 1.0
        table[2 * i + 1, i] += 0.5
        table[2 * i + 1, (i + 1) % length] += 0.5
    return table


def pair_matrix(length):
    return np.repeat(np.eye(length), 2, axis=0)


def split(table):
    high = table.astype(np.float32).astype(ml_dtypes.bfloat16)
    low = (table - high.astype(np.float64)).astype(np.float32).astype(ml_dtypes.bfloat16)
    return high, low


def left_table(table):
    high, low = split(table)
    return np.concatenate([high, low, high], axis=1)


def right_table(table):
    high, low = split(table)
    return np.concatenate([high, low, high], axis=0)


def split_value(value):
    high = value.astype(bf16)
    return high, (value - high.astype(f32)).astype(bf16)


def left_dot(table, value):
    high, low = split_value(value)
    return jnp.dot(table, jnp.concatenate([high, high, low], axis=0), preferred_element_type=f32)


def right_dot(value, table):
    high, low = split_value(value)
    return jnp.dot(
        jnp.concatenate([high, high, low], axis=1), table, preferred_element_type=f32
    )


def start_all(copies):
    for copy in copies:
        copy.start()
    for copy in copies:
        copy.wait()


def wrap_rows(ref, plane, count):
    size = ref.shape[2] - 2 * pad
    for field in range(count):
        ref[field, plane, pad - 1 : pad, :] = ref[field, plane, pad + size - 1 : pad + size, :]
        ref[field, plane, pad + size : pad + size + 1, :] = ref[field, plane, pad : pad + 1, :]


def rhs_rows(ref, base, plane, start):
    stop = start + rows_at_once
    center = [ref[base + c, plane, start:stop, :] for c in range(3)]
    size = ref.shape[3]
    results = []
    for c in range(3):
        x_up = ref[base + c, plane + 1, start:stop, :]
        x_down = ref[base + c, plane - 1, start:stop, :]
        y_up = ref[base + c, plane, start + 1 : stop + 1, :]
        y_down = ref[base + c, plane, start - 1 : stop - 1, :]
        z_up = pltpu.roll(center[c], size - 1, 1)
        z_down = pltpu.roll(center[c], 1, 1)
        advect = (
            center[0] * (x_up - x_down) + center[1] * (y_up - y_down) + center[2] * (z_up - z_down)
        )
        laplace = (x_up + x_down) + (y_up + y_down) + (z_up + z_down) - 6.0 * center[c]
        results.append(viscosity * laplace - 0.5 * advect)
    return center, results


def planes_in(source, low, high, held, sems):
    length = source.shape[1]
    size = source.shape[2]
    rows = pl.ds(pad, size)

    def inner(plane):
        return pltpu.make_async_copy(
            source.at[:, plane], held.at[:, plane + 1, rows, :], sems.at[plane]
        )

    below = pltpu.make_async_copy(low, held.at[:, 0, rows, :], sems.at[length])
    above = pltpu.make_async_copy(high, held.at[:, length + 1, rows, :], sems.at[length + 1])
    return inner, below, above


def arrive(step, source, low, high, held, sems):
    length = source.shape[1]
    count = source.shape[0]
    inner, below, above = planes_in(source, low, high, held, sems)

    @pl.when(step == 0)
    def _():
        below.start()

        def launch(plane, carry):
            inner(plane).start()
            return carry

        lax.fori_loop(0, length, launch, 0)
        above.start()
        below.wait()
        inner(0).wait()
        wrap_rows(held, 1, count)

    inner(2 * step + 1).wait()
    wrap_rows(held, 2 * step + 2, count)

    @pl.when(2 * step + 2 < length)
    def _():
        inner(2 * step + 2).wait()
        wrap_rows(held, 2 * step + 3, count)

    @pl.when(2 * step + 2 >= length)
    def _():
        above.wait()


def chunks(size):
    return range(0, size, rows_at_once)


def transform(summed, z_table, y_table):
    count, half = len(summed), summed[0].shape[0]
    couples = []
    for k in range(0, count, 2):
        couples.append(jnp.concatenate([summed[k], summed[min(k + 1, count - 1)]], axis=1))
    in_z = right_dot(jnp.concatenate(couples, axis=0), z_table[...])
    in_z = [in_z[k * half : (k + 1) * half] for k in range(len(couples))]
    in_y = left_dot(y_table[...], jnp.concatenate(in_z, axis=1))
    blocks = half // 2
    lane = lax.broadcasted_iota(jnp.int32, (blocks, lanes), 1)
    results = []
    for k in range(count):
        both = in_y[:, (k // 2) * lanes : (k // 2 + 1) * lanes]
        upper, lower = both[:blocks], both[blocks:]
        if k % 2 == 0:
            results.append(jnp.where(lane < lanes // 2, upper, pltpu.roll(lower, lanes // 2, 1)))
        else:
            results.append(jnp.where(lane < lanes // 2, pltpu.roll(upper, lanes // 2, 1), lower))
    return results


def spectral(pairs, z_table, y_table, count):
    half = pairs.shape[1] // 2
    summed = [
        pairs[k, pl.ds(0, half, 2), :] + pairs[k, pl.ds(1, half, 2), :] for k in range(count)
    ]
    return transform(summed, z_table, y_table)


def sweep_one_kernel(is_first, source, low, high, s1, w, u, v, held, sems):
    step = pl.program_id(0)
    size = source.shape[2]
    arrive(step, source, low, high, held, sems)
    for row in chunks(size):
        rows = slice(row, row + rows_at_once)
        for part in range(2):
            plane = 2 * step + part + 1
            total_first, total_second, start, initial = None, None, None, None
            for node in range(3):
                center, old = rhs_rows(held, 3 * node, plane, pad + row)
                a, b = first[node], second[node] - (half_step if node == 1 else 0.0)
                if node == 0:
                    start, initial = center, old
                    total_first = [start[c] + a * old[c] for c in range(3)]
                    total_second = [b * old[c] for c in range(3)]
                else:
                    total_first = [total_first[c] + a * old[c] for c in range(3)]
                    total_second = [total_second[c] + b * old[c] for c in range(3)]
                if node == 0:
                    for c in range(3):
                        mine = first[0] * old[c] + is_first[0] * start[c]
                        other = second[0] * old[c]
                        if part == 1:
                            mine = mine + u[c, 0, rows, :]
                            other = other + v[c, 0, rows, :]
                        u[c, 0, rows, :] = mine
                        v[c, 0, rows, :] = other
            for c in range(3):
                s1[c, part, rows, :] = total_first[c]
                w[c, part, rows, :] = total_first[c] + total_second[c]
                u[c, 0, rows, :] = u[c, 0, rows, :] - total_first[c]
                v[c, 0, rows, :] = v[c, 0, rows, :] + total_first[c]


def sweep_two_kernel(
    group, source, low, high, w, u, v, z_table, y_table, s2, u_out, v_out, g, held, pairs, sems
):
    step = pl.program_id(0)
    size = source.shape[2]
    arrive(step, source, low, high, held, sems)
    for row in chunks(size):
        rows = slice(row, row + rows_at_once)
        fresh_sum, sweep_sum = None, None
        for part in range(2):
            _, fresh = rhs_rows(held, 0, 2 * step + part + 1, pad + row)
            swept = [w[c, part, rows, :] + half_step * fresh[c] for c in range(3)]
            for c in range(3):
                s2[c, part, rows, :] = swept[c]
            if part == 0:
                fresh_sum, sweep_sum = fresh, swept
            else:
                fresh_sum = [fresh_sum[c] + fresh[c] for c in range(3)]
                sweep_sum = [sweep_sum[c] + swept[c] for c in range(3)]
        for c in range(3):
            u_out[c, 0, rows, :] = u[c, 0, rows, :] + first[1] * fresh_sum[c]
            v_out[c, 0, rows, :] = v[c, 0, rows, :] + second[1] * fresh_sum[c] - sweep_sum[c]
            pairs[c, rows, :] = sweep_sum[c]
    planes = source.shape[1] // 2
    blocks = g.shape[0] // group
    for c, value in enumerate(spectral(pairs, z_table, y_table, 3)):
        g[pl.ds(c * planes + step, blocks, group), :] = value


def source_kernel(
    group, g_group, source, low, high, u, v, g, z_table, y_table, out, held, pairs, sems
):
    step = pl.program_id(0)
    size = source.shape[2]
    arrive(step, source, low, high, held, sems)
    for row in chunks(size):
        rows = slice(row, row + rows_at_once)
        _, fresh = rhs_rows(held, 0, 2 * step + 1, pad + row)
        _, other = rhs_rows(held, 0, 2 * step + 2, pad + row)
        for c in range(3):
            total = fresh[c] + other[c]
            pairs[c, rows, :] = u[c, 0, rows, :] + first[2] * total
            pairs[3 + c, rows, :] = v[c, 0, rows, :] + second[2] * total
    planes = source.shape[1] // 2
    blocks = out.shape[0] // group
    for k, value in enumerate(spectral(pairs, z_table, y_table, 6)):
        if k < 3:
            value = value + g[pl.ds(k * planes + step, blocks, g_group), :]
        out[pl.ds(k * planes + step, blocks, group), :] = value


def solve_kernel(
    peers, intervals, planes, group, back, values, inverse_in, table_in,
    sent_1, sent_2, inverse, table, out_1, out_2, sems, out_sems
):
    start_all([
        pltpu.make_async_copy(table_in, table, sems.at[0]),
        pltpu.make_async_copy(inverse_in, inverse, sems.at[1]),
    ])
    sending = []
    rows_x = peers * planes
    start = [None] * 3
    for interval in range(intervals):
        loaded = []
        for field in range(6):
            parts = [
                values[
                    pl.ds(interval * group + field * planes + p, peers, intervals * group), :
                ]
                for p in range(planes)
            ]
            loaded.append(jnp.concatenate(parts, axis=0))
        spectra = left_dot(table[:rows_x, :], jnp.concatenate(loaded, axis=1))
        rates = inverse[...]
        wanted = []
        for field in range(6):
            c = field % 3
            value = spectra[:, field * lanes : (field + 1) * lanes]
            if start[c] is not None:
                value = value + start[c]
            start[c] = value * rates
            wanted.append(start[c])
        physical = left_dot(table[rows_x:, :], jnp.concatenate(wanted, axis=1))
        for field in range(6):
            out = (out_1, out_2)[field // 3]
            base = (field % 3) * (planes + 2)
            for e in range(planes + 2):
                out[pl.ds(interval * back + base + e, peers, intervals * back), :] = physical[
                    e * peers : (e + 1) * peers, field * lanes : (field + 1) * lanes
                ]
        for peer in range(peers):
            rows = pl.ds((peer * intervals + interval) * back, back)
            for k, (out, sent) in enumerate(((out_1, sent_1), (out_2, sent_2))):
                sem = out_sems.at[k, peer * intervals + interval]
                sending.append(pltpu.make_async_copy(out.at[rows], sent.at[rows], sem))
                sending[-1].start()
    for copy in sending:
        copy.wait()


def edges_kernel(source, low, high, sems):
    length = source.shape[1]
    start_all([
        pltpu.make_async_copy(source.at[:, 0], low, sems.at[0]),
        pltpu.make_async_copy(source.at[:, length - 1], high, sems.at[1]),
    ])


def sweep_one_plane(is_first, held, slot, put_s1, put_w, uv, cell):
    size = held.shape[2] - 2 * pad
    for row in chunks(size):
        rows = slice(row, row + rows_at_once)
        total_first, total_second = [], []
        for node in range(3):
            start, old = rhs_rows(held, 3 * node, slot, pad + row)
            a, b = first[node], second[node] - (half_step if node == 1 else 0.0)
            if node == 0:
                for c in range(3):
                    uv[c, cell, rows, :] += first[0] * old[c] + is_first[0] * start[c]
                    uv[3 + c, cell, rows, :] += second[0] * old[c]
                total_first = [start[c] + a * old[c] for c in range(3)]
                total_second = [b * old[c] for c in range(3)]
            else:
                total_first = [total_first[c] + a * old[c] for c in range(3)]
                total_second = [total_second[c] + b * old[c] for c in range(3)]
        for c in range(3):
            put_s1(c, row, total_first[c])
            put_w(c, row, total_first[c] + total_second[c])
            uv[c, cell, rows, :] -= total_first[c]
            uv[3 + c, cell, rows, :] += total_first[c]


def sweep_two_plane(held, slot, get_w, put_s2, uv, cell):
    size = held.shape[2] - 2 * pad
    for row in chunks(size):
        rows = slice(row, row + rows_at_once)
        _, fresh = rhs_rows(held, 0, slot, pad + row)
        for c in range(3):
            swept = get_w(c, row) + half_step * fresh[c]
            put_s2(c, row, swept)
            uv[c, cell, rows, :] += first[1] * fresh[c]
            uv[3 + c, cell, rows, :] += second[1] * fresh[c] - swept


def last_rhs_pair(held, slot, uv, cell):
    size = held.shape[2] - 2 * pad
    for row in chunks(size):
        rows = slice(row, row + rows_at_once)
        _, fresh = rhs_rows(held, 0, slot, pad + row)
        _, other = rhs_rows(held, 0, slot + 1, pad + row)
        for c in range(3):
            total = fresh[c] + other[c]
            uv[c, cell, rows, :] += first[2] * total
            uv[3 + c, cell, rows, :] += second[2] * total


def last_rhs_one(held, slot, uv, cell):
    size = held.shape[2] - 2 * pad
    for row in chunks(size):
        rows = slice(row, row + rows_at_once)
        _, fresh = rhs_rows(held, 0, slot, pad + row)
        for c in range(3):
            uv[c, cell, rows, :] += first[2] * fresh[c]
            uv[3 + c, cell, rows, :] += second[2] * fresh[c]


def uv_halves(uv, k, cell):
    half = uv.shape[2] // 2
    return uv[k, cell, pl.ds(0, half, 2), :] + uv[k, cell, pl.ds(1, half, 2), :]


def held_halves(held, c, slot):
    half = (held.shape[2] - 2 * pad) // 2
    total = held[c, slot, pl.ds(pad, half, 2), :] + held[c, slot, pl.ds(pad + 1, half, 2), :]
    total = total + held[c, slot + 1, pl.ds(pad, half, 2), :]
    return total + held[c, slot + 1, pl.ds(pad + 1, half, 2), :]


def interior_kernel(
    group, g_group, is_first, source, z_table, y_table,
    near, s1_out, s2_out, w_out, uv_end, uv_next, out, g,
    held, held_1, held_2, w, uv, sems, out_sems
):
    length, size = source.shape[1], source.shape[2]
    planes = length // 2
    blocks = out.shape[0] // group
    rows_all = pl.ds(pad, size)

    def arriving(plane):
        return pltpu.make_async_copy(
            source.at[:, plane], held.at[:, plane, rows_all, :], sems.at[plane]
        )

    def launch(plane, carry):
        arriving(plane).start()
        return carry

    lax.fori_loop(0, length, launch, 0)
    uv[...] = jnp.zeros(uv.shape, f32)
    arriving(0).wait()
    arriving(1).wait()
    wrap_rows(held, 1, 9)

    def s1_copy(plane):
        return pltpu.make_async_copy(
            held_1.at[:, plane, rows_all, :], s1_out.at[:, plane - 1], out_sems.at[0, plane]
        )

    def s2_copy(plane):
        return pltpu.make_async_copy(
            held_2.at[:, plane, rows_all, :], s2_out.at[:, plane - 2], out_sems.at[1, plane]
        )

    def phase_one(plane, carry):
        arriving(plane + 1).wait()
        wrap_rows(held, plane + 1, 9)

        def put_s1(c, row, value):
            held_1[c, plane, pad + row : pad + row + rows_at_once, :] = value

        def put_w(c, row, value):
            w[c, plane, row : row + rows_at_once, :] = value

        sweep_one_plane(is_first, held, plane, put_s1, put_w, uv, plane // 2)
        wrap_rows(held_1, plane, 3)
        s1_copy(plane).start()
        return carry

    lax.fori_loop(1, length - 1, phase_one, 0)

    def phase_two(plane, carry):
        def get_w(c, row):
            return w[c, plane, row : row + rows_at_once, :]

        def put_s2(c, row, value):
            held_2[c, plane, pad + row : pad + row + rows_at_once, :] = value

        sweep_two_plane(held_1, plane, get_w, put_s2, uv, plane // 2)
        wrap_rows(held_2, plane, 3)
        s2_copy(plane).start()
        return carry

    lax.fori_loop(2, length - 2, phase_two, 0)
    tails = []
    for k, plane in enumerate((0, 1, length - 2, length - 1)):
        tails.append(
            pltpu.make_async_copy(held.at[:, plane, rows_all, :], near.at[:, k], out_sems.at[2, 6 + k])
        )
    for k, plane in enumerate((1, length - 2)):
        tails.append(pltpu.make_async_copy(w.at[:, plane], w_out.at[:, k], out_sems.at[2, k]))
    for k, cell in enumerate((0, planes - 1)):
        tails.append(pltpu.make_async_copy(uv.at[:, cell], uv_end.at[:, k], out_sems.at[2, 2 + k]))
    for k, cell in enumerate((1, planes - 2)):
        tails.append(pltpu.make_async_copy(uv.at[:, cell], uv_next.at[:, k], out_sems.at[2, 4 + k]))
    for copy in tails:
        copy.start()

    def phase_three(cell, carry):
        last_rhs_pair(held_2, 2 * cell, uv, cell)
        return carry

    lax.fori_loop(2, planes - 2, phase_three, 0)
    for start in range(2, planes - 2, 2):
        cells = range(start, min(start + 2, planes - 2))
        entries = [(k, cell) for cell in cells for k in range(6)]
        values = transform([uv_halves(uv, k, cell) for k, cell in entries], z_table, y_table)
        for (k, cell), value in zip(entries, values):
            out[pl.ds(k * planes + cell, blocks, group), :] = value
    for start in range(1, planes - 1, 4):
        cells = range(start, min(start + 4, planes - 1))
        entries = [(c, cell) for cell in cells for c in range(3)]
        values = transform([held_halves(held_2, c, 2 * cell) for c, cell in entries], z_table, y_table)
        for (c, cell), value in zip(entries, values):
            g[pl.ds(c * planes + cell, blocks, g_group), :] = value

    def finish_one(plane, carry):
        s1_copy(plane).wait()
        return carry

    def finish_two(plane, carry):
        s2_copy(plane).wait()
        return carry

    lax.fori_loop(1, length - 1, finish_one, 0)
    lax.fori_loop(2, length - 2, finish_two, 0)
    for copy in tails:
        copy.wait()


def end_one_kernel(
    is_first, near, low, high, uv_in, low_out, high_out, w_out, uv, held, sems
):
    size = near.shape[2]
    rows_all = pl.ds(pad, size)
    sources = [low, *[near.at[:, k] for k in range(4)], high]
    start_all([
        pltpu.make_async_copy(ref, held.at[:, slot, rows_all, :], sems.at[slot])
        for slot, ref in enumerate(sources)
    ])
    uv[...] = uv_in[...]
    for k, (slot, ref) in enumerate(((1, low_out), (4, high_out))):
        wrap_rows(held, slot, 9)

        def put_s1(c, row, value):
            ref[c, row : row + rows_at_once, :] = value

        def put_w(c, row, value):
            w_out[c, k, row : row + rows_at_once, :] = value

        sweep_one_plane(is_first, held, slot, put_s1, put_w, uv, k)


def end_two_kernel(
    g_group, swept, low, low_end, high_end, high, w_end, w_next, uv_in, z_table, y_table,
    low_out, high_out, next_out, uv, g, held, held_2, sems
):
    count, size = swept.shape[1], swept.shape[2]
    rows_all = pl.ds(pad, size)
    sources = [low, low_end, swept.at[:, 0], swept.at[:, 1]]
    sources += [swept.at[:, count - 2], swept.at[:, count - 1], high_end, high]
    start_all([
        pltpu.make_async_copy(ref, held.at[:, slot, rows_all, :], sems.at[slot])
        for slot, ref in enumerate(sources)
    ])
    uv[...] = uv_in[...]
    places = ((1, 0, w_end, 0), (2, 0, w_next, 0), (5, 1, w_next, 1), (6, 1, w_end, 1))
    for index, (slot, cell, w, k) in enumerate(places):
        wrap_rows(held, slot, 3)

        def get_w(c, row):
            return w[c, k, row : row + rows_at_once, :]

        def put_s2(c, row, value):
            rows = slice(row, row + rows_at_once)
            if slot == 1:
                low_out[c, rows, :] = value
            elif slot == 6:
                high_out[c, rows, :] = value
            else:
                next_out[c, k, rows, :] = value
            held_2[c, index, pad + row : pad + row + rows_at_once, :] = value

        sweep_two_plane(held, slot, get_w, put_s2, uv, cell)
    blocks = g.shape[0] // g_group
    entries = [(c, k) for k in range(2) for c in range(3)]
    values = transform([held_halves(held_2, c, 2 * k) for c, k in entries], z_table, y_table)
    for (c, k), value in zip(entries, values):
        g[pl.ds(2 * c + k, blocks, g_group), :] = value


def middle_kernel(
    group, swept, low_end, nexts, high_end, uv_in, uv_next, f, z_table, y_table,
    uv, out, held, near, sems
):
    count, size = swept.shape[1], swept.shape[2]
    planes = (count + 4) // 2
    rows_all = pl.ds(pad, size)
    sources = [low_end, nexts.at[:, 0], swept.at[:, 0], swept.at[:, 1], swept.at[:, 2]]
    sources += [swept.at[:, count - 3], swept.at[:, count - 2], swept.at[:, count - 1]]
    sources += [nexts.at[:, 1], high_end]
    start_all([
        pltpu.make_async_copy(ref, held.at[:, slot, rows_all, :], sems.at[slot])
        for slot, ref in enumerate(sources)
    ])
    uv[...] = uv_in[...]
    near[...] = uv_next[...]
    out[...] = f[...]
    for slot in (1, 2, 3, 6, 7, 8):
        wrap_rows(held, slot, 3)
    last_rhs_one(held, 1, uv, 0)
    last_rhs_one(held, 8, uv, 1)
    last_rhs_pair(held, 2, near, 0)
    last_rhs_pair(held, 6, near, 1)
    blocks = out.shape[0] // group
    entries = [(k, index) for index in range(2) for k in range(6)]
    values = transform([uv_halves(near, k, index) for k, index in entries], z_table, y_table)
    for (k, index), value in zip(entries, values):
        out[pl.ds(k * planes + (1, planes - 2)[index], blocks, group), :] = value


def end_three_kernel(
    group, g_group, end_group, low, low_end, nexts, high_end, high, uv_in, f, g, g_end,
    z_table, y_table, pack, sent, out, held, uv, sems, out_sems
):
    size = held.shape[2] - 2 * pad
    rows_all = pl.ds(pad, size)
    blocks = out.shape[0] // group
    planes = g.shape[0] // blocks // 3
    sources = [low, low_end, nexts.at[:, 0], nexts.at[:, 1], high_end, high]
    start_all([
        pltpu.make_async_copy(ref, held.at[:, slot, rows_all, :], sems.at[slot])
        for slot, ref in enumerate(sources)
    ])
    packing = [
        pltpu.make_async_copy(held.at[:, slot, rows_all, :], pack.at[:, slot], out_sems.at[slot])
        for slot in range(6)
    ]
    uv[...] = uv_in[...]
    out[...] = f[...]
    for slot in (1, 4):
        wrap_rows(held, slot, 3)
    for copy in packing:
        copy.start()
    last_rhs_one(held, 1, uv, 0)
    last_rhs_one(held, 4, uv, 1)
    entries = [(k, index) for index in range(2) for k in range(6)]
    values = transform([uv_halves(uv, k, index) for k, index in entries], z_table, y_table)
    for (k, index), value in zip(entries, values):
        if k < 3:
            value = value + g_end[pl.ds(2 * k + index, blocks, end_group), :]
        out[pl.ds(k * planes + index * (planes - 1), blocks, group), :] = value
    for k in range(3):
        for cell in range(1, planes - 1):
            out[pl.ds(k * planes + cell, blocks, group), :] += g[
                pl.ds(k * planes + cell, blocks, g_group), :
            ]
    start_all([pltpu.make_async_copy(out, sent, out_sems.at[6])])
    for copy in packing:
        copy.wait()


def place(fields, layouts, is_first, staged, sems):
    def launch(layout):
        for slot, (number, index) in enumerate(layout):
            ref = fields[number]
            ref = ref.at[0:3, index] if index is not None else ref.at[0:3]
            pltpu.make_async_copy(ref, staged.at[:, slot], sems.at[slot]).start()

    if len(layouts) > 1:
        pl.when(is_first[0] > 0)(functools.partial(launch, layouts[0]))
        pl.when(is_first[0] <= 0)(functools.partial(launch, layouts[1]))
    else:
        launch(layouts[0])


def corrected_kernel(node, group, layouts, count, is_first, spectra, table, *refs):
    new_velocity, new_rhs, held, staged, coarse, result, sems, out_sems, rhs_sems = refs[-9:]
    place(refs[:count], layouts, is_first, staged, sems)
    length, size = staged.shape[1] - 2, staged.shape[2]
    planes = length // 2
    rows_all = pl.ds(pad, size)
    z_rows = 3 * lanes
    y_rows, y_columns = size, 3 * size // 2
    blocks = spectra.shape[0] // group
    for c in range(3):
        base = c * (planes + 2)
        parts = [spectra[pl.ds(base + e, blocks, group), :] for e in range(planes + 2)]
        in_z = right_dot(jnp.concatenate(parts, axis=0), table[:z_rows, :])
        for e in range(0, planes + 2, 2):
            stacked = []
            for k in (e, min(e + 1, planes + 1)):
                mine = in_z[k * blocks : (k + 1) * blocks]
                stacked.append(jnp.concatenate([mine[:, :size], mine[:, size:]], axis=0))
            both = left_dot(
                table[z_rows : z_rows + y_rows, :y_columns], jnp.concatenate(stacked, axis=1)
            )
            for k in range(min(2, planes + 2 - e)):
                coarse[c, e + k] = both[:, k * size : (k + 1) * size]

    def out_copy(plane):
        return pltpu.make_async_copy(
            held.at[:, plane + 1, rows_all, :], new_velocity.at[node, :, plane], out_sems.at[plane]
        )

    def rhs_copy(plane):
        return pltpu.make_async_copy(
            result.at[:, plane], new_rhs.at[node, :, plane], rhs_sems.at[plane]
        )

    def correct(plane, cell, odd):
        pltpu.make_async_copy(staged.at[:, plane], staged.at[:, plane], sems.at[plane]).wait()
        for field in range(3):
            for row in chunks(size):
                rows = slice(row, row + rows_at_once)
                held_rows = slice(pad + row, pad + row + rows_at_once)
                value = coarse[field, cell, rows, :]
                if odd:
                    value = 0.5 * (value + coarse[field, cell + 1, rows, :])
                held[field, plane, held_rows, :] = staged[field, plane, rows, :] + value
        wrap_rows(held, plane, 3)

    correct(0, 0, True)
    correct(1, 1, False)
    out_copy(0).start()

    def body(q, carry):
        correct(2 * q + 2, q + 1, True)
        correct(2 * q + 3, q + 2, False)
        out_copy(2 * q + 1).start()

        @pl.when(2 * q + 2 < length)
        def _():
            out_copy(2 * q + 2).start()

        for part in range(2):
            plane = 2 * q + part
            for row in chunks(size):
                _, fresh = rhs_rows(held, 0, plane + 1, pad + row)
                for c in range(3):
                    result[c, plane, row : row + rows_at_once, :] = fresh[c].astype(bf16)
            rhs_copy(plane).start()
        return carry

    lax.fori_loop(0, planes, body, 0)

    def finish(plane, carry):
        out_copy(plane).wait()
        rhs_copy(plane).wait()
        return carry

    lax.fori_loop(0, length, finish, 0)


anywhere = pl.BlockSpec(memory_space=pl.ANY)
scalar = pl.BlockSpec(memory_space=pltpu.SMEM)
vmem = pl.BlockSpec(memory_space=pltpu.VMEM)
hbm = pl.BlockSpec(memory_space=pltpu.HBM)


def whole(shape):
    return pl.BlockSpec(shape, lambda *index: (0,) * len(shape))


def struct(shape, dtype=f32):
    return jax.ShapeDtypeStruct(shape, dtype)


def slab(shape):
    return pl.BlockSpec(shape, lambda q: (0, q, 0, 0))


def held_planes(count, length, size_y, size_z):
    return pltpu.VMEM((count, length + 2, size_y + 2 * pad, size_z), f32)


def neighbours(low_plane, high_plane):
    count = lax.axis_size("space")
    up = [(i, (i + 1) % count) for i in range(count)]
    down = [(j, i) for i, j in up]
    return lax.ppermute(high_plane, "space", up), lax.ppermute(low_plane, "space", down)


def later_interval(value):
    count = lax.axis_size("tm")
    return lax.ppermute(value, "tm", [(i, i + 1) for i in range(count - 1)])


def corrected(node, spectra, table, placed, outs, is_first):
    fields, layouts = placed
    group, slots, (size_y, size_z) = spectra.shape[1], len(layouts[0]), fields[0].shape[-2:]
    length, planes = slots - 2, slots // 2 - 1
    operands = [is_first, spectra.reshape(-1, lanes), table, *fields]
    specs = [scalar, vmem, vmem] + [anywhere] * len(fields)
    shape = (3, 3, length, size_y, size_z)
    aliases = {}
    if outs is not None:
        aliases = {len(operands): 0, len(operands) + 1: 1}
        operands, specs = [*operands, *outs], specs + [hbm] * 2
    return pl.pallas_call(
        functools.partial(corrected_kernel, node, group, layouts, len(fields)),
        out_shape=(struct(shape), struct(shape, bf16)),
        in_specs=specs,
        out_specs=(hbm, hbm),
        input_output_aliases=aliases,
        scratch_shapes=[
            held_planes(3, length, size_y, size_z),
            pltpu.VMEM((3, slots, size_y, size_z), f32),
            pltpu.VMEM((3, planes + 2, size_y, size_z), f32),
            pltpu.VMEM((3, length, size_y, size_z), bf16),
            pltpu.SemaphoreType.DMA((slots,)),
            pltpu.SemaphoreType.DMA((length,)),
            pltpu.SemaphoreType.DMA((length,)),
        ],
        compiler_params=params_but(560),
        name=f"corrected_{node}",
    )(*operands)


def sweep_whole(fields, is_first, z_table, y_table, blocks):
    length, size_y, size_z = fields.shape[1:]
    planes = length // 2
    low, high = neighbours(fields[:, 0], fields[:, length - 1])
    fine = (3, length, size_y, size_z)
    halved = (3, planes, size_y, size_z)
    two = (3, 2, size_y, size_z)
    one = (3, 1, size_y, size_z)
    in_sems = pltpu.SemaphoreType.DMA((length + 2,))
    swept_1, w, u, v = pl.pallas_call(
        sweep_one_kernel,
        grid=(planes,),
        out_shape=(struct(fine), struct(fine), struct(halved), struct(halved)),
        in_specs=[scalar, anywhere, anywhere, anywhere],
        out_specs=(slab(two), slab(two), slab(one), slab(one)),
        scratch_shapes=[held_planes(9, length, size_y, size_z), in_sems],
        compiler_params=params(40960),
        name="sweep_one",
    )(is_first, fields, low, high)
    low_1, high_1 = neighbours(swept_1[:, 0], swept_1[:, length - 1])

    g_group = round_up(3 * planes, 8)
    swept_2, u, v, g = pl.pallas_call(
        functools.partial(sweep_two_kernel, g_group),
        grid=(planes,),
        out_shape=(struct(fine), struct(halved), struct(halved), struct((blocks * g_group, lanes))),
        in_specs=[anywhere, anywhere, anywhere, slab(two), slab(one), slab(one)]
        + [whole(z_table.shape), whole(y_table.shape)],
        out_specs=(slab(two), slab(one), slab(one), whole((blocks * g_group, lanes))),
        scratch_shapes=[
            held_planes(3, length, size_y, size_z),
            pltpu.VMEM((3, size_y, size_z), f32),
            in_sems,
        ],
        compiler_params=params(40960),
        name="sweep_two",
    )(swept_1, low_1, high_1, w, u, v, z_table, y_table)
    low_2, high_2 = neighbours(swept_2[:, 0], swept_2[:, length - 1])
    g = later_interval(g)

    group = round_up(6 * planes, 8)
    sources = pl.pallas_call(
        functools.partial(source_kernel, group, g_group),
        grid=(planes,),
        out_shape=struct((blocks * group, lanes)),
        in_specs=[anywhere, anywhere, anywhere, slab(one), slab(one), whole(g.shape)]
        + [whole(z_table.shape), whole(y_table.shape)],
        out_specs=whole((blocks * group, lanes)),
        scratch_shapes=[
            held_planes(3, length, size_y, size_z),
            pltpu.VMEM((6, size_y, size_z), f32),
            in_sems,
        ],
        compiler_params=params(40960),
        name="sources",
    )(swept_2, low_2, high_2, u, v, g, z_table, y_table)
    layout = tuple([(0, None)] + [(1, p) for p in range(length)] + [(2, None)])
    carried = [later_interval(value) for value in (low_2, swept_2, high_2)]
    own = tuple((3 + number, index) for number, index in layout)
    return (
        sources,
        ((low_1, swept_1, high_1), (layout,)),
        ((low_2, swept_2, high_2), (layout,)),
        tuple(carried),
        ((low, fields, high), (own, layout)),
    )


def sweep_split(fields, is_first, z_table, y_table, blocks):
    length, size_y, size_z = fields.shape[1:]
    planes = length // 2
    plane, g_group, group = (size_y, size_z), round_up(3 * planes, 8), round_up(6 * planes, 8)

    def held(count, slots):
        return pltpu.VMEM((count, slots, size_y + 2 * pad, size_z), f32)

    def sems(*shape):
        return pltpu.SemaphoreType.DMA(shape)

    low, high = pl.pallas_call(
        edges_kernel,
        out_shape=(struct((9, *plane)),) * 2,
        in_specs=[hbm],
        out_specs=(vmem,) * 2,
        scratch_shapes=[sems(2)],
        compiler_params=params_but(300),
        name="edges",
    )(fields)
    low, high = neighbours(low, high)
    near, swept_1, swept_2, w_next, uv_end, uv_next, f, g = pl.pallas_call(
        functools.partial(interior_kernel, group, g_group),
        out_shape=(
            struct((9, 4, *plane)),
            struct((3, length - 2, *plane)),
            struct((3, length - 4, *plane)),
            struct((3, 2, *plane)),
            struct((6, 2, *plane)),
            struct((6, 2, *plane)),
            struct((blocks * group, lanes)),
            struct((blocks * g_group, lanes)),
        ),
        in_specs=[scalar, hbm, vmem, vmem],
        out_specs=(hbm,) * 6 + (vmem,) * 2,
        scratch_shapes=[
            held(9, length),
            held(3, length),
            held(3, length),
            pltpu.VMEM((3, length, *plane), f32),
            pltpu.VMEM((6, planes, *plane), f32),
            sems(length),
            sems(3, max(length, 10)),
        ],
        compiler_params=params(40960),
        cost_estimate=pl.CostEstimate(flops=4 * 10**9, bytes_accessed=6 * 10**7, transcendentals=0),
        name="interior",
    )(is_first, fields, z_table, y_table)
    g_moved = later_interval(g)
    low_end_1, high_end_1, w_end, uv_end = pl.pallas_call(
        end_one_kernel,
        out_shape=(
            struct((3, *plane)),
            struct((3, *plane)),
            struct((3, 2, *plane)),
            struct((6, 2, *plane)),
        ),
        in_specs=[scalar, anywhere, anywhere, anywhere, vmem],
        out_specs=(vmem,) * 4,
        scratch_shapes=[held(9, 6), sems(6)],
        compiler_params=params(16384),
        name="end_one",
    )(is_first, near, low, high, uv_end)
    low_1, high_1 = neighbours(low_end_1, high_end_1)
    end_group = 8
    low_end_2, high_end_2, next_2, uv_end, g_end = pl.pallas_call(
        functools.partial(end_two_kernel, end_group),
        out_shape=(
            struct((3, *plane)),
            struct((3, *plane)),
            struct((3, 2, *plane)),
            struct((6, 2, *plane)),
            struct((blocks * end_group, lanes)),
        ),
        in_specs=[hbm] + [anywhere] * 4 + [vmem] * 5,
        out_specs=(vmem,) * 5,
        scratch_shapes=[held(3, 8), held(3, 4), sems(8)],
        compiler_params=params(16384),
        name="end_two",
    )(swept_1, low_1, low_end_1, high_end_1, high_1, w_end, w_next, uv_end, z_table, y_table)
    low_2, high_2 = neighbours(low_end_2, high_end_2)
    uv_end, f = pl.pallas_call(
        functools.partial(middle_kernel, group),
        out_shape=(struct((6, 2, *plane)), struct((blocks * group, lanes))),
        in_specs=[hbm] + [anywhere] * 3 + [vmem] * 5,
        out_specs=(vmem,) * 2,
        scratch_shapes=[held(3, 10), pltpu.VMEM((6, 2, *plane), f32), sems(10)],
        compiler_params=params(16384),
        name="middle",
    )(swept_2, low_end_2, next_2, high_end_2, uv_end, uv_next, f, z_table, y_table)
    pack, sources = pl.pallas_call(
        functools.partial(end_three_kernel, group, g_group, end_group),
        out_shape=(struct((3, 6, *plane)), struct((blocks * group, lanes))),
        in_specs=[anywhere] * 5 + [vmem] * 6,
        out_specs=(hbm, hbm),
        scratch_shapes=[
            pltpu.VMEM((blocks * group, lanes), f32),
            held(3, 6),
            pltpu.VMEM((6, 2, *plane), f32),
            sems(6),
            sems(7),
        ],
        compiler_params=params(16384),
        name="end_three",
    )(
        low_2, low_end_2, next_2, high_end_2, high_2, uv_end, f,
        g_moved, later_interval(g_end), z_table, y_table
    )
    inner_1 = [(2, p) for p in range(length - 2)]
    inner_2 = [(1, p) for p in range(length - 4)]
    layout_1 = [(0, None), (1, None)] + inner_1 + [(3, None), (4, None)]
    layout_2 = [(0, 0), (0, 1), (0, 2)] + inner_2 + [(0, 3), (0, 4), (0, 5)]
    layout_0 = [(2, None)] + [(3, p) for p in range(length)] + [(4, None)]
    return (
        sources,
        ((low_1, low_end_1, swept_1, high_end_1, high_1), (tuple(layout_1),)),
        ((pack, swept_2), (tuple(layout_2),)),
        (later_interval(pack), later_interval(swept_2)),
        ((low, fields, high), (tuple(layout_0), tuple(layout_2))),
    )


def per_device(velocity):
    length, size_y, size_z = velocity.shape[3:]
    planes = length // 2
    peers, intervals = lax.axis_size("space"), lax.axis_size("tm")
    devices = peers * intervals
    coarse_x, coarse_y, coarse_z = peers * planes, size_y // 2, size_z // 2
    blocks = coarse_y * coarse_z // lanes
    per_block = devices // blocks
    columns = lanes // per_block
    device = lax.axis_index("space") * intervals + lax.axis_index("tm")
    tm_first = lax.axis_index("tm") == 0
    fields = velocity.reshape(9, length, size_y, size_z)

    x_basis, y_basis, z_basis = basis(coarse_x), basis(coarse_y), basis(coarse_z)
    z_forward = 0.25 * pair_matrix(coarse_z) @ z_basis.T
    z_table = right_table(np.kron(np.eye(2), z_forward))
    y_table = left_table(0.5 * y_basis)
    order = np.arange(coarse_x).reshape(peers, planes).T.reshape(-1)
    x_forward = left_table(x_basis[:, order])
    wanted_x = np.arange(peers)[None, :] * planes + np.arange(-1, planes + 1)[:, None]
    x_backward = left_table(x_basis.T[wanted_x.reshape(-1) % coarse_x])
    z_back = (refine_matrix(coarse_z) @ z_basis.T).T
    z_back_table = right_table(np.kron(np.eye(2), z_back))
    y_back_table = left_table(refine_matrix(coarse_y) @ y_basis.T)
    y_of = np.arange(2)[:, None] * blocks + np.arange(blocks)[None, :]
    waves = wave_squares(coarse_y)[y_of.T][:, :, None] + wave_squares(coarse_z)[None, None, :]
    waves = waves.reshape(devices, columns)
    waves = np.pad(waves, ((0, 0), (0, lanes - columns)))
    mine = lax.dynamic_slice_in_dim(jnp.asarray(waves, f32), device, 1, axis=0)
    total = jnp.asarray(wave_squares(coarse_x), f32)[:, None] + mine
    rates = 1.0 / (1.0 + half_step * coarse_viscosity * (4.0 / (2.0 * 2.0)) * total)

    is_first = tm_first.astype(f32).reshape(1)
    sweep = sweep_split if length >= 10 else sweep_whole
    moved_at = 1
    sources, one, two, carried, zero = sweep(fields, is_first, z_table, y_table, blocks)
    group = round_up(6 * planes, 8)

    both = ("space", "tm")

    def to_columns(value, rows):
        if per_block > 1:
            value = value.reshape(blocks, rows, per_block, columns).swapaxes(1, 2)
        value = value.reshape(devices, rows, columns)
        value = lax.all_to_all(value, both, split_axis=0, concat_axis=0, tiled=True)
        value = jnp.pad(value, ((0, 0), (0, 0), (0, lanes - columns)))
        return value.reshape(devices * rows, lanes)

    def to_planes(value, rows):
        value = value.reshape(devices, rows, lanes)[:, :, :columns]
        value = lax.all_to_all(value, both, split_axis=0, concat_axis=0, tiled=True)
        if per_block > 1:
            value = value.reshape(blocks, per_block, rows, columns).swapaxes(1, 2)
        return value.reshape(blocks, rows, lanes)

    back = round_up(3 * (planes + 2), 8)
    x_table = np.concatenate([x_forward, x_backward], axis=0)
    y_back_table = np.pad(y_back_table, ((0, 0), (0, z_back_table.shape[1] - y_back_table.shape[1])))
    table = np.concatenate([z_back_table, y_back_table], axis=0)
    columned = to_columns(sources, group)
    moved = carried[moved_at]
    columned, moved = lax.optimization_barrier((columned, moved))
    carried = (*carried[:moved_at], moved, *carried[moved_at + 1 :])
    solved_1, solved_2 = pl.pallas_call(
        functools.partial(solve_kernel, peers, intervals, planes, group, back),
        out_shape=(struct((devices * back, lanes)),) * 2,
        in_specs=[vmem, hbm, hbm],
        out_specs=(hbm, hbm),
        scratch_shapes=[
            pltpu.VMEM(rates.shape, f32),
            pltpu.VMEM(x_table.shape, bf16),
            pltpu.VMEM((devices * back, lanes), f32),
            pltpu.VMEM((devices * back, lanes), f32),
            pltpu.SemaphoreType.DMA((2,)),
            pltpu.SemaphoreType.DMA((2, devices)),
        ],
        compiler_params=params_but(790),
        name="solve",
    )(columned, rates, x_table)
    spectra_2 = to_planes(solved_2, back)
    solved_1, *carried = lax.optimization_barrier((solved_1, *carried))
    zero = ((*carried, *zero[0]), zero[1])
    spectra_1 = to_planes(solved_1, back)
    outs = corrected(2, spectra_2, table, two, None, is_first)
    outs = corrected(0, later_interval(spectra_2), table, zero, outs, is_first)
    new_velocity, new_rhs = corrected(1, spectra_1, table, one, outs, is_first)
    return (new_velocity[None], new_rhs[None])


def solution(mesh):
    placed = P("tm", None, None, "space", None, None)
    return jax.shard_map(
        per_device,
        mesh=mesh,
        in_specs=(placed,),
        out_specs=(placed, placed),
        check_vma=False,
    )
```

```python
import functools

import jax
import jax.numpy as jnp
import ml_dtypes
import numpy as np
from jax import lax
from jax.experimental import pallas as pl
from jax.experimental.pallas import tpu as pltpu
from jax.sharding import PartitionSpec as P

viscosity = 1.0
coarse_viscosity = 10.0
time_step = 0.3
weights_first = (5.0 / 24.0, 1.0 / 3.0, -1.0 / 24.0)
weights_second = (-1.0 / 24.0, 1.0 / 3.0, 5.0 / 24.0)
half_step = 0.5 * time_step
first = tuple(time_step * w for w in weights_first)
second = tuple(time_step * w for w in weights_second)
lanes = 128
pad = 8
rows_at_once = 32


def params(kibibytes):
    return pltpu.CompilerParams(vmem_limit_bytes=kibibytes * 1024)


def params_but(kibibytes):
    return params(64 * 1024 - kibibytes)


f32 = jnp.float32
bf16 = jnp.bfloat16


def round_up(value, multiple):
    return -(-value // multiple) * multiple


def frequencies(length):
    index = np.arange(length)
    return np.where(index <= length // 2, index, index - length // 2)


def basis(length):
    index = np.arange(length)
    waves = frequencies(length)
    angles = 2.0 * np.pi * (waves[:, None] * index[None, :] % length) / length
    table = np.where(index[:, None] <= length // 2, np.cos(angles), np.sin(angles))
    edge = (waves == 0) | (2 * waves == length)
    return table * np.sqrt(np.where(edge, 1.0, 2.0) / length)[:, None]


def wave_squares(length):
    return np.sin(np.pi * frequencies(length) / length) ** 2


def refine_matrix(length):
    table = np.zeros((2 * length, length))
    for i in range(length):
        table[2 * i, i] += 1.0
        table[2 * i + 1, i] += 0.5
        table[2 * i + 1, (i + 1) % length] += 0.5
    return table


def pair_matrix(length):
    return np.repeat(np.eye(length), 2, axis=0)


def split(table):
    high = table.astype(np.float32).astype(ml_dtypes.bfloat16)
    low = (table - high.astype(np.float64)).astype(np.float32).astype(ml_dtypes.bfloat16)
    return high, low


def left_table(table):
    high, low = split(table)
    return np.concatenate([high, low, high], axis=1)


def right_table(table):
    high, low = split(table)
    return np.concatenate([high, low, high], axis=0)


def split_value(value):
    high = value.astype(bf16)
    return high, (value - high.astype(f32)).astype(bf16)


def left_dot(table, value):
    high, low = split_value(value)
    return jnp.dot(table, jnp.concatenate([high, high, low], axis=0), preferred_element_type=f32)


def right_dot(value, table):
    high, low = split_value(value)
    return jnp.dot(
        jnp.concatenate([high, high, low], axis=1), table, preferred_element_type=f32
    )


def start_all(copies):
    for copy in copies:
        copy.start()
    for copy in copies:
        copy.wait()


def wrap_rows(ref, plane, count):
    size = ref.shape[2] - 2 * pad
    for field in range(count):
        ref[field, plane, pad - 1 : pad, :] = ref[field, plane, pad + size - 1 : pad + size, :]
        ref[field, plane, pad + size : pad + size + 1, :] = ref[field, plane, pad : pad + 1, :]


def rhs_rows(ref, base, plane, start):
    stop = start + rows_at_once
    center = [ref[base + c, plane, start:stop, :] for c in range(3)]
    size = ref.shape[3]
    results = []
    for c in range(3):
        x_up = ref[base + c, plane + 1, start:stop, :]
        x_down = ref[base + c, plane - 1, start:stop, :]
        y_up = ref[base + c, plane, start + 1 : stop + 1, :]
        y_down = ref[base + c, plane, start - 1 : stop - 1, :]
        z_up = pltpu.roll(center[c], size - 1, 1)
        z_down = pltpu.roll(center[c], 1, 1)
        advect = (
            center[0] * (x_up - x_down) + center[1] * (y_up - y_down) + center[2] * (z_up - z_down)
        )
        laplace = (x_up + x_down) + (y_up + y_down) + (z_up + z_down) - 6.0 * center[c]
        results.append(viscosity * laplace - 0.5 * advect)
    return center, results


def planes_in(source, low, high, held, sems):
    length = source.shape[1]
    size = source.shape[2]
    rows = pl.ds(pad, size)

    def inner(plane):
        return pltpu.make_async_copy(
            source.at[:, plane], held.at[:, plane + 1, rows, :], sems.at[plane]
        )

    below = pltpu.make_async_copy(low, held.at[:, 0, rows, :], sems.at[length])
    above = pltpu.make_async_copy(high, held.at[:, length + 1, rows, :], sems.at[length + 1])
    return inner, below, above


def arrive(step, source, low, high, held, sems):
    length = source.shape[1]
    count = source.shape[0]
    inner, below, above = planes_in(source, low, high, held, sems)

    @pl.when(step == 0)
    def _():
        below.start()

        def launch(plane, carry):
            inner(plane).start()
            return carry

        lax.fori_loop(0, length, launch, 0)
        above.start()
        below.wait()
        inner(0).wait()
        wrap_rows(held, 1, count)

    inner(2 * step + 1).wait()
    wrap_rows(held, 2 * step + 2, count)

    @pl.when(2 * step + 2 < length)
    def _():
        inner(2 * step + 2).wait()
        wrap_rows(held, 2 * step + 3, count)

    @pl.when(2 * step + 2 >= length)
    def _():
        above.wait()


def chunks(size):
    return range(0, size, rows_at_once)


def transform(summed, z_table, y_table):
    count, half = len(summed), summed[0].shape[0]
    couples = []
    for k in range(0, count, 2):
        couples.append(jnp.concatenate([summed[k], summed[min(k + 1, count - 1)]], axis=1))
    in_z = right_dot(jnp.concatenate(couples, axis=0), z_table[...])
    in_z = [in_z[k * half : (k + 1) * half] for k in range(len(couples))]
    in_y = left_dot(y_table[...], jnp.concatenate(in_z, axis=1))
    blocks = half // 2
    lane = lax.broadcasted_iota(jnp.int32, (blocks, lanes), 1)
    results = []
    for k in range(count):
        both = in_y[:, (k // 2) * lanes : (k // 2 + 1) * lanes]
        upper, lower = both[:blocks], both[blocks:]
        if k % 2 == 0:
            results.append(jnp.where(lane < lanes // 2, upper, pltpu.roll(lower, lanes // 2, 1)))
        else:
            results.append(jnp.where(lane < lanes // 2, pltpu.roll(upper, lanes // 2, 1), lower))
    return results


def spectral(pairs, z_table, y_table, count):
    half = pairs.shape[1] // 2
    summed = [
        pairs[k, pl.ds(0, half, 2), :] + pairs[k, pl.ds(1, half, 2), :] for k in range(count)
    ]
    return transform(summed, z_table, y_table)


def sweep_one_kernel(is_first, source, low, high, s1, w, u, v, held, sems):
    step = pl.program_id(0)
    size = source.shape[2]
    arrive(step, source, low, high, held, sems)
    for row in chunks(size):
        rows = slice(row, row + rows_at_once)
        for part in range(2):
            plane = 2 * step + part + 1
            total_first, total_second, start, initial = None, None, None, None
            for node in range(3):
                center, old = rhs_rows(held, 3 * node, plane, pad + row)
                a, b = first[node], second[node] - (half_step if node == 1 else 0.0)
                if node == 0:
                    start, initial = center, old
                    total_first = [start[c] + a * old[c] for c in range(3)]
                    total_second = [b * old[c] for c in range(3)]
                else:
                    total_first = [total_first[c] + a * old[c] for c in range(3)]
                    total_second = [total_second[c] + b * old[c] for c in range(3)]
                if node == 0:
                    for c in range(3):
                        mine = first[0] * old[c] + is_first[0] * start[c]
                        other = second[0] * old[c]
                        if part == 1:
                            mine = mine + u[c, 0, rows, :]
                            other = other + v[c, 0, rows, :]
                        u[c, 0, rows, :] = mine
                        v[c, 0, rows, :] = other
            for c in range(3):
                s1[c, part, rows, :] = total_first[c]
                w[c, part, rows, :] = total_first[c] + total_second[c]
                u[c, 0, rows, :] = u[c, 0, rows, :] - total_first[c]
                v[c, 0, rows, :] = v[c, 0, rows, :] + total_first[c]


def sweep_two_kernel(
    group, source, low, high, w, u, v, z_table, y_table, s2, u_out, v_out, g, held, pairs, sems
):
    step = pl.program_id(0)
    size = source.shape[2]
    arrive(step, source, low, high, held, sems)
    for row in chunks(size):
        rows = slice(row, row + rows_at_once)
        fresh_sum, sweep_sum = None, None
        for part in range(2):
            _, fresh = rhs_rows(held, 0, 2 * step + part + 1, pad + row)
            swept = [w[c, part, rows, :] + half_step * fresh[c] for c in range(3)]
            for c in range(3):
                s2[c, part, rows, :] = swept[c]
            if part == 0:
                fresh_sum, sweep_sum = fresh, swept
            else:
                fresh_sum = [fresh_sum[c] + fresh[c] for c in range(3)]
                sweep_sum = [sweep_sum[c] + swept[c] for c in range(3)]
        for c in range(3):
            u_out[c, 0, rows, :] = u[c, 0, rows, :] + first[1] * fresh_sum[c]
            v_out[c, 0, rows, :] = v[c, 0, rows, :] + second[1] * fresh_sum[c] - sweep_sum[c]
            pairs[c, rows, :] = sweep_sum[c]
    planes = source.shape[1] // 2
    blocks = g.shape[0] // group
    for c, value in enumerate(spectral(pairs, z_table, y_table, 3)):
        g[pl.ds(c * planes + step, blocks, group), :] = value


def source_kernel(
    group, g_group, source, low, high, u, v, g, z_table, y_table, out, held, pairs, sems
):
    step = pl.program_id(0)
    size = source.shape[2]
    arrive(step, source, low, high, held, sems)
    for row in chunks(size):
        rows = slice(row, row + rows_at_once)
        _, fresh = rhs_rows(held, 0, 2 * step + 1, pad + row)
        _, other = rhs_rows(held, 0, 2 * step + 2, pad + row)
        for c in range(3):
            total = fresh[c] + other[c]
            pairs[c, rows, :] = u[c, 0, rows, :] + first[2] * total
            pairs[3 + c, rows, :] = v[c, 0, rows, :] + second[2] * total
    planes = source.shape[1] // 2
    blocks = out.shape[0] // group
    for k, value in enumerate(spectral(pairs, z_table, y_table, 6)):
        if k < 3:
            value = value + g[pl.ds(k * planes + step, blocks, g_group), :]
        out[pl.ds(k * planes + step, blocks, group), :] = value


def solve_kernel(
    peers, intervals, planes, group, back, values, inverse_in, table_in,
    sent_1, sent_2, inverse, table, out_1, out_2, sems, out_sems
):
    start_all([
        pltpu.make_async_copy(table_in, table, sems.at[0]),
        pltpu.make_async_copy(inverse_in, inverse, sems.at[1]),
    ])
    sending = []
    rows_x = peers * planes
    start = [None] * 3
    for interval in range(intervals):
        loaded = []
        for field in range(6):
            parts = [
                values[
                    pl.ds(interval * group + field * planes + p, peers, intervals * group), :
                ]
                for p in range(planes)
            ]
            loaded.append(jnp.concatenate(parts, axis=0))
        spectra = left_dot(table[:rows_x, :], jnp.concatenate(loaded, axis=1))
        rates = inverse[...]
        wanted = []
        for field in range(6):
            c = field % 3
            value = spectra[:, field * lanes : (field + 1) * lanes]
            if start[c] is not None:
                value = value + start[c]
            start[c] = value * rates
            wanted.append(start[c])
        physical = left_dot(table[rows_x:, :], jnp.concatenate(wanted, axis=1))
        for field in range(6):
            out = (out_1, out_2)[field // 3]
            base = (field % 3) * (planes + 2)
            for e in range(planes + 2):
                out[pl.ds(interval * back + base + e, peers, intervals * back), :] = physical[
                    e * peers : (e + 1) * peers, field * lanes : (field + 1) * lanes
                ]
        for peer in range(peers):
            rows = pl.ds((peer * intervals + interval) * back, back)
            for k, (out, sent) in enumerate(((out_1, sent_1), (out_2, sent_2))):
                sem = out_sems.at[k, peer * intervals + interval]
                sending.append(pltpu.make_async_copy(out.at[rows], sent.at[rows], sem))
                sending[-1].start()
    for copy in sending:
        copy.wait()


def edges_kernel(source, low, high, sems):
    length = source.shape[1]
    start_all([
        pltpu.make_async_copy(source.at[:, 0], low, sems.at[0]),
        pltpu.make_async_copy(source.at[:, length - 1], high, sems.at[1]),
    ])


def sweep_one_plane(is_first, held, slot, put_s1, put_w, uv, cell):
    size = held.shape[2] - 2 * pad
    for row in chunks(size):
        rows = slice(row, row + rows_at_once)
        total_first, total_second = [], []
        for node in range(3):
            start, old = rhs_rows(held, 3 * node, slot, pad + row)
            a, b = first[node], second[node] - (half_step if node == 1 else 0.0)
            if node == 0:
                for c in range(3):
                    uv[c, cell, rows, :] += first[0] * old[c] + is_first[0] * start[c]
                    uv[3 + c, cell, rows, :] += second[0] * old[c]
                total_first = [start[c] + a * old[c] for c in range(3)]
                total_second = [b * old[c] for c in range(3)]
            else:
                total_first = [total_first[c] + a * old[c] for c in range(3)]
                total_second = [total_second[c] + b * old[c] for c in range(3)]
        for c in range(3):
            put_s1(c, row, total_first[c])
            put_w(c, row, total_first[c] + total_second[c])
            uv[c, cell, rows, :] -= total_first[c]
            uv[3 + c, cell, rows, :] += total_first[c]


def sweep_two_plane(held, slot, get_w, put_s2, uv, cell):
    size = held.shape[2] - 2 * pad
    for row in chunks(size):
        rows = slice(row, row + rows_at_once)
        _, fresh = rhs_rows(held, 0, slot, pad + row)
        for c in range(3):
            swept = get_w(c, row) + half_step * fresh[c]
            put_s2(c, row, swept)
            uv[c, cell, rows, :] += first[1] * fresh[c]
            uv[3 + c, cell, rows, :] += second[1] * fresh[c] - swept


def last_rhs_pair(held, slot, uv, cell):
    size = held.shape[2] - 2 * pad
    for row in chunks(size):
        rows = slice(row, row + rows_at_once)
        _, fresh = rhs_rows(held, 0, slot, pad + row)
        _, other = rhs_rows(held, 0, slot + 1, pad + row)
        for c in range(3):
            total = fresh[c] + other[c]
            uv[c, cell, rows, :] += first[2] * total
            uv[3 + c, cell, rows, :] += second[2] * total


def last_rhs_one(held, slot, uv, cell):
    size = held.shape[2] - 2 * pad
    for row in chunks(size):
        rows = slice(row, row + rows_at_once)
        _, fresh = rhs_rows(held, 0, slot, pad + row)
        for c in range(3):
            uv[c, cell, rows, :] += first[2] * fresh[c]
            uv[3 + c, cell, rows, :] += second[2] * fresh[c]


def uv_halves(uv, k, cell):
    half = uv.shape[2] // 2
    return uv[k, cell, pl.ds(0, half, 2), :] + uv[k, cell, pl.ds(1, half, 2), :]


def held_halves(held, c, slot):
    half = (held.shape[2] - 2 * pad) // 2
    total = held[c, slot, pl.ds(pad, half, 2), :] + held[c, slot, pl.ds(pad + 1, half, 2), :]
    total = total + held[c, slot + 1, pl.ds(pad, half, 2), :]
    return total + held[c, slot + 1, pl.ds(pad + 1, half, 2), :]


def interior_kernel(
    group, g_group, is_first, source, z_table, y_table,
    near, s1_out, s2_out, s2_side, w_out, uv_end, uv_next, out, g,
    held, held_1, held_2, w, uv, sems, out_sems
):
    length, size = source.shape[1], source.shape[2]
    planes = length // 2
    blocks = out.shape[0] // group
    rows_all = pl.ds(pad, size)

    def arriving(plane):
        return pltpu.make_async_copy(
            source.at[:, plane], held.at[:, plane, rows_all, :], sems.at[plane]
        )

    def launch(plane, carry):
        arriving(plane).start()
        return carry

    lax.fori_loop(0, length, launch, 0)
    uv[...] = jnp.zeros(uv.shape, f32)
    arriving(0).wait()
    arriving(1).wait()
    wrap_rows(held, 1, 9)

    def s1_copy(plane):
        return pltpu.make_async_copy(
            held_1.at[:, plane, rows_all, :], s1_out.at[:, plane - 1], out_sems.at[0, plane]
        )

    sides = (2, 3, length - 4, length - 3)

    def s2_copy(plane):
        inner = plane not in sides
        target = s2_out.at[:, plane - 4] if inner else s2_side.at[:, sides.index(plane)]
        return pltpu.make_async_copy(
            held_2.at[:, plane, rows_all, :], target, out_sems.at[1, plane]
        )

    def phase_one(plane, carry):
        arriving(plane + 1).wait()
        wrap_rows(held, plane + 1, 9)

        def put_s1(c, row, value):
            held_1[c, plane, pad + row : pad + row + rows_at_once, :] = value

        def put_w(c, row, value):
            w[c, plane, row : row + rows_at_once, :] = value

        sweep_one_plane(is_first, held, plane, put_s1, put_w, uv, plane // 2)
        wrap_rows(held_1, plane, 3)
        s1_copy(plane).start()
        return carry

    lax.fori_loop(1, length - 1, phase_one, 0)

    def phase_two(plane, carry):
        def get_w(c, row):
            return w[c, plane, row : row + rows_at_once, :]

        def put_s2(c, row, value):
            held_2[c, plane, pad + row : pad + row + rows_at_once, :] = value

        sweep_two_plane(held_1, plane, get_w, put_s2, uv, plane // 2)
        wrap_rows(held_2, plane, 3)
        return carry

    lax.fori_loop(2, length - 2, phase_two, 0)
    for plane in range(2, length - 2):
        s2_copy(plane).start()
    tails = []
    for k, plane in enumerate((0, 1, length - 2, length - 1)):
        tails.append(
            pltpu.make_async_copy(held.at[:, plane, rows_all, :], near.at[:, k], out_sems.at[2, 6 + k])
        )
    for k, plane in enumerate((1, length - 2)):
        tails.append(pltpu.make_async_copy(w.at[:, plane], w_out.at[:, k], out_sems.at[2, k]))
    for k, cell in enumerate((0, planes - 1)):
        tails.append(pltpu.make_async_copy(uv.at[:, cell], uv_end.at[:, k], out_sems.at[2, 2 + k]))
    for k, cell in enumerate((1, planes - 2)):
        tails.append(pltpu.make_async_copy(uv.at[:, cell], uv_next.at[:, k], out_sems.at[2, 4 + k]))
    for copy in tails:
        copy.start()

    def phase_three(cell, carry):
        last_rhs_pair(held_2, 2 * cell, uv, cell)
        return carry

    lax.fori_loop(2, planes - 2, phase_three, 0)
    for start in range(2, planes - 2, 2):
        cells = range(start, min(start + 2, planes - 2))
        entries = [(k, cell) for cell in cells for k in range(6)]
        values = transform([uv_halves(uv, k, cell) for k, cell in entries], z_table, y_table)
        for (k, cell), value in zip(entries, values):
            out[pl.ds(k * planes + cell, blocks, group), :] = value
    for start in range(1, planes - 1, 4):
        cells = range(start, min(start + 4, planes - 1))
        entries = [(c, cell) for cell in cells for c in range(3)]
        values = transform([held_halves(held_2, c, 2 * cell) for c, cell in entries], z_table, y_table)
        for (c, cell), value in zip(entries, values):
            g[pl.ds(c * planes + cell, blocks, g_group), :] = value

    def finish_one(plane, carry):
        s1_copy(plane).wait()
        return carry

    lax.fori_loop(1, length - 1, finish_one, 0)
    for plane in range(2, length - 2):
        s2_copy(plane).wait()
    for copy in tails:
        copy.wait()


def end_one_kernel(
    is_first, near, low, high, uv_in, low_out, high_out, w_out, uv, held, sems
):
    size = near.shape[2]
    rows_all = pl.ds(pad, size)
    sources = [low, *[near.at[:, k] for k in range(4)], high]
    start_all([
        pltpu.make_async_copy(ref, held.at[:, slot, rows_all, :], sems.at[slot])
        for slot, ref in enumerate(sources)
    ])
    uv[...] = uv_in[...]
    for k, (slot, ref) in enumerate(((1, low_out), (4, high_out))):
        wrap_rows(held, slot, 9)

        def put_s1(c, row, value):
            ref[c, row : row + rows_at_once, :] = value

        def put_w(c, row, value):
            w_out[c, k, row : row + rows_at_once, :] = value

        sweep_one_plane(is_first, held, slot, put_s1, put_w, uv, k)


def end_two_kernel(
    g_group, swept, low, low_end, high_end, high, w_end, w_next, uv_in, z_table, y_table,
    low_out, high_out, next_out, uv, g, held, held_2, sems
):
    count, size = swept.shape[1], swept.shape[2]
    rows_all = pl.ds(pad, size)
    sources = [low, low_end, swept.at[:, 0], swept.at[:, 1]]
    sources += [swept.at[:, count - 2], swept.at[:, count - 1], high_end, high]
    start_all([
        pltpu.make_async_copy(ref, held.at[:, slot, rows_all, :], sems.at[slot])
        for slot, ref in enumerate(sources)
    ])
    uv[...] = uv_in[...]
    places = ((1, 0, w_end, 0), (2, 0, w_next, 0), (5, 1, w_next, 1), (6, 1, w_end, 1))
    for index, (slot, cell, w, k) in enumerate(places):
        wrap_rows(held, slot, 3)

        def get_w(c, row):
            return w[c, k, row : row + rows_at_once, :]

        def put_s2(c, row, value):
            rows = slice(row, row + rows_at_once)
            if slot == 1:
                low_out[c, rows, :] = value
            elif slot == 6:
                high_out[c, rows, :] = value
            else:
                next_out[c, k, rows, :] = value
            held_2[c, index, pad + row : pad + row + rows_at_once, :] = value

        sweep_two_plane(held, slot, get_w, put_s2, uv, cell)
    blocks = g.shape[0] // g_group
    entries = [(c, k) for k in range(2) for c in range(3)]
    values = transform([held_halves(held_2, c, 2 * k) for c, k in entries], z_table, y_table)
    for (c, k), value in zip(entries, values):
        g[pl.ds(2 * c + k, blocks, g_group), :] = value


def middle_kernel(
    group, swept, side, low_end, nexts, high_end, uv_in, uv_next, f, z_table, y_table,
    uv, out, held, near, sems
):
    count, size = swept.shape[1], swept.shape[2]
    planes = (count + 8) // 2
    rows_all = pl.ds(pad, size)
    sources = [low_end, nexts.at[:, 0], side.at[:, 0], side.at[:, 1], swept.at[:, 0]]
    sources += [swept.at[:, count - 1], side.at[:, 2], side.at[:, 3], nexts.at[:, 1], high_end]
    start_all([
        pltpu.make_async_copy(ref, held.at[:, slot, rows_all, :], sems.at[slot])
        for slot, ref in enumerate(sources)
    ])
    uv[...] = uv_in[...]
    near[...] = uv_next[...]
    out[...] = f[...]
    for slot in (1, 2, 3, 6, 7, 8):
        wrap_rows(held, slot, 3)
    last_rhs_one(held, 1, uv, 0)
    last_rhs_one(held, 8, uv, 1)
    last_rhs_pair(held, 2, near, 0)
    last_rhs_pair(held, 6, near, 1)
    blocks = out.shape[0] // group
    entries = [(k, index) for index in range(2) for k in range(6)]
    values = transform([uv_halves(near, k, index) for k, index in entries], z_table, y_table)
    for (k, index), value in zip(entries, values):
        out[pl.ds(k * planes + (1, planes - 2)[index], blocks, group), :] = value


def end_three_kernel(
    group, g_group, end_group, side, low, low_end, nexts, high_end, high, uv_in, f, g, g_end,
    z_table, y_table, pack, sent, out, held, side_held, uv, sems, out_sems
):
    size = held.shape[2] - 2 * pad
    rows_all = pl.ds(pad, size)
    blocks = out.shape[0] // group
    planes = g.shape[0] // blocks // 3
    sources = [low, low_end, nexts.at[:, 0], nexts.at[:, 1], high_end, high]
    side_in = pltpu.make_async_copy(side, side_held, sems.at[6])
    side_in.start()
    start_all([
        pltpu.make_async_copy(ref, held.at[:, slot, rows_all, :], sems.at[slot])
        for slot, ref in enumerate(sources)
    ])
    packing = [
        pltpu.make_async_copy(
            held.at[:, slot, rows_all, :], pack.at[:, (0, 1, 2, 7, 8, 9)[slot]], out_sems.at[slot]
        )
        for slot in range(6)
    ]
    packing.append(pltpu.make_async_copy(side_held, pack.at[:, 3:7], out_sems.at[7]))
    uv[...] = uv_in[...]
    out[...] = f[...]
    for slot in (1, 4):
        wrap_rows(held, slot, 3)
    side_in.wait()
    for copy in packing:
        copy.start()
    last_rhs_one(held, 1, uv, 0)
    last_rhs_one(held, 4, uv, 1)
    entries = [(k, index) for index in range(2) for k in range(6)]
    values = transform([uv_halves(uv, k, index) for k, index in entries], z_table, y_table)
    for (k, index), value in zip(entries, values):
        if k < 3:
            value = value + g_end[pl.ds(2 * k + index, blocks, end_group), :]
        out[pl.ds(k * planes + index * (planes - 1), blocks, group), :] = value
    for k in range(3):
        for cell in range(1, planes - 1):
            out[pl.ds(k * planes + cell, blocks, group), :] += g[
                pl.ds(k * planes + cell, blocks, g_group), :
            ]
    start_all([pltpu.make_async_copy(out, sent, out_sems.at[6])])
    for copy in packing:
        copy.wait()


def place(fields, layouts, is_first, staged, sems):
    def launch(layout):
        for slot, (number, index) in enumerate(layout):
            ref = fields[number]
            ref = ref.at[0:3, index] if index is not None else ref.at[0:3]
            pltpu.make_async_copy(ref, staged.at[:, slot], sems.at[slot]).start()

    if len(layouts) > 1:
        pl.when(is_first[0] > 0)(functools.partial(launch, layouts[0]))
        pl.when(is_first[0] <= 0)(functools.partial(launch, layouts[1]))
    else:
        launch(layouts[0])


def corrected_kernel(node, group, layouts, count, is_first, spectra, table, *refs):
    new_velocity, new_rhs, held, staged, coarse, result, sems, out_sems, rhs_sems = refs[-9:]
    place(refs[:count], layouts, is_first, staged, sems)
    length, size = staged.shape[1] - 2, staged.shape[2]
    planes = length // 2
    rows_all = pl.ds(pad, size)
    z_rows = 3 * lanes
    y_rows, y_columns = size, 3 * size // 2
    blocks = spectra.shape[0] // group
    for c in range(3):
        base = c * (planes + 2)
        parts = [spectra[pl.ds(base + e, blocks, group), :] for e in range(planes + 2)]
        in_z = right_dot(jnp.concatenate(parts, axis=0), table[:z_rows, :])
        for e in range(0, planes + 2, 2):
            stacked = []
            for k in (e, min(e + 1, planes + 1)):
                mine = in_z[k * blocks : (k + 1) * blocks]
                stacked.append(jnp.concatenate([mine[:, :size], mine[:, size:]], axis=0))
            both = left_dot(
                table[z_rows : z_rows + y_rows, :y_columns], jnp.concatenate(stacked, axis=1)
            )
            for k in range(min(2, planes + 2 - e)):
                coarse[c, e + k] = both[:, k * size : (k + 1) * size]

    def out_copy(plane):
        return pltpu.make_async_copy(
            held.at[:, plane + 1, rows_all, :], new_velocity.at[node, :, plane], out_sems.at[plane]
        )

    def rhs_copy(plane):
        return pltpu.make_async_copy(
            result.at[:, plane], new_rhs.at[node, :, plane], rhs_sems.at[plane]
        )

    def correct(plane, cell, odd):
        pltpu.make_async_copy(staged.at[:, plane], staged.at[:, plane], sems.at[plane]).wait()
        for field in range(3):
            for row in chunks(size):
                rows = slice(row, row + rows_at_once)
                held_rows = slice(pad + row, pad + row + rows_at_once)
                value = coarse[field, cell, rows, :]
                if odd:
                    value = 0.5 * (value + coarse[field, cell + 1, rows, :])
                held[field, plane, held_rows, :] = staged[field, plane, rows, :] + value
        wrap_rows(held, plane, 3)

    correct(0, 0, True)
    correct(1, 1, False)
    out_copy(0).start()

    def body(q, carry):
        correct(2 * q + 2, q + 1, True)
        correct(2 * q + 3, q + 2, False)
        out_copy(2 * q + 1).start()

        @pl.when(2 * q + 2 < length)
        def _():
            out_copy(2 * q + 2).start()

        for part in range(2):
            plane = 2 * q + part
            for row in chunks(size):
                _, fresh = rhs_rows(held, 0, plane + 1, pad + row)
                for c in range(3):
                    result[c, plane, row : row + rows_at_once, :] = fresh[c].astype(bf16)
            rhs_copy(plane).start()
        return carry

    lax.fori_loop(0, planes, body, 0)

    def finish(plane, carry):
        out_copy(plane).wait()
        rhs_copy(plane).wait()
        return carry

    lax.fori_loop(0, length, finish, 0)


anywhere = pl.BlockSpec(memory_space=pl.ANY)
scalar = pl.BlockSpec(memory_space=pltpu.SMEM)
vmem = pl.BlockSpec(memory_space=pltpu.VMEM)
hbm = pl.BlockSpec(memory_space=pltpu.HBM)


def whole(shape):
    return pl.BlockSpec(shape, lambda *index: (0,) * len(shape))


def struct(shape, dtype=f32):
    return jax.ShapeDtypeStruct(shape, dtype)


def slab(shape):
    return pl.BlockSpec(shape, lambda q: (0, q, 0, 0))


def held_planes(count, length, size_y, size_z):
    return pltpu.VMEM((count, length + 2, size_y + 2 * pad, size_z), f32)


def neighbours(low_plane, high_plane):
    count = lax.axis_size("space")
    up = [(i, (i + 1) % count) for i in range(count)]
    down = [(j, i) for i, j in up]
    return lax.ppermute(high_plane, "space", up), lax.ppermute(low_plane, "space", down)


def later_interval(value):
    count = lax.axis_size("tm")
    return lax.ppermute(value, "tm", [(i, i + 1) for i in range(count - 1)])


def corrected(node, spectra, table, placed, outs, is_first):
    fields, layouts = placed
    group, slots, (size_y, size_z) = spectra.shape[1], len(layouts[0]), fields[0].shape[-2:]
    length, planes = slots - 2, slots // 2 - 1
    operands = [is_first, spectra.reshape(-1, lanes), table, *fields]
    specs = [scalar, vmem, vmem] + [anywhere] * len(fields)
    shape = (3, 3, length, size_y, size_z)
    aliases = {}
    if outs is not None:
        aliases = {len(operands): 0, len(operands) + 1: 1}
        operands, specs = [*operands, *outs], specs + [hbm] * 2
    return pl.pallas_call(
        functools.partial(corrected_kernel, node, group, layouts, len(fields)),
        out_shape=(struct(shape), struct(shape, bf16)),
        in_specs=specs,
        out_specs=(hbm, hbm),
        input_output_aliases=aliases,
        scratch_shapes=[
            held_planes(3, length, size_y, size_z),
            pltpu.VMEM((3, slots, size_y, size_z), f32),
            pltpu.VMEM((3, planes + 2, size_y, size_z), f32),
            pltpu.VMEM((3, length, size_y, size_z), bf16),
            pltpu.SemaphoreType.DMA((slots,)),
            pltpu.SemaphoreType.DMA((length,)),
            pltpu.SemaphoreType.DMA((length,)),
        ],
        compiler_params=params_but(560),
        name=f"corrected_{node}",
    )(*operands)


def sweep_whole(fields, is_first, z_table, y_table, blocks):
    length, size_y, size_z = fields.shape[1:]
    planes = length // 2
    low, high = neighbours(fields[:, 0], fields[:, length - 1])
    fine = (3, length, size_y, size_z)
    halved = (3, planes, size_y, size_z)
    two = (3, 2, size_y, size_z)
    one = (3, 1, size_y, size_z)
    in_sems = pltpu.SemaphoreType.DMA((length + 2,))
    swept_1, w, u, v = pl.pallas_call(
        sweep_one_kernel,
        grid=(planes,),
        out_shape=(struct(fine), struct(fine), struct(halved), struct(halved)),
        in_specs=[scalar, anywhere, anywhere, anywhere],
        out_specs=(slab(two), slab(two), slab(one), slab(one)),
        scratch_shapes=[held_planes(9, length, size_y, size_z), in_sems],
        compiler_params=params(40960),
        name="sweep_one",
    )(is_first, fields, low, high)
    low_1, high_1 = neighbours(swept_1[:, 0], swept_1[:, length - 1])

    g_group = round_up(3 * planes, 8)
    swept_2, u, v, g = pl.pallas_call(
        functools.partial(sweep_two_kernel, g_group),
        grid=(planes,),
        out_shape=(struct(fine), struct(halved), struct(halved), struct((blocks * g_group, lanes))),
        in_specs=[anywhere, anywhere, anywhere, slab(two), slab(one), slab(one)]
        + [whole(z_table.shape), whole(y_table.shape)],
        out_specs=(slab(two), slab(one), slab(one), whole((blocks * g_group, lanes))),
        scratch_shapes=[
            held_planes(3, length, size_y, size_z),
            pltpu.VMEM((3, size_y, size_z), f32),
            in_sems,
        ],
        compiler_params=params(40960),
        name="sweep_two",
    )(swept_1, low_1, high_1, w, u, v, z_table, y_table)
    low_2, high_2 = neighbours(swept_2[:, 0], swept_2[:, length - 1])
    g = later_interval(g)

    group = round_up(6 * planes, 8)
    sources = pl.pallas_call(
        functools.partial(source_kernel, group, g_group),
        grid=(planes,),
        out_shape=struct((blocks * group, lanes)),
        in_specs=[anywhere, anywhere, anywhere, slab(one), slab(one), whole(g.shape)]
        + [whole(z_table.shape), whole(y_table.shape)],
        out_specs=whole((blocks * group, lanes)),
        scratch_shapes=[
            held_planes(3, length, size_y, size_z),
            pltpu.VMEM((6, size_y, size_z), f32),
            in_sems,
        ],
        compiler_params=params(40960),
        name="sources",
    )(swept_2, low_2, high_2, u, v, g, z_table, y_table)
    layout = tuple([(0, None)] + [(1, p) for p in range(length)] + [(2, None)])
    carried = [later_interval(value) for value in (low_2, swept_2, high_2)]
    own = tuple((3 + number, index) for number, index in layout)
    return (
        sources,
        ((low_1, swept_1, high_1), (layout,)),
        ((low_2, swept_2, high_2), (layout,)),
        tuple(carried),
        ((low, fields, high), (own, layout)),
    )


def sweep_split(fields, is_first, z_table, y_table, blocks):
    length, size_y, size_z = fields.shape[1:]
    planes = length // 2
    plane, g_group, group = (size_y, size_z), round_up(3 * planes, 8), round_up(6 * planes, 8)

    def held(count, slots):
        return pltpu.VMEM((count, slots, size_y + 2 * pad, size_z), f32)

    def sems(*shape):
        return pltpu.SemaphoreType.DMA(shape)

    low, high = pl.pallas_call(
        edges_kernel,
        out_shape=(struct((9, *plane)),) * 2,
        in_specs=[hbm],
        out_specs=(vmem,) * 2,
        scratch_shapes=[sems(2)],
        compiler_params=params_but(300),
        name="edges",
    )(fields)
    low, high = neighbours(low, high)
    near, swept_1, swept_2, side_2, w_next, uv_end, uv_next, f, g = pl.pallas_call(
        functools.partial(interior_kernel, group, g_group),
        out_shape=(
            struct((9, 4, *plane)),
            struct((3, length - 2, *plane)),
            struct((3, length - 8, *plane)),
            struct((3, 4, *plane)),
            struct((3, 2, *plane)),
            struct((6, 2, *plane)),
            struct((6, 2, *plane)),
            struct((blocks * group, lanes)),
            struct((blocks * g_group, lanes)),
        ),
        in_specs=[scalar, hbm, vmem, vmem],
        out_specs=(hbm,) * 7 + (vmem,) * 2,
        scratch_shapes=[
            held(9, length),
            held(3, length),
            held(3, length),
            pltpu.VMEM((3, length, *plane), f32),
            pltpu.VMEM((6, planes, *plane), f32),
            sems(length),
            sems(3, max(length, 10)),
        ],
        compiler_params=params(40960),
        cost_estimate=pl.CostEstimate(flops=4 * 10**9, bytes_accessed=6 * 10**7, transcendentals=0),
        name="interior",
    )(is_first, fields, z_table, y_table)
    g_moved = later_interval(g)
    low_end_1, high_end_1, w_end, uv_end = pl.pallas_call(
        end_one_kernel,
        out_shape=(
            struct((3, *plane)),
            struct((3, *plane)),
            struct((3, 2, *plane)),
            struct((6, 2, *plane)),
        ),
        in_specs=[scalar, anywhere, anywhere, anywhere, vmem],
        out_specs=(vmem,) * 4,
        scratch_shapes=[held(9, 6), sems(6)],
        compiler_params=params(16384),
        name="end_one",
    )(is_first, near, low, high, uv_end)
    low_1, high_1 = neighbours(low_end_1, high_end_1)
    end_group = 8
    low_end_2, high_end_2, next_2, uv_end, g_end = pl.pallas_call(
        functools.partial(end_two_kernel, end_group),
        out_shape=(
            struct((3, *plane)),
            struct((3, *plane)),
            struct((3, 2, *plane)),
            struct((6, 2, *plane)),
            struct((blocks * end_group, lanes)),
        ),
        in_specs=[hbm] + [anywhere] * 4 + [vmem] * 5,
        out_specs=(vmem,) * 5,
        scratch_shapes=[held(3, 8), held(3, 4), sems(8)],
        compiler_params=params(16384),
        name="end_two",
    )(swept_1, low_1, low_end_1, high_end_1, high_1, w_end, w_next, uv_end, z_table, y_table)
    low_2, high_2 = neighbours(low_end_2, high_end_2)
    uv_end, f = pl.pallas_call(
        functools.partial(middle_kernel, group),
        out_shape=(struct((6, 2, *plane)), struct((blocks * group, lanes))),
        in_specs=[hbm, hbm] + [anywhere] * 3 + [vmem] * 5,
        out_specs=(vmem,) * 2,
        scratch_shapes=[held(3, 10), pltpu.VMEM((6, 2, *plane), f32), sems(10)],
        compiler_params=params(16384),
        name="middle",
    )(swept_2, side_2, low_end_2, next_2, high_end_2, uv_end, uv_next, f, z_table, y_table)
    pack, sources = pl.pallas_call(
        functools.partial(end_three_kernel, group, g_group, end_group),
        out_shape=(struct((3, 10, *plane)), struct((blocks * group, lanes))),
        in_specs=[hbm] + [anywhere] * 5 + [vmem] * 6,
        out_specs=(hbm, hbm),
        scratch_shapes=[
            pltpu.VMEM((blocks * group, lanes), f32),
            held(3, 6),
            pltpu.VMEM((3, 4, *plane), f32),
            pltpu.VMEM((6, 2, *plane), f32),
            sems(7),
            sems(8),
        ],
        compiler_params=params(16384),
        name="end_three",
    )(
        side_2, low_2, low_end_2, next_2, high_end_2, high_2, uv_end, f,
        g_moved, later_interval(g_end), z_table, y_table
    )
    inner_1 = [(2, p) for p in range(length - 2)]
    inner_2 = [(1, p) for p in range(length - 8)]
    layout_1 = [(0, None), (1, None)] + inner_1 + [(3, None), (4, None)]
    layout_2 = [(0, p) for p in range(5)] + inner_2 + [(0, p) for p in range(5, 10)]
    layout_0 = [(2, None)] + [(3, p) for p in range(length)] + [(4, None)]
    return (
        sources,
        ((low_1, low_end_1, swept_1, high_end_1, high_1), (tuple(layout_1),)),
        ((pack, swept_2), (tuple(layout_2),)),
        (later_interval(pack), later_interval(swept_2)),
        ((low, fields, high), (tuple(layout_0), tuple(layout_2))),
    )


def per_device(velocity):
    length, size_y, size_z = velocity.shape[3:]
    planes = length // 2
    peers, intervals = lax.axis_size("space"), lax.axis_size("tm")
    devices = peers * intervals
    coarse_x, coarse_y, coarse_z = peers * planes, size_y // 2, size_z // 2
    blocks = coarse_y * coarse_z // lanes
    per_block = devices // blocks
    columns = lanes // per_block
    device = lax.axis_index("space") * intervals + lax.axis_index("tm")
    tm_first = lax.axis_index("tm") == 0
    fields = velocity.reshape(9, length, size_y, size_z)

    x_basis, y_basis, z_basis = basis(coarse_x), basis(coarse_y), basis(coarse_z)
    z_forward = 0.25 * pair_matrix(coarse_z) @ z_basis.T
    z_table = right_table(np.kron(np.eye(2), z_forward))
    y_table = left_table(0.5 * y_basis)
    order = np.arange(coarse_x).reshape(peers, planes).T.reshape(-1)
    x_forward = left_table(x_basis[:, order])
    wanted_x = np.arange(peers)[None, :] * planes + np.arange(-1, planes + 1)[:, None]
    x_backward = left_table(x_basis.T[wanted_x.reshape(-1) % coarse_x])
    z_back = (refine_matrix(coarse_z) @ z_basis.T).T
    z_back_table = right_table(np.kron(np.eye(2), z_back))
    y_back_table = left_table(refine_matrix(coarse_y) @ y_basis.T)
    y_of = np.arange(2)[:, None] * blocks + np.arange(blocks)[None, :]
    waves = wave_squares(coarse_y)[y_of.T][:, :, None] + wave_squares(coarse_z)[None, None, :]
    waves = waves.reshape(devices, columns)
    waves = np.pad(waves, ((0, 0), (0, lanes - columns)))
    mine = lax.dynamic_slice_in_dim(jnp.asarray(waves, f32), device, 1, axis=0)
    total = jnp.asarray(wave_squares(coarse_x), f32)[:, None] + mine
    rates = 1.0 / (1.0 + half_step * coarse_viscosity * (4.0 / (2.0 * 2.0)) * total)

    is_first = tm_first.astype(f32).reshape(1)
    sweep = sweep_split if length >= 12 else sweep_whole
    moved_at = 1
    sources, one, two, carried, zero = sweep(fields, is_first, z_table, y_table, blocks)
    group = round_up(6 * planes, 8)

    both = ("space", "tm")

    def to_columns(value, rows):
        if per_block > 1:
            value = value.reshape(blocks, rows, per_block, columns).swapaxes(1, 2)
        value = value.reshape(devices, rows, columns)
        value = lax.all_to_all(value, both, split_axis=0, concat_axis=0, tiled=True)
        value = jnp.pad(value, ((0, 0), (0, 0), (0, lanes - columns)))
        return value.reshape(devices * rows, lanes)

    def to_planes(value, rows):
        value = value.reshape(devices, rows, lanes)[:, :, :columns]
        value = lax.all_to_all(value, both, split_axis=0, concat_axis=0, tiled=True)
        if per_block > 1:
            value = value.reshape(blocks, per_block, rows, columns).swapaxes(1, 2)
        return value.reshape(blocks, rows, lanes)

    back = round_up(3 * (planes + 2), 8)
    x_table = np.concatenate([x_forward, x_backward], axis=0)
    y_back_table = np.pad(y_back_table, ((0, 0), (0, z_back_table.shape[1] - y_back_table.shape[1])))
    table = np.concatenate([z_back_table, y_back_table], axis=0)
    columned = to_columns(sources, group)
    moved = carried[moved_at]
    columned, moved = lax.optimization_barrier((columned, moved))
    carried = (*carried[:moved_at], moved, *carried[moved_at + 1 :])
    solved_1, solved_2 = pl.pallas_call(
        functools.partial(solve_kernel, peers, intervals, planes, group, back),
        out_shape=(struct((devices * back, lanes)),) * 2,
        in_specs=[vmem, hbm, hbm],
        out_specs=(hbm, hbm),
        scratch_shapes=[
            pltpu.VMEM(rates.shape, f32),
            pltpu.VMEM(x_table.shape, bf16),
            pltpu.VMEM((devices * back, lanes), f32),
            pltpu.VMEM((devices * back, lanes), f32),
            pltpu.SemaphoreType.DMA((2,)),
            pltpu.SemaphoreType.DMA((2, devices)),
        ],
        compiler_params=params_but(790),
        name="solve",
    )(columned, rates, x_table)
    spectra_2 = to_planes(solved_2, back)
    solved_1, *carried = lax.optimization_barrier((solved_1, *carried))
    zero = ((*carried, *zero[0]), zero[1])
    spectra_1 = to_planes(solved_1, back)
    outs = corrected(2, spectra_2, table, two, None, is_first)
    outs = corrected(0, later_interval(spectra_2), table, zero, outs, is_first)
    new_velocity, new_rhs = corrected(1, spectra_1, table, one, outs, is_first)
    return (new_velocity[None], new_rhs[None])


def solution(mesh):
    placed = P("tm", None, None, "space", None, None)
    return jax.shard_map(
        per_device,
        mesh=mesh,
        in_specs=(placed,),
        out_specs=(placed, placed),
        check_vma=False,
    )
```

```python
import functools

import jax
import jax.numpy as jnp
import ml_dtypes
import numpy as np
from jax import lax
from jax.experimental import pallas as pl
from jax.experimental.pallas import tpu as pltpu
from jax.sharding import PartitionSpec as P

viscosity = 1.0
coarse_viscosity = 10.0
time_step = 0.3
weights_first = (5.0 / 24.0, 1.0 / 3.0, -1.0 / 24.0)
weights_second = (-1.0 / 24.0, 1.0 / 3.0, 5.0 / 24.0)
half_step = 0.5 * time_step
first = tuple(time_step * w for w in weights_first)
second = tuple(time_step * w for w in weights_second)
lanes = 128
pad = 8
rows_at_once = 32


def params(kibibytes):
    return pltpu.CompilerParams(vmem_limit_bytes=kibibytes * 1024)


def params_but(kibibytes):
    return params(64 * 1024 - kibibytes)


f32 = jnp.float32
bf16 = jnp.bfloat16


def round_up(value, multiple):
    return -(-value // multiple) * multiple


def frequencies(length):
    index = np.arange(length)
    return np.where(index <= length // 2, index, index - length // 2)


def basis(length):
    index = np.arange(length)
    waves = frequencies(length)
    angles = 2.0 * np.pi * (waves[:, None] * index[None, :] % length) / length
    table = np.where(index[:, None] <= length // 2, np.cos(angles), np.sin(angles))
    edge = (waves == 0) | (2 * waves == length)
    return table * np.sqrt(np.where(edge, 1.0, 2.0) / length)[:, None]


def wave_squares(length):
    return np.sin(np.pi * frequencies(length) / length) ** 2


def refine_matrix(length):
    table = np.zeros((2 * length, length))
    for i in range(length):
        table[2 * i, i] += 1.0
        table[2 * i + 1, i] += 0.5
        table[2 * i + 1, (i + 1) % length] += 0.5
    return table


def pair_matrix(length):
    return np.repeat(np.eye(length), 2, axis=0)


def split(table):
    high = table.astype(np.float32).astype(ml_dtypes.bfloat16)
    low = (table - high.astype(np.float64)).astype(np.float32).astype(ml_dtypes.bfloat16)
    return high, low


def left_table(table):
    high, low = split(table)
    return np.concatenate([high, low, high], axis=1)


def right_table(table):
    high, low = split(table)
    return np.concatenate([high, low, high], axis=0)


def split_value(value):
    high = value.astype(bf16)
    return high, (value - high.astype(f32)).astype(bf16)


def left_dot(table, value):
    high, low = split_value(value)
    return jnp.dot(table, jnp.concatenate([high, high, low], axis=0), preferred_element_type=f32)


def right_dot(value, table):
    high, low = split_value(value)
    return jnp.dot(
        jnp.concatenate([high, high, low], axis=1), table, preferred_element_type=f32
    )


def start_all(copies):
    for copy in copies:
        copy.start()
    for copy in copies:
        copy.wait()


def wrap_rows(ref, plane, count):
    size = ref.shape[2] - 2 * pad
    for field in range(count):
        ref[field, plane, pad - 1 : pad, :] = ref[field, plane, pad + size - 1 : pad + size, :]
        ref[field, plane, pad + size : pad + size + 1, :] = ref[field, plane, pad : pad + 1, :]


def rhs_rows(ref, base, plane, start):
    stop = start + rows_at_once
    center = [ref[base + c, plane, start:stop, :] for c in range(3)]
    size = ref.shape[3]
    results = []
    for c in range(3):
        x_up = ref[base + c, plane + 1, start:stop, :]
        x_down = ref[base + c, plane - 1, start:stop, :]
        y_up = ref[base + c, plane, start + 1 : stop + 1, :]
        y_down = ref[base + c, plane, start - 1 : stop - 1, :]
        z_up = pltpu.roll(center[c], size - 1, 1)
        z_down = pltpu.roll(center[c], 1, 1)
        advect = (
            center[0] * (x_up - x_down) + center[1] * (y_up - y_down) + center[2] * (z_up - z_down)
        )
        laplace = (x_up + x_down) + (y_up + y_down) + (z_up + z_down) - 6.0 * center[c]
        results.append(viscosity * laplace - 0.5 * advect)
    return center, results


def planes_in(source, low, high, held, sems):
    length = source.shape[1]
    size = source.shape[2]
    rows = pl.ds(pad, size)

    def inner(plane):
        return pltpu.make_async_copy(
            source.at[:, plane], held.at[:, plane + 1, rows, :], sems.at[plane]
        )

    below = pltpu.make_async_copy(low, held.at[:, 0, rows, :], sems.at[length])
    above = pltpu.make_async_copy(high, held.at[:, length + 1, rows, :], sems.at[length + 1])
    return inner, below, above


def arrive(step, source, low, high, held, sems):
    length = source.shape[1]
    count = source.shape[0]
    inner, below, above = planes_in(source, low, high, held, sems)

    @pl.when(step == 0)
    def _():
        below.start()

        def launch(plane, carry):
            inner(plane).start()
            return carry

        lax.fori_loop(0, length, launch, 0)
        above.start()
        below.wait()
        inner(0).wait()
        wrap_rows(held, 1, count)

    inner(2 * step + 1).wait()
    wrap_rows(held, 2 * step + 2, count)

    @pl.when(2 * step + 2 < length)
    def _():
        inner(2 * step + 2).wait()
        wrap_rows(held, 2 * step + 3, count)

    @pl.when(2 * step + 2 >= length)
    def _():
        above.wait()


def chunks(size):
    return range(0, size, rows_at_once)


def transform(summed, z_table, y_table):
    count, half = len(summed), summed[0].shape[0]
    couples = []
    for k in range(0, count, 2):
        couples.append(jnp.concatenate([summed[k], summed[min(k + 1, count - 1)]], axis=1))
    in_z = right_dot(jnp.concatenate(couples, axis=0), z_table[...])
    in_z = [in_z[k * half : (k + 1) * half] for k in range(len(couples))]
    in_y = left_dot(y_table[...], jnp.concatenate(in_z, axis=1))
    blocks = half // 2
    lane = lax.broadcasted_iota(jnp.int32, (blocks, lanes), 1)
    results = []
    for k in range(count):
        both = in_y[:, (k // 2) * lanes : (k // 2 + 1) * lanes]
        upper, lower = both[:blocks], both[blocks:]
        if k % 2 == 0:
            results.append(jnp.where(lane < lanes // 2, upper, pltpu.roll(lower, lanes // 2, 1)))
        else:
            results.append(jnp.where(lane < lanes // 2, pltpu.roll(upper, lanes // 2, 1), lower))
    return results


def spectral(pairs, z_table, y_table, count):
    half = pairs.shape[1] // 2
    summed = [
        pairs[k, pl.ds(0, half, 2), :] + pairs[k, pl.ds(1, half, 2), :] for k in range(count)
    ]
    return transform(summed, z_table, y_table)


def sweep_one_kernel(is_first, source, low, high, s1, w, u, v, held, sems):
    step = pl.program_id(0)
    size = source.shape[2]
    arrive(step, source, low, high, held, sems)
    for row in chunks(size):
        rows = slice(row, row + rows_at_once)
        for part in range(2):
            plane = 2 * step + part + 1
            total_first, total_second, start, initial = None, None, None, None
            for node in range(3):
                center, old = rhs_rows(held, 3 * node, plane, pad + row)
                a, b = first[node], second[node] - (half_step if node == 1 else 0.0)
                if node == 0:
                    start, initial = center, old
                    total_first = [start[c] + a * old[c] for c in range(3)]
                    total_second = [b * old[c] for c in range(3)]
                else:
                    total_first = [total_first[c] + a * old[c] for c in range(3)]
                    total_second = [total_second[c] + b * old[c] for c in range(3)]
                if node == 0:
                    for c in range(3):
                        mine = first[0] * old[c] + is_first[0] * start[c]
                        other = second[0] * old[c]
                        if part == 1:
                            mine = mine + u[c, 0, rows, :]
                            other = other + v[c, 0, rows, :]
                        u[c, 0, rows, :] = mine
                        v[c, 0, rows, :] = other
            for c in range(3):
                s1[c, part, rows, :] = total_first[c]
                w[c, part, rows, :] = total_first[c] + total_second[c]
                u[c, 0, rows, :] = u[c, 0, rows, :] - total_first[c]
                v[c, 0, rows, :] = v[c, 0, rows, :] + total_first[c]


def sweep_two_kernel(
    group, source, low, high, w, u, v, z_table, y_table, s2, u_out, v_out, g, held, pairs, sems
):
    step = pl.program_id(0)
    size = source.shape[2]
    arrive(step, source, low, high, held, sems)
    for row in chunks(size):
        rows = slice(row, row + rows_at_once)
        fresh_sum, sweep_sum = None, None
        for part in range(2):
            _, fresh = rhs_rows(held, 0, 2 * step + part + 1, pad + row)
            swept = [w[c, part, rows, :] + half_step * fresh[c] for c in range(3)]
            for c in range(3):
                s2[c, part, rows, :] = swept[c]
            if part == 0:
                fresh_sum, sweep_sum = fresh, swept
            else:
                fresh_sum = [fresh_sum[c] + fresh[c] for c in range(3)]
                sweep_sum = [sweep_sum[c] + swept[c] for c in range(3)]
        for c in range(3):
            u_out[c, 0, rows, :] = u[c, 0, rows, :] + first[1] * fresh_sum[c]
            v_out[c, 0, rows, :] = v[c, 0, rows, :] + second[1] * fresh_sum[c] - sweep_sum[c]
            pairs[c, rows, :] = sweep_sum[c]
    planes = source.shape[1] // 2
    blocks = g.shape[0] // group
    for c, value in enumerate(spectral(pairs, z_table, y_table, 3)):
        g[pl.ds(c * planes + step, blocks, group), :] = value


def source_kernel(
    group, g_group, source, low, high, u, v, g, z_table, y_table, out, held, pairs, sems
):
    step = pl.program_id(0)
    size = source.shape[2]
    arrive(step, source, low, high, held, sems)
    for row in chunks(size):
        rows = slice(row, row + rows_at_once)
        _, fresh = rhs_rows(held, 0, 2 * step + 1, pad + row)
        _, other = rhs_rows(held, 0, 2 * step + 2, pad + row)
        for c in range(3):
            total = fresh[c] + other[c]
            pairs[c, rows, :] = u[c, 0, rows, :] + first[2] * total
            pairs[3 + c, rows, :] = v[c, 0, rows, :] + second[2] * total
    planes = source.shape[1] // 2
    blocks = out.shape[0] // group
    for k, value in enumerate(spectral(pairs, z_table, y_table, 6)):
        if k < 3:
            value = value + g[pl.ds(k * planes + step, blocks, g_group), :]
        out[pl.ds(k * planes + step, blocks, group), :] = value


def solve_kernel(
    peers, intervals, planes, group, back, values, inverse, table,
    sent_1, sent_2, out_1, out_2, out_sems
):
    sending = []
    rows_x = peers * planes
    start = [None] * 3
    for interval in range(intervals):
        loaded = []
        for field in range(6):
            parts = [
                values[
                    pl.ds(interval * group + field * planes + p, peers, intervals * group), :
                ]
                for p in range(planes)
            ]
            loaded.append(jnp.concatenate(parts, axis=0))
        spectra = left_dot(table[:rows_x, :], jnp.concatenate(loaded, axis=1))
        rates = inverse[...]
        wanted = []
        for field in range(6):
            c = field % 3
            value = spectra[:, field * lanes : (field + 1) * lanes]
            if start[c] is not None:
                value = value + start[c]
            start[c] = value * rates
            wanted.append(start[c])
        physical = left_dot(table[rows_x:, :], jnp.concatenate(wanted, axis=1))
        for field in range(6):
            out = (out_1, out_2)[field // 3]
            base = (field % 3) * (planes + 2)
            for e in range(planes + 2):
                out[pl.ds(interval * back + base + e, peers, intervals * back), :] = physical[
                    e * peers : (e + 1) * peers, field * lanes : (field + 1) * lanes
                ]
        for peer in range(peers):
            rows = pl.ds((peer * intervals + interval) * back, back)
            for k, (out, sent) in enumerate(((out_1, sent_1), (out_2, sent_2))):
                sem = out_sems.at[k, peer * intervals + interval]
                sending.append(pltpu.make_async_copy(out.at[rows], sent.at[rows], sem))
                sending[-1].start()
    for copy in sending:
        copy.wait()


def edges_kernel(source, low, high, sems):
    length = source.shape[1]
    start_all([
        pltpu.make_async_copy(source.at[:, 0], low, sems.at[0]),
        pltpu.make_async_copy(source.at[:, length - 1], high, sems.at[1]),
    ])


def sweep_one_plane(is_first, held, slot, put_s1, put_w, uv, cell):
    size = held.shape[2] - 2 * pad
    for row in chunks(size):
        rows = slice(row, row + rows_at_once)
        total_first, total_second = [], []
        for node in range(3):
            start, old = rhs_rows(held, 3 * node, slot, pad + row)
            a, b = first[node], second[node] - (half_step if node == 1 else 0.0)
            if node == 0:
                for c in range(3):
                    uv[c, cell, rows, :] += first[0] * old[c] + is_first[0] * start[c]
                    uv[3 + c, cell, rows, :] += second[0] * old[c]
                total_first = [start[c] + a * old[c] for c in range(3)]
                total_second = [b * old[c] for c in range(3)]
            else:
                total_first = [total_first[c] + a * old[c] for c in range(3)]
                total_second = [total_second[c] + b * old[c] for c in range(3)]
        for c in range(3):
            put_s1(c, row, total_first[c])
            put_w(c, row, total_first[c] + total_second[c])
            uv[c, cell, rows, :] -= total_first[c]
            uv[3 + c, cell, rows, :] += total_first[c]


def sweep_two_plane(held, slot, get_w, put_s2, uv, cell):
    size = held.shape[2] - 2 * pad
    for row in chunks(size):
        rows = slice(row, row + rows_at_once)
        _, fresh = rhs_rows(held, 0, slot, pad + row)
        for c in range(3):
            swept = get_w(c, row) + half_step * fresh[c]
            put_s2(c, row, swept)
            uv[c, cell, rows, :] += first[1] * fresh[c]
            uv[3 + c, cell, rows, :] += second[1] * fresh[c] - swept


def last_rhs_pair(held, slot, uv, cell):
    size = held.shape[2] - 2 * pad
    for row in chunks(size):
        rows = slice(row, row + rows_at_once)
        _, fresh = rhs_rows(held, 0, slot, pad + row)
        _, other = rhs_rows(held, 0, slot + 1, pad + row)
        for c in range(3):
            total = fresh[c] + other[c]
            uv[c, cell, rows, :] += first[2] * total
            uv[3 + c, cell, rows, :] += second[2] * total


def last_rhs_one(held, slot, uv, cell):
    size = held.shape[2] - 2 * pad
    for row in chunks(size):
        rows = slice(row, row + rows_at_once)
        _, fresh = rhs_rows(held, 0, slot, pad + row)
        for c in range(3):
            uv[c, cell, rows, :] += first[2] * fresh[c]
            uv[3 + c, cell, rows, :] += second[2] * fresh[c]


def uv_halves(uv, k, cell):
    half = uv.shape[2] // 2
    return uv[k, cell, pl.ds(0, half, 2), :] + uv[k, cell, pl.ds(1, half, 2), :]


def held_halves(held, c, slot):
    half = (held.shape[2] - 2 * pad) // 2
    total = held[c, slot, pl.ds(pad, half, 2), :] + held[c, slot, pl.ds(pad + 1, half, 2), :]
    total = total + held[c, slot + 1, pl.ds(pad, half, 2), :]
    return total + held[c, slot + 1, pl.ds(pad + 1, half, 2), :]


def interior_kernel(
    group, g_group, is_first, source, z_table, y_table,
    near, s1_out, s2_out, s2_side, w_out, uv_end, uv_next, out, g,
    held, held_1, held_2, w, uv, sems, out_sems
):
    length, size = source.shape[1], source.shape[2]
    planes = length // 2
    blocks = out.shape[0] // group
    rows_all = pl.ds(pad, size)

    def arriving(plane):
        return pltpu.make_async_copy(
            source.at[:, plane], held.at[:, plane, rows_all, :], sems.at[plane]
        )

    def launch(plane, carry):
        arriving(plane).start()
        return carry

    lax.fori_loop(0, length, launch, 0)
    uv[...] = jnp.zeros(uv.shape, f32)
    arriving(0).wait()
    arriving(1).wait()
    wrap_rows(held, 1, 9)

    def s1_copy(plane):
        return pltpu.make_async_copy(
            held_1.at[:, plane, rows_all, :], s1_out.at[:, plane - 1], out_sems.at[0, plane]
        )

    sides = (2, 3, length - 4, length - 3)

    def s2_copy(plane):
        inner = plane not in sides
        target = s2_out.at[:, plane - 4] if inner else s2_side.at[:, sides.index(plane)]
        return pltpu.make_async_copy(
            held_2.at[:, plane, rows_all, :], target, out_sems.at[1, plane]
        )

    def phase_one(plane, carry):
        arriving(plane + 1).wait()
        wrap_rows(held, plane + 1, 9)

        def put_s1(c, row, value):
            held_1[c, plane, pad + row : pad + row + rows_at_once, :] = value

        def put_w(c, row, value):
            w[c, plane, row : row + rows_at_once, :] = value

        sweep_one_plane(is_first, held, plane, put_s1, put_w, uv, plane // 2)
        wrap_rows(held_1, plane, 3)
        s1_copy(plane).start()
        return carry

    lax.fori_loop(1, length - 1, phase_one, 0)

    def phase_two(plane, carry):
        def get_w(c, row):
            return w[c, plane, row : row + rows_at_once, :]

        def put_s2(c, row, value):
            held_2[c, plane, pad + row : pad + row + rows_at_once, :] = value

        sweep_two_plane(held_1, plane, get_w, put_s2, uv, plane // 2)
        wrap_rows(held_2, plane, 3)
        return carry

    lax.fori_loop(2, length - 2, phase_two, 0)
    for plane in range(2, length - 2):
        s2_copy(plane).start()
    tails = []
    for k, plane in enumerate((0, 1, length - 2, length - 1)):
        tails.append(
            pltpu.make_async_copy(held.at[:, plane, rows_all, :], near.at[:, k], out_sems.at[2, 6 + k])
        )
    for k, plane in enumerate((1, length - 2)):
        tails.append(pltpu.make_async_copy(w.at[:, plane], w_out.at[:, k], out_sems.at[2, k]))
    for k, cell in enumerate((0, planes - 1)):
        tails.append(pltpu.make_async_copy(uv.at[:, cell], uv_end.at[:, k], out_sems.at[2, 2 + k]))
    for k, cell in enumerate((1, planes - 2)):
        tails.append(pltpu.make_async_copy(uv.at[:, cell], uv_next.at[:, k], out_sems.at[2, 4 + k]))
    for copy in tails:
        copy.start()

    def phase_three(cell, carry):
        last_rhs_pair(held_2, 2 * cell, uv, cell)
        return carry

    lax.fori_loop(2, planes - 2, phase_three, 0)
    for start in range(2, planes - 2, 2):
        cells = range(start, min(start + 2, planes - 2))
        entries = [(k, cell) for cell in cells for k in range(6)]
        values = transform([uv_halves(uv, k, cell) for k, cell in entries], z_table, y_table)
        for (k, cell), value in zip(entries, values):
            out[pl.ds(k * planes + cell, blocks, group), :] = value
    for start in range(1, planes - 1, 4):
        cells = range(start, min(start + 4, planes - 1))
        entries = [(c, cell) for cell in cells for c in range(3)]
        values = transform([held_halves(held_2, c, 2 * cell) for c, cell in entries], z_table, y_table)
        for (c, cell), value in zip(entries, values):
            g[pl.ds(c * planes + cell, blocks, g_group), :] = value

    def finish_one(plane, carry):
        s1_copy(plane).wait()
        return carry

    lax.fori_loop(1, length - 1, finish_one, 0)
    for plane in range(2, length - 2):
        s2_copy(plane).wait()
    for copy in tails:
        copy.wait()


def end_one_kernel(
    is_first, near, low, high, uv_in, low_out, high_out, w_out, uv, held, sems
):
    size = near.shape[2]
    rows_all = pl.ds(pad, size)
    sources = [low, *[near.at[:, k] for k in range(4)], high]
    start_all([
        pltpu.make_async_copy(ref, held.at[:, slot, rows_all, :], sems.at[slot])
        for slot, ref in enumerate(sources)
    ])
    uv[...] = uv_in[...]
    for k, (slot, ref) in enumerate(((1, low_out), (4, high_out))):
        wrap_rows(held, slot, 9)

        def put_s1(c, row, value):
            ref[c, row : row + rows_at_once, :] = value

        def put_w(c, row, value):
            w_out[c, k, row : row + rows_at_once, :] = value

        sweep_one_plane(is_first, held, slot, put_s1, put_w, uv, k)


def end_two_kernel(
    g_group, swept, low, low_end, high_end, high, w_end, w_next, uv_in, z_table, y_table,
    low_out, high_out, next_out, uv, g, held, held_2, sems
):
    count, size = swept.shape[1], swept.shape[2]
    rows_all = pl.ds(pad, size)
    sources = [low, low_end, swept.at[:, 0], swept.at[:, 1]]
    sources += [swept.at[:, count - 2], swept.at[:, count - 1], high_end, high]
    start_all([
        pltpu.make_async_copy(ref, held.at[:, slot, rows_all, :], sems.at[slot])
        for slot, ref in enumerate(sources)
    ])
    uv[...] = uv_in[...]
    places = ((1, 0, w_end, 0), (2, 0, w_next, 0), (5, 1, w_next, 1), (6, 1, w_end, 1))
    for index, (slot, cell, w, k) in enumerate(places):
        wrap_rows(held, slot, 3)

        def get_w(c, row):
            return w[c, k, row : row + rows_at_once, :]

        def put_s2(c, row, value):
            rows = slice(row, row + rows_at_once)
            if slot == 1:
                low_out[c, rows, :] = value
            elif slot == 6:
                high_out[c, rows, :] = value
            else:
                next_out[c, k, rows, :] = value
            held_2[c, index, pad + row : pad + row + rows_at_once, :] = value

        sweep_two_plane(held, slot, get_w, put_s2, uv, cell)
    blocks = g.shape[0] // g_group
    entries = [(c, k) for k in range(2) for c in range(3)]
    values = transform([held_halves(held_2, c, 2 * k) for c, k in entries], z_table, y_table)
    for (c, k), value in zip(entries, values):
        g[pl.ds(2 * c + k, blocks, g_group), :] = value


def middle_kernel(
    group, swept, side, low_end, nexts, high_end, uv_in, uv_next, f, z_table, y_table,
    uv, out, held, near, sems
):
    count, size = swept.shape[1], swept.shape[2]
    planes = (count + 8) // 2
    rows_all = pl.ds(pad, size)
    sources = [low_end, nexts.at[:, 0], side.at[:, 0], side.at[:, 1], swept.at[:, 0]]
    sources += [swept.at[:, count - 1], side.at[:, 2], side.at[:, 3], nexts.at[:, 1], high_end]
    start_all([
        pltpu.make_async_copy(ref, held.at[:, slot, rows_all, :], sems.at[slot])
        for slot, ref in enumerate(sources)
    ])
    uv[...] = uv_in[...]
    near[...] = uv_next[...]
    out[...] = f[...]
    for slot in (1, 2, 3, 6, 7, 8):
        wrap_rows(held, slot, 3)
    last_rhs_one(held, 1, uv, 0)
    last_rhs_one(held, 8, uv, 1)
    last_rhs_pair(held, 2, near, 0)
    last_rhs_pair(held, 6, near, 1)
    blocks = out.shape[0] // group
    entries = [(k, index) for index in range(2) for k in range(6)]
    values = transform([uv_halves(near, k, index) for k, index in entries], z_table, y_table)
    for (k, index), value in zip(entries, values):
        out[pl.ds(k * planes + (1, planes - 2)[index], blocks, group), :] = value


def end_three_kernel(
    group, g_group, end_group, side, low, low_end, nexts, high_end, high, uv_in, f, g, g_end,
    z_table, y_table, pack, sent, out, held, side_held, uv, sems, out_sems
):
    size = held.shape[2] - 2 * pad
    rows_all = pl.ds(pad, size)
    blocks = out.shape[0] // group
    planes = g.shape[0] // blocks // 3
    sources = [low, low_end, nexts.at[:, 0], nexts.at[:, 1], high_end, high]
    side_in = pltpu.make_async_copy(side, side_held, sems.at[6])
    side_in.start()
    start_all([
        pltpu.make_async_copy(ref, held.at[:, slot, rows_all, :], sems.at[slot])
        for slot, ref in enumerate(sources)
    ])
    packing = [
        pltpu.make_async_copy(
            held.at[:, slot, rows_all, :], pack.at[:, (0, 1, 2, 7, 8, 9)[slot]], out_sems.at[slot]
        )
        for slot in range(6)
    ]
    packing.append(pltpu.make_async_copy(side_held, pack.at[:, 3:7], out_sems.at[7]))
    uv[...] = uv_in[...]
    out[...] = f[...]
    for slot in (1, 4):
        wrap_rows(held, slot, 3)
    side_in.wait()
    for copy in packing:
        copy.start()
    last_rhs_one(held, 1, uv, 0)
    last_rhs_one(held, 4, uv, 1)
    entries = [(k, index) for index in range(2) for k in range(6)]
    values = transform([uv_halves(uv, k, index) for k, index in entries], z_table, y_table)
    for (k, index), value in zip(entries, values):
        if k < 3:
            value = value + g_end[pl.ds(2 * k + index, blocks, end_group), :]
        out[pl.ds(k * planes + index * (planes - 1), blocks, group), :] = value
    for k in range(3):
        for cell in range(1, planes - 1):
            out[pl.ds(k * planes + cell, blocks, group), :] += g[
                pl.ds(k * planes + cell, blocks, g_group), :
            ]
    start_all([pltpu.make_async_copy(out, sent, out_sems.at[6])])
    for copy in packing:
        copy.wait()


def place(fields, layouts, is_first, staged, sems):
    def launch(layout):
        for slot, (number, index) in enumerate(layout):
            ref = fields[number]
            ref = ref.at[0:3, index] if index is not None else ref.at[0:3]
            pltpu.make_async_copy(ref, staged.at[:, slot], sems.at[slot]).start()

    if len(layouts) > 1:
        pl.when(is_first[0] > 0)(functools.partial(launch, layouts[0]))
        pl.when(is_first[0] <= 0)(functools.partial(launch, layouts[1]))
    else:
        launch(layouts[0])


def corrected_kernel(node, group, layouts, count, is_first, spectra, table, *refs):
    new_velocity, new_rhs, held, staged, coarse, result, sems, out_sems, rhs_sems = refs[-9:]
    place(refs[:count], layouts, is_first, staged, sems)
    length, size = staged.shape[1] - 2, staged.shape[2]
    planes = length // 2
    rows_all = pl.ds(pad, size)
    z_rows = 3 * lanes
    y_rows, y_columns = size, 3 * size // 2
    blocks = spectra.shape[0] // group
    for c in range(3):
        base = c * (planes + 2)
        parts = [spectra[pl.ds(base + e, blocks, group), :] for e in range(planes + 2)]
        in_z = right_dot(jnp.concatenate(parts, axis=0), table[:z_rows, :])
        for e in range(0, planes + 2, 2):
            stacked = []
            for k in (e, min(e + 1, planes + 1)):
                mine = in_z[k * blocks : (k + 1) * blocks]
                stacked.append(jnp.concatenate([mine[:, :size], mine[:, size:]], axis=0))
            both = left_dot(
                table[z_rows : z_rows + y_rows, :y_columns], jnp.concatenate(stacked, axis=1)
            )
            for k in range(min(2, planes + 2 - e)):
                coarse[c, e + k] = both[:, k * size : (k + 1) * size]

    def out_copy(plane):
        return pltpu.make_async_copy(
            held.at[:, plane + 1, rows_all, :], new_velocity.at[node, :, plane], out_sems.at[plane]
        )

    def rhs_copy(plane):
        return pltpu.make_async_copy(
            result.at[:, plane], new_rhs.at[node, :, plane], rhs_sems.at[plane]
        )

    def correct(plane, cell, odd):
        pltpu.make_async_copy(staged.at[:, plane], staged.at[:, plane], sems.at[plane]).wait()
        for field in range(3):
            for row in chunks(size):
                rows = slice(row, row + rows_at_once)
                held_rows = slice(pad + row, pad + row + rows_at_once)
                value = coarse[field, cell, rows, :]
                if odd:
                    value = 0.5 * (value + coarse[field, cell + 1, rows, :])
                held[field, plane, held_rows, :] = staged[field, plane, rows, :] + value
        wrap_rows(held, plane, 3)

    correct(0, 0, True)
    correct(1, 1, False)
    out_copy(0).start()

    def body(q, carry):
        correct(2 * q + 2, q + 1, True)
        correct(2 * q + 3, q + 2, False)
        out_copy(2 * q + 1).start()

        @pl.when(2 * q + 2 < length)
        def _():
            out_copy(2 * q + 2).start()

        for part in range(2):
            plane = 2 * q + part
            for row in chunks(size):
                _, fresh = rhs_rows(held, 0, plane + 1, pad + row)
                for c in range(3):
                    result[c, plane, row : row + rows_at_once, :] = fresh[c].astype(bf16)
            rhs_copy(plane).start()
        return carry

    lax.fori_loop(0, planes, body, 0)

    def finish(plane, carry):
        out_copy(plane).wait()
        rhs_copy(plane).wait()
        return carry

    lax.fori_loop(0, length, finish, 0)


anywhere = pl.BlockSpec(memory_space=pl.ANY)
scalar = pl.BlockSpec(memory_space=pltpu.SMEM)
vmem = pl.BlockSpec(memory_space=pltpu.VMEM)
hbm = pl.BlockSpec(memory_space=pltpu.HBM)


def whole(shape):
    return pl.BlockSpec(shape, lambda *index: (0,) * len(shape))


def struct(shape, dtype=f32):
    return jax.ShapeDtypeStruct(shape, dtype)


def slab(shape):
    return pl.BlockSpec(shape, lambda q: (0, q, 0, 0))


def held_planes(count, length, size_y, size_z):
    return pltpu.VMEM((count, length + 2, size_y + 2 * pad, size_z), f32)


def neighbours(low_plane, high_plane):
    count = lax.axis_size("space")
    up = [(i, (i + 1) % count) for i in range(count)]
    down = [(j, i) for i, j in up]
    return lax.ppermute(high_plane, "space", up), lax.ppermute(low_plane, "space", down)


def later_interval(value):
    count = lax.axis_size("tm")
    return lax.ppermute(value, "tm", [(i, i + 1) for i in range(count - 1)])


def corrected(node, spectra, table, placed, outs, is_first):
    fields, layouts = placed
    group, slots, (size_y, size_z) = spectra.shape[1], len(layouts[0]), fields[0].shape[-2:]
    length, planes = slots - 2, slots // 2 - 1
    operands = [is_first, spectra.reshape(-1, lanes), table, *fields]
    specs = [scalar, vmem, vmem] + [anywhere] * len(fields)
    shape = (3, 3, length, size_y, size_z)
    aliases = {}
    if outs is not None:
        aliases = {len(operands): 0, len(operands) + 1: 1}
        operands, specs = [*operands, *outs], specs + [hbm] * 2
    return pl.pallas_call(
        functools.partial(corrected_kernel, node, group, layouts, len(fields)),
        out_shape=(struct(shape), struct(shape, bf16)),
        in_specs=specs,
        out_specs=(hbm, hbm),
        input_output_aliases=aliases,
        scratch_shapes=[
            held_planes(3, length, size_y, size_z),
            pltpu.VMEM((3, slots, size_y, size_z), f32),
            pltpu.VMEM((3, planes + 2, size_y, size_z), f32),
            pltpu.VMEM((3, length, size_y, size_z), bf16),
            pltpu.SemaphoreType.DMA((slots,)),
            pltpu.SemaphoreType.DMA((length,)),
            pltpu.SemaphoreType.DMA((length,)),
        ],
        compiler_params=params_but(560),
        name=f"corrected_{node}",
    )(*operands)


def sweep_whole(fields, is_first, z_table, y_table, blocks):
    length, size_y, size_z = fields.shape[1:]
    planes = length // 2
    low, high = neighbours(fields[:, 0], fields[:, length - 1])
    fine = (3, length, size_y, size_z)
    halved = (3, planes, size_y, size_z)
    two = (3, 2, size_y, size_z)
    one = (3, 1, size_y, size_z)
    in_sems = pltpu.SemaphoreType.DMA((length + 2,))
    swept_1, w, u, v = pl.pallas_call(
        sweep_one_kernel,
        grid=(planes,),
        out_shape=(struct(fine), struct(fine), struct(halved), struct(halved)),
        in_specs=[scalar, anywhere, anywhere, anywhere],
        out_specs=(slab(two), slab(two), slab(one), slab(one)),
        scratch_shapes=[held_planes(9, length, size_y, size_z), in_sems],
        compiler_params=params(40960),
        name="sweep_one",
    )(is_first, fields, low, high)
    low_1, high_1 = neighbours(swept_1[:, 0], swept_1[:, length - 1])

    g_group = round_up(3 * planes, 8)
    swept_2, u, v, g = pl.pallas_call(
        functools.partial(sweep_two_kernel, g_group),
        grid=(planes,),
        out_shape=(struct(fine), struct(halved), struct(halved), struct((blocks * g_group, lanes))),
        in_specs=[anywhere, anywhere, anywhere, slab(two), slab(one), slab(one)]
        + [whole(z_table.shape), whole(y_table.shape)],
        out_specs=(slab(two), slab(one), slab(one), whole((blocks * g_group, lanes))),
        scratch_shapes=[
            held_planes(3, length, size_y, size_z),
            pltpu.VMEM((3, size_y, size_z), f32),
            in_sems,
        ],
        compiler_params=params(40960),
        name="sweep_two",
    )(swept_1, low_1, high_1, w, u, v, z_table, y_table)
    low_2, high_2 = neighbours(swept_2[:, 0], swept_2[:, length - 1])
    g = later_interval(g)

    group = round_up(6 * planes, 8)
    sources = pl.pallas_call(
        functools.partial(source_kernel, group, g_group),
        grid=(planes,),
        out_shape=struct((blocks * group, lanes)),
        in_specs=[anywhere, anywhere, anywhere, slab(one), slab(one), whole(g.shape)]
        + [whole(z_table.shape), whole(y_table.shape)],
        out_specs=whole((blocks * group, lanes)),
        scratch_shapes=[
            held_planes(3, length, size_y, size_z),
            pltpu.VMEM((6, size_y, size_z), f32),
            in_sems,
        ],
        compiler_params=params(40960),
        name="sources",
    )(swept_2, low_2, high_2, u, v, g, z_table, y_table)
    layout = tuple([(0, None)] + [(1, p) for p in range(length)] + [(2, None)])
    carried = [later_interval(value) for value in (low_2, swept_2, high_2)]
    own = tuple((3 + number, index) for number, index in layout)
    return (
        sources,
        ((low_1, swept_1, high_1), (layout,)),
        ((low_2, swept_2, high_2), (layout,)),
        tuple(carried),
        ((low, fields, high), (own, layout)),
    )


def sweep_split(fields, is_first, z_table, y_table, blocks):
    length, size_y, size_z = fields.shape[1:]
    planes = length // 2
    plane, g_group, group = (size_y, size_z), round_up(3 * planes, 8), round_up(6 * planes, 8)

    def held(count, slots):
        return pltpu.VMEM((count, slots, size_y + 2 * pad, size_z), f32)

    def sems(*shape):
        return pltpu.SemaphoreType.DMA(shape)

    low, high = pl.pallas_call(
        edges_kernel,
        out_shape=(struct((9, *plane)),) * 2,
        in_specs=[hbm],
        out_specs=(vmem,) * 2,
        scratch_shapes=[sems(2)],
        compiler_params=params_but(300),
        name="edges",
    )(fields)
    low, high = neighbours(low, high)
    near, swept_1, swept_2, side_2, w_next, uv_end, uv_next, f, g = pl.pallas_call(
        functools.partial(interior_kernel, group, g_group),
        out_shape=(
            struct((9, 4, *plane)),
            struct((3, length - 2, *plane)),
            struct((3, length - 8, *plane)),
            struct((3, 4, *plane)),
            struct((3, 2, *plane)),
            struct((6, 2, *plane)),
            struct((6, 2, *plane)),
            struct((blocks * group, lanes)),
            struct((blocks * g_group, lanes)),
        ),
        in_specs=[scalar, hbm, vmem, vmem],
        out_specs=(hbm,) * 7 + (vmem,) * 2,
        scratch_shapes=[
            held(9, length),
            held(3, length),
            held(3, length),
            pltpu.VMEM((3, length, *plane), f32),
            pltpu.VMEM((6, planes, *plane), f32),
            sems(length),
            sems(3, max(length, 10)),
        ],
        compiler_params=params(40960),
        cost_estimate=pl.CostEstimate(flops=4 * 10**9, bytes_accessed=6 * 10**7, transcendentals=0),
        name="interior",
    )(is_first, fields, z_table, y_table)
    g_moved = later_interval(g)
    low_end_1, high_end_1, w_end, uv_end = pl.pallas_call(
        end_one_kernel,
        out_shape=(
            struct((3, *plane)),
            struct((3, *plane)),
            struct((3, 2, *plane)),
            struct((6, 2, *plane)),
        ),
        in_specs=[scalar, anywhere, anywhere, anywhere, vmem],
        out_specs=(vmem,) * 4,
        scratch_shapes=[held(9, 6), sems(6)],
        compiler_params=params(16384),
        name="end_one",
    )(is_first, near, low, high, uv_end)
    low_1, high_1 = neighbours(low_end_1, high_end_1)
    end_group = 8
    low_end_2, high_end_2, next_2, uv_end, g_end = pl.pallas_call(
        functools.partial(end_two_kernel, end_group),
        out_shape=(
            struct((3, *plane)),
            struct((3, *plane)),
            struct((3, 2, *plane)),
            struct((6, 2, *plane)),
            struct((blocks * end_group, lanes)),
        ),
        in_specs=[hbm] + [anywhere] * 4 + [vmem] * 5,
        out_specs=(vmem,) * 5,
        scratch_shapes=[held(3, 8), held(3, 4), sems(8)],
        compiler_params=params(16384),
        name="end_two",
    )(swept_1, low_1, low_end_1, high_end_1, high_1, w_end, w_next, uv_end, z_table, y_table)
    low_2, high_2 = neighbours(low_end_2, high_end_2)
    uv_end, f = pl.pallas_call(
        functools.partial(middle_kernel, group),
        out_shape=(struct((6, 2, *plane)), struct((blocks * group, lanes))),
        in_specs=[hbm, hbm] + [anywhere] * 3 + [vmem] * 5,
        out_specs=(vmem,) * 2,
        scratch_shapes=[held(3, 10), pltpu.VMEM((6, 2, *plane), f32), sems(10)],
        compiler_params=params(16384),
        name="middle",
    )(swept_2, side_2, low_end_2, next_2, high_end_2, uv_end, uv_next, f, z_table, y_table)
    pack, sources = pl.pallas_call(
        functools.partial(end_three_kernel, group, g_group, end_group),
        out_shape=(struct((3, 10, *plane)), struct((blocks * group, lanes))),
        in_specs=[hbm] + [anywhere] * 5 + [vmem] * 6,
        out_specs=(hbm, hbm),
        scratch_shapes=[
            pltpu.VMEM((blocks * group, lanes), f32),
            held(3, 6),
            pltpu.VMEM((3, 4, *plane), f32),
            pltpu.VMEM((6, 2, *plane), f32),
            sems(7),
            sems(8),
        ],
        compiler_params=params(16384),
        name="end_three",
    )(
        side_2, low_2, low_end_2, next_2, high_end_2, high_2, uv_end, f,
        g_moved, later_interval(g_end), z_table, y_table
    )
    inner_1 = [(2, p) for p in range(length - 2)]
    inner_2 = [(1, p) for p in range(length - 8)]
    layout_1 = [(0, None), (1, None)] + inner_1 + [(3, None), (4, None)]
    layout_2 = [(0, p) for p in range(5)] + inner_2 + [(0, p) for p in range(5, 10)]
    layout_0 = [(2, None)] + [(3, p) for p in range(length)] + [(4, None)]
    return (
        sources,
        ((low_1, low_end_1, swept_1, high_end_1, high_1), (tuple(layout_1),)),
        ((pack, swept_2), (tuple(layout_2),)),
        (later_interval(pack), later_interval(swept_2)),
        ((low, fields, high), (tuple(layout_0), tuple(layout_2))),
    )


def per_device(velocity):
    length, size_y, size_z = velocity.shape[3:]
    planes = length // 2
    peers, intervals = lax.axis_size("space"), lax.axis_size("tm")
    devices = peers * intervals
    coarse_x, coarse_y, coarse_z = peers * planes, size_y // 2, size_z // 2
    blocks = coarse_y * coarse_z // lanes
    per_block = devices // blocks
    columns = lanes // per_block
    device = lax.axis_index("space") * intervals + lax.axis_index("tm")
    tm_first = lax.axis_index("tm") == 0
    fields = velocity.reshape(9, length, size_y, size_z)

    x_basis, y_basis, z_basis = basis(coarse_x), basis(coarse_y), basis(coarse_z)
    z_forward = 0.25 * pair_matrix(coarse_z) @ z_basis.T
    z_table = right_table(np.kron(np.eye(2), z_forward))
    y_table = left_table(0.5 * y_basis)
    order = np.arange(coarse_x).reshape(peers, planes).T.reshape(-1)
    x_forward = left_table(x_basis[:, order])
    wanted_x = np.arange(peers)[None, :] * planes + np.arange(-1, planes + 1)[:, None]
    x_backward = left_table(x_basis.T[wanted_x.reshape(-1) % coarse_x])
    z_back = (refine_matrix(coarse_z) @ z_basis.T).T
    z_back_table = right_table(np.kron(np.eye(2), z_back))
    y_back_table = left_table(refine_matrix(coarse_y) @ y_basis.T)
    y_of = np.arange(2)[:, None] * blocks + np.arange(blocks)[None, :]
    waves = wave_squares(coarse_y)[y_of.T][:, :, None] + wave_squares(coarse_z)[None, None, :]
    waves = waves.reshape(devices, columns)
    waves = np.pad(waves, ((0, 0), (0, lanes - columns)))
    mine = lax.dynamic_slice_in_dim(jnp.asarray(waves, f32), device, 1, axis=0)
    total = jnp.asarray(wave_squares(coarse_x), f32)[:, None] + mine
    rates = 1.0 / (1.0 + half_step * coarse_viscosity * (4.0 / (2.0 * 2.0)) * total)

    is_first = tm_first.astype(f32).reshape(1)
    sweep = sweep_split if length >= 12 else sweep_whole
    moved_at = 1
    sources, one, two, carried, zero = sweep(fields, is_first, z_table, y_table, blocks)
    group = round_up(6 * planes, 8)

    both = ("space", "tm")

    def to_columns(value, rows):
        if per_block > 1:
            value = value.reshape(blocks, rows, per_block, columns).swapaxes(1, 2)
        value = value.reshape(devices, rows, columns)
        value = lax.all_to_all(value, both, split_axis=0, concat_axis=0, tiled=True)
        value = jnp.pad(value, ((0, 0), (0, 0), (0, lanes - columns)))
        return value.reshape(devices * rows, lanes)

    def to_planes(value, rows):
        value = value.reshape(devices, rows, lanes)[:, :, :columns]
        value = lax.all_to_all(value, both, split_axis=0, concat_axis=0, tiled=True)
        if per_block > 1:
            value = value.reshape(blocks, per_block, rows, columns).swapaxes(1, 2)
        return value.reshape(blocks, rows, lanes)

    back = round_up(3 * (planes + 2), 8)
    x_table = np.concatenate([x_forward, x_backward], axis=0)
    y_back_table = np.pad(y_back_table, ((0, 0), (0, z_back_table.shape[1] - y_back_table.shape[1])))
    table = np.concatenate([z_back_table, y_back_table], axis=0)
    columned = to_columns(sources, group)
    moved = carried[moved_at]
    columned, moved = lax.optimization_barrier((columned, moved))
    carried = (*carried[:moved_at], moved, *carried[moved_at + 1 :])
    solved_1, solved_2 = pl.pallas_call(
        functools.partial(solve_kernel, peers, intervals, planes, group, back),
        out_shape=(struct((devices * back, lanes)),) * 2,
        in_specs=[vmem, vmem, vmem],
        out_specs=(hbm, hbm),
        scratch_shapes=[
            pltpu.VMEM((devices * back, lanes), f32),
            pltpu.VMEM((devices * back, lanes), f32),
            pltpu.SemaphoreType.DMA((2, devices)),
        ],
        compiler_params=params_but(790),
        name="solve",
    )(columned, rates, x_table)
    spectra_2 = to_planes(solved_2, back)
    solved_1, *carried = lax.optimization_barrier((solved_1, *carried))
    zero = ((*carried, *zero[0]), zero[1])
    spectra_1 = to_planes(solved_1, back)
    outs = corrected(2, spectra_2, table, two, None, is_first)
    outs = corrected(0, later_interval(spectra_2), table, zero, outs, is_first)
    new_velocity, new_rhs = corrected(1, spectra_1, table, one, outs, is_first)
    return (new_velocity[None], new_rhs[None])


def solution(mesh):
    placed = P("tm", None, None, "space", None, None)
    return jax.shard_map(
        per_device,
        mesh=mesh,
        in_specs=(placed,),
        out_specs=(placed, placed),
        check_vma=False,
    )
```

```python
import functools

import jax
import jax.numpy as jnp
import ml_dtypes
import numpy as np
from jax import lax
from jax.experimental import pallas as pl
from jax.experimental.pallas import tpu as pltpu
from jax.sharding import PartitionSpec as P

viscosity = 1.0
coarse_viscosity = 10.0
time_step = 0.3
weights_first = (5.0 / 24.0, 1.0 / 3.0, -1.0 / 24.0)
weights_second = (-1.0 / 24.0, 1.0 / 3.0, 5.0 / 24.0)
half_step = 0.5 * time_step
first = tuple(time_step * w for w in weights_first)
second = tuple(time_step * w for w in weights_second)
lanes = 128
pad = 8
rows_at_once = 32


def params(kibibytes):
    return pltpu.CompilerParams(vmem_limit_bytes=kibibytes * 1024)


def params_but(kibibytes):
    return params(64 * 1024 - kibibytes)


f32 = jnp.float32
bf16 = jnp.bfloat16


def round_up(value, multiple):
    return -(-value // multiple) * multiple


def frequencies(length):
    index = np.arange(length)
    return np.where(index <= length // 2, index, index - length // 2)


def basis(length):
    index = np.arange(length)
    waves = frequencies(length)
    angles = 2.0 * np.pi * (waves[:, None] * index[None, :] % length) / length
    table = np.where(index[:, None] <= length // 2, np.cos(angles), np.sin(angles))
    edge = (waves == 0) | (2 * waves == length)
    return table * np.sqrt(np.where(edge, 1.0, 2.0) / length)[:, None]


def wave_squares(length):
    return np.sin(np.pi * frequencies(length) / length) ** 2


def refine_matrix(length):
    table = np.zeros((2 * length, length))
    for i in range(length):
        table[2 * i, i] += 1.0
        table[2 * i + 1, i] += 0.5
        table[2 * i + 1, (i + 1) % length] += 0.5
    return table


def pair_matrix(length):
    return np.repeat(np.eye(length), 2, axis=0)


def split(table):
    high = table.astype(np.float32).astype(ml_dtypes.bfloat16)
    low = (table - high.astype(np.float64)).astype(np.float32).astype(ml_dtypes.bfloat16)
    return high, low


def left_table(table):
    high, low = split(table)
    return np.concatenate([high, low, high], axis=1)


def right_table(table):
    high, low = split(table)
    return np.concatenate([high, low, high], axis=0)


def split_value(value):
    high = value.astype(bf16)
    return high, (value - high.astype(f32)).astype(bf16)


def left_dot(table, value):
    high, low = split_value(value)
    return jnp.dot(table, jnp.concatenate([high, high, low], axis=0), preferred_element_type=f32)


def right_dot(value, table):
    high, low = split_value(value)
    return jnp.dot(
        jnp.concatenate([high, high, low], axis=1), table, preferred_element_type=f32
    )


def start_all(copies):
    for copy in copies:
        copy.start()
    for copy in copies:
        copy.wait()


def wrap_rows(ref, plane, count):
    size = ref.shape[2] - 2 * pad
    for field in range(count):
        ref[field, plane, pad - 1 : pad, :] = ref[field, plane, pad + size - 1 : pad + size, :]
        ref[field, plane, pad + size : pad + size + 1, :] = ref[field, plane, pad : pad + 1, :]


def rhs_rows(ref, base, plane, start):
    stop = start + rows_at_once
    center = [ref[base + c, plane, start:stop, :] for c in range(3)]
    size = ref.shape[3]
    results = []
    for c in range(3):
        x_up = ref[base + c, plane + 1, start:stop, :]
        x_down = ref[base + c, plane - 1, start:stop, :]
        y_up = ref[base + c, plane, start + 1 : stop + 1, :]
        y_down = ref[base + c, plane, start - 1 : stop - 1, :]
        z_up = pltpu.roll(center[c], size - 1, 1)
        z_down = pltpu.roll(center[c], 1, 1)
        advect = (
            center[0] * (x_up - x_down) + center[1] * (y_up - y_down) + center[2] * (z_up - z_down)
        )
        laplace = (x_up + x_down) + (y_up + y_down) + (z_up + z_down) - 6.0 * center[c]
        results.append(viscosity * laplace - 0.5 * advect)
    return center, results


def planes_in(source, low, high, held, sems):
    length = source.shape[1]
    size = source.shape[2]
    rows = pl.ds(pad, size)

    def inner(plane):
        return pltpu.make_async_copy(
            source.at[:, plane], held.at[:, plane + 1, rows, :], sems.at[plane]
        )

    below = pltpu.make_async_copy(low, held.at[:, 0, rows, :], sems.at[length])
    above = pltpu.make_async_copy(high, held.at[:, length + 1, rows, :], sems.at[length + 1])
    return inner, below, above


def arrive(step, source, low, high, held, sems):
    length = source.shape[1]
    count = source.shape[0]
    inner, below, above = planes_in(source, low, high, held, sems)

    @pl.when(step == 0)
    def _():
        below.start()

        def launch(plane, carry):
            inner(plane).start()
            return carry

        lax.fori_loop(0, length, launch, 0)
        above.start()
        below.wait()
        inner(0).wait()
        wrap_rows(held, 1, count)

    inner(2 * step + 1).wait()
    wrap_rows(held, 2 * step + 2, count)

    @pl.when(2 * step + 2 < length)
    def _():
        inner(2 * step + 2).wait()
        wrap_rows(held, 2 * step + 3, count)

    @pl.when(2 * step + 2 >= length)
    def _():
        above.wait()


def chunks(size):
    return range(0, size, rows_at_once)


def transform(summed, z_table, y_table):
    count, half = len(summed), summed[0].shape[0]
    couples = []
    for k in range(0, count, 2):
        couples.append(jnp.concatenate([summed[k], summed[min(k + 1, count - 1)]], axis=1))
    in_z = right_dot(jnp.concatenate(couples, axis=0), z_table[...])
    in_z = [in_z[k * half : (k + 1) * half] for k in range(len(couples))]
    in_y = left_dot(y_table[...], jnp.concatenate(in_z, axis=1))
    blocks = half // 2
    lane = lax.broadcasted_iota(jnp.int32, (blocks, lanes), 1)
    results = []
    for k in range(count):
        both = in_y[:, (k // 2) * lanes : (k // 2 + 1) * lanes]
        upper, lower = both[:blocks], both[blocks:]
        if k % 2 == 0:
            results.append(jnp.where(lane < lanes // 2, upper, pltpu.roll(lower, lanes // 2, 1)))
        else:
            results.append(jnp.where(lane < lanes // 2, pltpu.roll(upper, lanes // 2, 1), lower))
    return results


def spectral(pairs, z_table, y_table, count):
    half = pairs.shape[1] // 2
    summed = [
        pairs[k, pl.ds(0, half, 2), :] + pairs[k, pl.ds(1, half, 2), :] for k in range(count)
    ]
    return transform(summed, z_table, y_table)


def sweep_one_kernel(is_first, source, low, high, s1, w, u, v, held, sems):
    step = pl.program_id(0)
    size = source.shape[2]
    arrive(step, source, low, high, held, sems)
    for row in chunks(size):
        rows = slice(row, row + rows_at_once)
        for part in range(2):
            plane = 2 * step + part + 1
            total_first, total_second, start, initial = None, None, None, None
            for node in range(3):
                center, old = rhs_rows(held, 3 * node, plane, pad + row)
                a, b = first[node], second[node] - (half_step if node == 1 else 0.0)
                if node == 0:
                    start, initial = center, old
                    total_first = [start[c] + a * old[c] for c in range(3)]
                    total_second = [b * old[c] for c in range(3)]
                else:
                    total_first = [total_first[c] + a * old[c] for c in range(3)]
                    total_second = [total_second[c] + b * old[c] for c in range(3)]
                if node == 0:
                    for c in range(3):
                        mine = first[0] * old[c] + is_first[0] * start[c]
                        other = second[0] * old[c]
                        if part == 1:
                            mine = mine + u[c, 0, rows, :]
                            other = other + v[c, 0, rows, :]
                        u[c, 0, rows, :] = mine
                        v[c, 0, rows, :] = other
            for c in range(3):
                s1[c, part, rows, :] = total_first[c]
                w[c, part, rows, :] = total_first[c] + total_second[c]
                u[c, 0, rows, :] = u[c, 0, rows, :] - total_first[c]
                v[c, 0, rows, :] = v[c, 0, rows, :] + total_first[c]


def sweep_two_kernel(
    group, source, low, high, w, u, v, z_table, y_table, s2, u_out, v_out, g, held, pairs, sems
):
    step = pl.program_id(0)
    size = source.shape[2]
    arrive(step, source, low, high, held, sems)
    for row in chunks(size):
        rows = slice(row, row + rows_at_once)
        fresh_sum, sweep_sum = None, None
        for part in range(2):
            _, fresh = rhs_rows(held, 0, 2 * step + part + 1, pad + row)
            swept = [w[c, part, rows, :] + half_step * fresh[c] for c in range(3)]
            for c in range(3):
                s2[c, part, rows, :] = swept[c]
            if part == 0:
                fresh_sum, sweep_sum = fresh, swept
            else:
                fresh_sum = [fresh_sum[c] + fresh[c] for c in range(3)]
                sweep_sum = [sweep_sum[c] + swept[c] for c in range(3)]
        for c in range(3):
            u_out[c, 0, rows, :] = u[c, 0, rows, :] + first[1] * fresh_sum[c]
            v_out[c, 0, rows, :] = v[c, 0, rows, :] + second[1] * fresh_sum[c] - sweep_sum[c]
            pairs[c, rows, :] = sweep_sum[c]
    planes = source.shape[1] // 2
    blocks = g.shape[0] // group
    for c, value in enumerate(spectral(pairs, z_table, y_table, 3)):
        g[pl.ds(c * planes + step, blocks, group), :] = value


def source_kernel(
    group, g_group, source, low, high, u, v, g, z_table, y_table, out, held, pairs, sems
):
    step = pl.program_id(0)
    size = source.shape[2]
    arrive(step, source, low, high, held, sems)
    for row in chunks(size):
        rows = slice(row, row + rows_at_once)
        _, fresh = rhs_rows(held, 0, 2 * step + 1, pad + row)
        _, other = rhs_rows(held, 0, 2 * step + 2, pad + row)
        for c in range(3):
            total = fresh[c] + other[c]
            pairs[c, rows, :] = u[c, 0, rows, :] + first[2] * total
            pairs[3 + c, rows, :] = v[c, 0, rows, :] + second[2] * total
    planes = source.shape[1] // 2
    blocks = out.shape[0] // group
    for k, value in enumerate(spectral(pairs, z_table, y_table, 6)):
        if k < 3:
            value = value + g[pl.ds(k * planes + step, blocks, g_group), :]
        out[pl.ds(k * planes + step, blocks, group), :] = value


def solve_kernel(
    peers, intervals, planes, group, back, values, inverse, table,
    sent_1, sent_2, out_1, out_2, out_sems
):
    sending = []
    rows_x = peers * planes
    start = [None] * 3
    for interval in range(intervals):
        loaded = []
        for field in range(6):
            parts = [
                values[
                    pl.ds(interval * group + field * planes + p, peers, intervals * group), :
                ]
                for p in range(planes)
            ]
            loaded.append(jnp.concatenate(parts, axis=0))
        spectra = left_dot(table[:rows_x, :], jnp.concatenate(loaded, axis=1))
        rates = inverse[...]
        wanted = []
        for field in range(6):
            c = field % 3
            value = spectra[:, field * lanes : (field + 1) * lanes]
            if start[c] is not None:
                value = value + start[c]
            start[c] = value * rates
            wanted.append(start[c])
        physical = left_dot(table[rows_x:, :], jnp.concatenate(wanted, axis=1))
        for field in range(6):
            out = (out_1, out_2)[field // 3]
            base = (field % 3) * (planes + 2)
            for e in range(planes + 2):
                out[pl.ds(interval * back + base + e, peers, intervals * back), :] = physical[
                    e * peers : (e + 1) * peers, field * lanes : (field + 1) * lanes
                ]
        for peer in range(peers):
            rows = pl.ds((peer * intervals + interval) * back, back)
            for k, (out, sent) in enumerate(((out_1, sent_1), (out_2, sent_2))):
                sem = out_sems.at[k, peer * intervals + interval]
                sending.append(pltpu.make_async_copy(out.at[rows], sent.at[rows], sem))
                sending[-1].start()
    for copy in sending:
        copy.wait()


def edges_kernel(source, low, high, held, sems):
    ends = (source.at[:, 0], low), (source.at[:, source.shape[1] - 1], high)
    arriving = [pltpu.make_async_copy(e[0], held.at[k], sems.at[k]) for k, e in enumerate(ends)]
    leaving = [pltpu.make_async_copy(held.at[k], e[1], sems.at[2 + k]) for k, e in enumerate(ends)]
    for copy in arriving:
        copy.start()
    for k in range(2):
        arriving[k].wait()
        leaving[k].start()
    for copy in leaving:
        copy.wait()


def sweep_one_plane(is_first, held, slot, put_s1, put_w, uv, cell):
    size = held.shape[2] - 2 * pad
    for row in chunks(size):
        rows = slice(row, row + rows_at_once)
        total_first, total_second = [], []
        for node in range(3):
            start, old = rhs_rows(held, 3 * node, slot, pad + row)
            a, b = first[node], second[node] - (half_step if node == 1 else 0.0)
            if node == 0:
                for c in range(3):
                    uv[c, cell, rows, :] += first[0] * old[c] + is_first[0] * start[c]
                    uv[3 + c, cell, rows, :] += second[0] * old[c]
                total_first = [start[c] + a * old[c] for c in range(3)]
                total_second = [b * old[c] for c in range(3)]
            else:
                total_first = [total_first[c] + a * old[c] for c in range(3)]
                total_second = [total_second[c] + b * old[c] for c in range(3)]
        for c in range(3):
            put_s1(c, row, total_first[c])
            put_w(c, row, total_first[c] + total_second[c])
            uv[c, cell, rows, :] -= total_first[c]
            uv[3 + c, cell, rows, :] += total_first[c]


def sweep_two_plane(held, slot, get_w, put_s2, uv, cell):
    size = held.shape[2] - 2 * pad
    for row in chunks(size):
        rows = slice(row, row + rows_at_once)
        _, fresh = rhs_rows(held, 0, slot, pad + row)
        for c in range(3):
            swept = get_w(c, row) + half_step * fresh[c]
            put_s2(c, row, swept)
            uv[c, cell, rows, :] += first[1] * fresh[c]
            uv[3 + c, cell, rows, :] += second[1] * fresh[c] - swept


def last_rhs_pair(held, slot, uv, cell):
    size = held.shape[2] - 2 * pad
    for row in chunks(size):
        rows = slice(row, row + rows_at_once)
        _, fresh = rhs_rows(held, 0, slot, pad + row)
        _, other = rhs_rows(held, 0, slot + 1, pad + row)
        for c in range(3):
            total = fresh[c] + other[c]
            uv[c, cell, rows, :] += first[2] * total
            uv[3 + c, cell, rows, :] += second[2] * total


def last_rhs_one(held, slot, uv, cell):
    size = held.shape[2] - 2 * pad
    for row in chunks(size):
        rows = slice(row, row + rows_at_once)
        _, fresh = rhs_rows(held, 0, slot, pad + row)
        for c in range(3):
            uv[c, cell, rows, :] += first[2] * fresh[c]
            uv[3 + c, cell, rows, :] += second[2] * fresh[c]


def uv_halves(uv, k, cell):
    half = uv.shape[2] // 2
    return uv[k, cell, pl.ds(0, half, 2), :] + uv[k, cell, pl.ds(1, half, 2), :]


def held_halves(held, c, slot):
    half = (held.shape[2] - 2 * pad) // 2
    total = held[c, slot, pl.ds(pad, half, 2), :] + held[c, slot, pl.ds(pad + 1, half, 2), :]
    total = total + held[c, slot + 1, pl.ds(pad, half, 2), :]
    return total + held[c, slot + 1, pl.ds(pad + 1, half, 2), :]


def interior_kernel(
    group, g_group, is_first, source, z_table, y_table,
    near, s1_out, s2_out, s2_side, w_out, uv_end, uv_next, out, g,
    held, held_1, held_2, w, uv, sems, out_sems
):
    length, size = source.shape[1], source.shape[2]
    planes = length // 2
    blocks = out.shape[0] // group
    rows_all = pl.ds(pad, size)

    def arriving(plane):
        return pltpu.make_async_copy(
            source.at[:, plane], held.at[:, plane, rows_all, :], sems.at[plane]
        )

    def launch(plane, carry):
        arriving(plane).start()
        return carry

    lax.fori_loop(0, length, launch, 0)
    uv[...] = jnp.zeros(uv.shape, f32)
    arriving(0).wait()
    arriving(1).wait()
    wrap_rows(held, 1, 9)

    def s1_copy(plane):
        return pltpu.make_async_copy(
            held_1.at[:, plane, rows_all, :], s1_out.at[:, plane - 1], out_sems.at[0, plane]
        )

    sides = (2, 3, length - 4, length - 3)

    def s2_copy(plane):
        inner = plane not in sides
        target = s2_out.at[:, plane - 4] if inner else s2_side.at[:, sides.index(plane)]
        return pltpu.make_async_copy(
            held_2.at[:, plane, rows_all, :], target, out_sems.at[1, plane]
        )

    def phase_one(plane, carry):
        arriving(plane + 1).wait()
        wrap_rows(held, plane + 1, 9)

        def put_s1(c, row, value):
            held_1[c, plane, pad + row : pad + row + rows_at_once, :] = value

        def put_w(c, row, value):
            w[c, plane, row : row + rows_at_once, :] = value

        sweep_one_plane(is_first, held, plane, put_s1, put_w, uv, plane // 2)
        wrap_rows(held_1, plane, 3)
        s1_copy(plane).start()
        return carry

    lax.fori_loop(1, length - 1, phase_one, 0)

    def phase_two(plane, carry):
        def get_w(c, row):
            return w[c, plane, row : row + rows_at_once, :]

        def put_s2(c, row, value):
            held_2[c, plane, pad + row : pad + row + rows_at_once, :] = value

        sweep_two_plane(held_1, plane, get_w, put_s2, uv, plane // 2)
        wrap_rows(held_2, plane, 3)
        return carry

    lax.fori_loop(2, length - 2, phase_two, 0)
    for plane in range(2, length - 2):
        s2_copy(plane).start()
    tails = []
    for k, plane in enumerate((0, 1, length - 2, length - 1)):
        tails.append(
            pltpu.make_async_copy(held.at[:, plane, rows_all, :], near.at[:, k], out_sems.at[2, 6 + k])
        )
    for k, plane in enumerate((1, length - 2)):
        tails.append(pltpu.make_async_copy(w.at[:, plane], w_out.at[:, k], out_sems.at[2, k]))
    for k, cell in enumerate((0, planes - 1)):
        tails.append(pltpu.make_async_copy(uv.at[:, cell], uv_end.at[:, k], out_sems.at[2, 2 + k]))
    for k, cell in enumerate((1, planes - 2)):
        tails.append(pltpu.make_async_copy(uv.at[:, cell], uv_next.at[:, k], out_sems.at[2, 4 + k]))
    for copy in tails:
        copy.start()

    def phase_three(cell, carry):
        last_rhs_pair(held_2, 2 * cell, uv, cell)
        return carry

    lax.fori_loop(2, planes - 2, phase_three, 0)
    for start in range(2, planes - 2, 2):
        cells = range(start, min(start + 2, planes - 2))
        entries = [(k, cell) for cell in cells for k in range(6)]
        values = transform([uv_halves(uv, k, cell) for k, cell in entries], z_table, y_table)
        for (k, cell), value in zip(entries, values):
            out[pl.ds(k * planes + cell, blocks, group), :] = value
    for start in range(1, planes - 1, 4):
        cells = range(start, min(start + 4, planes - 1))
        entries = [(c, cell) for cell in cells for c in range(3)]
        values = transform([held_halves(held_2, c, 2 * cell) for c, cell in entries], z_table, y_table)
        for (c, cell), value in zip(entries, values):
            g[pl.ds(c * planes + cell, blocks, g_group), :] = value

    def finish_one(plane, carry):
        s1_copy(plane).wait()
        return carry

    lax.fori_loop(1, length - 1, finish_one, 0)
    for plane in range(2, length - 2):
        s2_copy(plane).wait()
    for copy in tails:
        copy.wait()


def end_one_kernel(
    is_first, near, low, high, uv_in, low_out, high_out, w_out, uv, held, sems
):
    size = near.shape[2]
    rows_all = pl.ds(pad, size)
    sources = [low, *[near.at[:, k] for k in range(4)], high]
    start_all([
        pltpu.make_async_copy(ref, held.at[:, slot, rows_all, :], sems.at[slot])
        for slot, ref in enumerate(sources)
    ])
    uv[...] = uv_in[...]
    for k, (slot, ref) in enumerate(((1, low_out), (4, high_out))):
        wrap_rows(held, slot, 9)

        def put_s1(c, row, value):
            ref[c, row : row + rows_at_once, :] = value

        def put_w(c, row, value):
            w_out[c, k, row : row + rows_at_once, :] = value

        sweep_one_plane(is_first, held, slot, put_s1, put_w, uv, k)


def end_two_kernel(
    g_group, swept, low, low_end, high_end, high, w_end, w_next, uv_in, z_table, y_table,
    low_out, high_out, next_out, uv, g, held, held_2, sems
):
    count, size = swept.shape[1], swept.shape[2]
    rows_all = pl.ds(pad, size)
    sources = [low, low_end, swept.at[:, 0], swept.at[:, 1]]
    sources += [swept.at[:, count - 2], swept.at[:, count - 1], high_end, high]
    start_all([
        pltpu.make_async_copy(ref, held.at[:, slot, rows_all, :], sems.at[slot])
        for slot, ref in enumerate(sources)
    ])
    uv[...] = uv_in[...]
    places = ((1, 0, w_end, 0), (2, 0, w_next, 0), (5, 1, w_next, 1), (6, 1, w_end, 1))
    for index, (slot, cell, w, k) in enumerate(places):
        wrap_rows(held, slot, 3)

        def get_w(c, row):
            return w[c, k, row : row + rows_at_once, :]

        def put_s2(c, row, value):
            rows = slice(row, row + rows_at_once)
            if slot == 1:
                low_out[c, rows, :] = value
            elif slot == 6:
                high_out[c, rows, :] = value
            else:
                next_out[c, k, rows, :] = value
            held_2[c, index, pad + row : pad + row + rows_at_once, :] = value

        sweep_two_plane(held, slot, get_w, put_s2, uv, cell)
    blocks = g.shape[0] // g_group
    entries = [(c, k) for k in range(2) for c in range(3)]
    values = transform([held_halves(held_2, c, 2 * k) for c, k in entries], z_table, y_table)
    for (c, k), value in zip(entries, values):
        g[pl.ds(2 * c + k, blocks, g_group), :] = value


def middle_kernel(
    group, swept, side, low_end, nexts, high_end, uv_in, uv_next, f, z_table, y_table,
    uv, out, held, near, sems
):
    count, size = swept.shape[1], swept.shape[2]
    planes = (count + 8) // 2
    rows_all = pl.ds(pad, size)
    sources = [low_end, nexts.at[:, 0], side.at[:, 0], side.at[:, 1], swept.at[:, 0]]
    sources += [swept.at[:, count - 1], side.at[:, 2], side.at[:, 3], nexts.at[:, 1], high_end]
    start_all([
        pltpu.make_async_copy(ref, held.at[:, slot, rows_all, :], sems.at[slot])
        for slot, ref in enumerate(sources)
    ])
    uv[...] = uv_in[...]
    near[...] = uv_next[...]
    out[...] = f[...]
    for slot in (1, 2, 3, 6, 7, 8):
        wrap_rows(held, slot, 3)
    last_rhs_one(held, 1, uv, 0)
    last_rhs_one(held, 8, uv, 1)
    last_rhs_pair(held, 2, near, 0)
    last_rhs_pair(held, 6, near, 1)
    blocks = out.shape[0] // group
    entries = [(k, index) for index in range(2) for k in range(6)]
    values = transform([uv_halves(near, k, index) for k, index in entries], z_table, y_table)
    for (k, index), value in zip(entries, values):
        out[pl.ds(k * planes + (1, planes - 2)[index], blocks, group), :] = value


def end_three_kernel(
    group, g_group, end_group, side, low, low_end, nexts, high_end, high, uv_in, f, g, g_end,
    z_table, y_table, pack, sent, out, held, side_held, uv, sems, out_sems
):
    size = held.shape[2] - 2 * pad
    rows_all = pl.ds(pad, size)
    blocks = out.shape[0] // group
    planes = g.shape[0] // blocks // 3
    sources = [low, low_end, nexts.at[:, 0], nexts.at[:, 1], high_end, high]
    side_in = pltpu.make_async_copy(side, side_held, sems.at[6])
    side_in.start()
    start_all([
        pltpu.make_async_copy(ref, held.at[:, slot, rows_all, :], sems.at[slot])
        for slot, ref in enumerate(sources)
    ])
    packing = [
        pltpu.make_async_copy(
            held.at[:, slot, rows_all, :], pack.at[:, (0, 1, 2, 7, 8, 9)[slot]], out_sems.at[slot]
        )
        for slot in range(6)
    ]
    packing.append(pltpu.make_async_copy(side_held, pack.at[:, 3:7], out_sems.at[7]))
    uv[...] = uv_in[...]
    out[...] = f[...]
    for slot in (1, 4):
        wrap_rows(held, slot, 3)
    side_in.wait()
    for copy in packing:
        copy.start()
    last_rhs_one(held, 1, uv, 0)
    last_rhs_one(held, 4, uv, 1)
    entries = [(k, index) for index in range(2) for k in range(6)]
    values = transform([uv_halves(uv, k, index) for k, index in entries], z_table, y_table)
    for (k, index), value in zip(entries, values):
        if k < 3:
            value = value + g_end[pl.ds(2 * k + index, blocks, end_group), :]
        out[pl.ds(k * planes + index * (planes - 1), blocks, group), :] = value
    for k in range(3):
        for cell in range(1, planes - 1):
            out[pl.ds(k * planes + cell, blocks, group), :] += g[
                pl.ds(k * planes + cell, blocks, g_group), :
            ]
    start_all([pltpu.make_async_copy(out, sent, out_sems.at[6])])
    for copy in packing:
        copy.wait()


def place(fields, layouts, is_first, staged, sems):
    def launch(layout):
        for slot, (number, index) in enumerate(layout):
            ref = fields[number]
            ref = ref.at[0:3, index] if index is not None else ref.at[0:3]
            pltpu.make_async_copy(ref, staged.at[:, slot], sems.at[slot]).start()

    if len(layouts) > 1:
        pl.when(is_first[0] > 0)(functools.partial(launch, layouts[0]))
        pl.when(is_first[0] <= 0)(functools.partial(launch, layouts[1]))
    else:
        launch(layouts[0])


def corrected_kernel(node, group, layouts, count, is_first, spectra, table, *refs):
    new_velocity, new_rhs, held, staged, coarse, result, sems, out_sems, rhs_sems = refs[-9:]
    place(refs[:count], layouts, is_first, staged, sems)
    length, size = staged.shape[1] - 2, staged.shape[2]
    planes = length // 2
    rows_all = pl.ds(pad, size)
    z_rows = 3 * lanes
    y_rows, y_columns = size, 3 * size // 2
    blocks = spectra.shape[0] // group
    for c in range(3):
        base = c * (planes + 2)
        parts = [spectra[pl.ds(base + e, blocks, group), :] for e in range(planes + 2)]
        in_z = right_dot(jnp.concatenate(parts, axis=0), table[:z_rows, :])
        for e in range(0, planes + 2, 2):
            stacked = []
            for k in (e, min(e + 1, planes + 1)):
                mine = in_z[k * blocks : (k + 1) * blocks]
                stacked.append(jnp.concatenate([mine[:, :size], mine[:, size:]], axis=0))
            both = left_dot(
                table[z_rows : z_rows + y_rows, :y_columns], jnp.concatenate(stacked, axis=1)
            )
            for k in range(min(2, planes + 2 - e)):
                coarse[c, e + k] = both[:, k * size : (k + 1) * size]

    def out_copy(plane):
        return pltpu.make_async_copy(
            held.at[:, plane + 1, rows_all, :], new_velocity.at[node, :, plane], out_sems.at[plane]
        )

    def rhs_copy(plane):
        return pltpu.make_async_copy(
            result.at[:, plane], new_rhs.at[node, :, plane], rhs_sems.at[plane]
        )

    def correct(plane, cell, odd):
        pltpu.make_async_copy(staged.at[:, plane], staged.at[:, plane], sems.at[plane]).wait()
        for field in range(3):
            for row in chunks(size):
                rows = slice(row, row + rows_at_once)
                held_rows = slice(pad + row, pad + row + rows_at_once)
                value = coarse[field, cell, rows, :]
                if odd:
                    value = 0.5 * (value + coarse[field, cell + 1, rows, :])
                held[field, plane, held_rows, :] = staged[field, plane, rows, :] + value
        wrap_rows(held, plane, 3)

    correct(0, 0, True)
    correct(1, 1, False)
    out_copy(0).start()

    def body(q, carry):
        correct(2 * q + 2, q + 1, True)
        correct(2 * q + 3, q + 2, False)
        out_copy(2 * q + 1).start()

        @pl.when(2 * q + 2 < length)
        def _():
            out_copy(2 * q + 2).start()

        for part in range(2):
            plane = 2 * q + part
            for row in chunks(size):
                _, fresh = rhs_rows(held, 0, plane + 1, pad + row)
                for c in range(3):
                    result[c, plane, row : row + rows_at_once, :] = fresh[c].astype(bf16)
            rhs_copy(plane).start()
        return carry

    lax.fori_loop(0, planes, body, 0)

    def finish(plane, carry):
        out_copy(plane).wait()
        rhs_copy(plane).wait()
        return carry

    lax.fori_loop(0, length, finish, 0)


anywhere = pl.BlockSpec(memory_space=pl.ANY)
scalar = pl.BlockSpec(memory_space=pltpu.SMEM)
vmem = pl.BlockSpec(memory_space=pltpu.VMEM)
hbm = pl.BlockSpec(memory_space=pltpu.HBM)


def whole(shape):
    return pl.BlockSpec(shape, lambda *index: (0,) * len(shape))


def struct(shape, dtype=f32):
    return jax.ShapeDtypeStruct(shape, dtype)


def slab(shape):
    return pl.BlockSpec(shape, lambda q: (0, q, 0, 0))


def held_planes(count, length, size_y, size_z):
    return pltpu.VMEM((count, length + 2, size_y + 2 * pad, size_z), f32)


def neighbours(low_plane, high_plane):
    count = lax.axis_size("space")
    up = [(i, (i + 1) % count) for i in range(count)]
    down = [(j, i) for i, j in up]
    return lax.ppermute(high_plane, "space", up), lax.ppermute(low_plane, "space", down)


def later_interval(value):
    count = lax.axis_size("tm")
    return lax.ppermute(value, "tm", [(i, i + 1) for i in range(count - 1)])


def corrected(node, spectra, table, placed, outs, is_first):
    fields, layouts = placed
    group, slots, (size_y, size_z) = spectra.shape[1], len(layouts[0]), fields[0].shape[-2:]
    length, planes = slots - 2, slots // 2 - 1
    operands = [is_first, spectra.reshape(-1, lanes), table, *fields]
    specs = [scalar, vmem, vmem] + [anywhere] * len(fields)
    shape = (3, 3, length, size_y, size_z)
    aliases = {}
    if outs is not None:
        aliases = {len(operands): 0, len(operands) + 1: 1}
        operands, specs = [*operands, *outs], specs + [hbm] * 2
    return pl.pallas_call(
        functools.partial(corrected_kernel, node, group, layouts, len(fields)),
        out_shape=(struct(shape), struct(shape, bf16)),
        in_specs=specs,
        out_specs=(hbm, hbm),
        input_output_aliases=aliases,
        scratch_shapes=[
            held_planes(3, length, size_y, size_z),
            pltpu.VMEM((3, slots, size_y, size_z), f32),
            pltpu.VMEM((3, planes + 2, size_y, size_z), f32),
            pltpu.VMEM((3, length, size_y, size_z), bf16),
            pltpu.SemaphoreType.DMA((slots,)),
            pltpu.SemaphoreType.DMA((length,)),
            pltpu.SemaphoreType.DMA((length,)),
        ],
        compiler_params=params_but(560),
        name=f"corrected_{node}",
    )(*operands)


def sweep_whole(fields, is_first, z_table, y_table, blocks):
    length, size_y, size_z = fields.shape[1:]
    planes = length // 2
    low, high = neighbours(fields[:, 0], fields[:, length - 1])
    fine = (3, length, size_y, size_z)
    halved = (3, planes, size_y, size_z)
    two = (3, 2, size_y, size_z)
    one = (3, 1, size_y, size_z)
    in_sems = pltpu.SemaphoreType.DMA((length + 2,))
    swept_1, w, u, v = pl.pallas_call(
        sweep_one_kernel,
        grid=(planes,),
        out_shape=(struct(fine), struct(fine), struct(halved), struct(halved)),
        in_specs=[scalar, anywhere, anywhere, anywhere],
        out_specs=(slab(two), slab(two), slab(one), slab(one)),
        scratch_shapes=[held_planes(9, length, size_y, size_z), in_sems],
        compiler_params=params(40960),
        name="sweep_one",
    )(is_first, fields, low, high)
    low_1, high_1 = neighbours(swept_1[:, 0], swept_1[:, length - 1])

    g_group = round_up(3 * planes, 8)
    swept_2, u, v, g = pl.pallas_call(
        functools.partial(sweep_two_kernel, g_group),
        grid=(planes,),
        out_shape=(struct(fine), struct(halved), struct(halved), struct((blocks * g_group, lanes))),
        in_specs=[anywhere, anywhere, anywhere, slab(two), slab(one), slab(one)]
        + [whole(z_table.shape), whole(y_table.shape)],
        out_specs=(slab(two), slab(one), slab(one), whole((blocks * g_group, lanes))),
        scratch_shapes=[
            held_planes(3, length, size_y, size_z),
            pltpu.VMEM((3, size_y, size_z), f32),
            in_sems,
        ],
        compiler_params=params(40960),
        name="sweep_two",
    )(swept_1, low_1, high_1, w, u, v, z_table, y_table)
    low_2, high_2 = neighbours(swept_2[:, 0], swept_2[:, length - 1])
    g = later_interval(g)

    group = round_up(6 * planes, 8)
    sources = pl.pallas_call(
        functools.partial(source_kernel, group, g_group),
        grid=(planes,),
        out_shape=struct((blocks * group, lanes)),
        in_specs=[anywhere, anywhere, anywhere, slab(one), slab(one), whole(g.shape)]
        + [whole(z_table.shape), whole(y_table.shape)],
        out_specs=whole((blocks * group, lanes)),
        scratch_shapes=[
            held_planes(3, length, size_y, size_z),
            pltpu.VMEM((6, size_y, size_z), f32),
            in_sems,
        ],
        compiler_params=params(40960),
        name="sources",
    )(swept_2, low_2, high_2, u, v, g, z_table, y_table)
    layout = tuple([(0, None)] + [(1, p) for p in range(length)] + [(2, None)])
    carried = [later_interval(value) for value in (low_2, swept_2, high_2)]
    own = tuple((3 + number, index) for number, index in layout)
    return (
        sources,
        ((low_1, swept_1, high_1), (layout,)),
        ((low_2, swept_2, high_2), (layout,)),
        tuple(carried),
        ((low, fields, high), (own, layout)),
    )


def sweep_split(fields, is_first, z_table, y_table, blocks):
    length, size_y, size_z = fields.shape[1:]
    planes = length // 2
    plane, g_group, group = (size_y, size_z), round_up(3 * planes, 8), round_up(6 * planes, 8)

    def held(count, slots):
        return pltpu.VMEM((count, slots, size_y + 2 * pad, size_z), f32)

    def sems(*shape):
        return pltpu.SemaphoreType.DMA(shape)

    low, high = pl.pallas_call(
        edges_kernel,
        out_shape=(struct((9, *plane)),) * 2,
        in_specs=[hbm],
        out_specs=(hbm,) * 2,
        scratch_shapes=[pltpu.VMEM((2, 9, *plane), f32), sems(4)],
        compiler_params=params_but(300),
        name="edges",
    )(fields)
    low, high = neighbours(low, high)
    near, swept_1, swept_2, side_2, w_next, uv_end, uv_next, f, g = pl.pallas_call(
        functools.partial(interior_kernel, group, g_group),
        out_shape=(
            struct((9, 4, *plane)),
            struct((3, length - 2, *plane)),
            struct((3, length - 8, *plane)),
            struct((3, 4, *plane)),
            struct((3, 2, *plane)),
            struct((6, 2, *plane)),
            struct((6, 2, *plane)),
            struct((blocks * group, lanes)),
            struct((blocks * g_group, lanes)),
        ),
        in_specs=[scalar, hbm, vmem, vmem],
        out_specs=(hbm,) * 7 + (vmem,) * 2,
        scratch_shapes=[
            held(9, length),
            held(3, length),
            held(3, length),
            pltpu.VMEM((3, length, *plane), f32),
            pltpu.VMEM((6, planes, *plane), f32),
            sems(length),
            sems(3, max(length, 10)),
        ],
        compiler_params=params(40960),
        cost_estimate=pl.CostEstimate(flops=4 * 10**9, bytes_accessed=6 * 10**7, transcendentals=0),
        name="interior",
    )(is_first, fields, z_table, y_table)
    g_moved = later_interval(g)
    low_end_1, high_end_1, w_end, uv_end = pl.pallas_call(
        end_one_kernel,
        out_shape=(
            struct((3, *plane)),
            struct((3, *plane)),
            struct((3, 2, *plane)),
            struct((6, 2, *plane)),
        ),
        in_specs=[scalar, anywhere, anywhere, anywhere, vmem],
        out_specs=(vmem,) * 4,
        scratch_shapes=[held(9, 6), sems(6)],
        compiler_params=params(16384),
        name="end_one",
    )(is_first, near, low, high, uv_end)
    low_1, high_1 = neighbours(low_end_1, high_end_1)
    end_group = 8
    low_end_2, high_end_2, next_2, uv_end, g_end = pl.pallas_call(
        functools.partial(end_two_kernel, end_group),
        out_shape=(
            struct((3, *plane)),
            struct((3, *plane)),
            struct((3, 2, *plane)),
            struct((6, 2, *plane)),
            struct((blocks * end_group, lanes)),
        ),
        in_specs=[hbm] + [anywhere] * 4 + [vmem] * 5,
        out_specs=(vmem,) * 5,
        scratch_shapes=[held(3, 8), held(3, 4), sems(8)],
        compiler_params=params(16384),
        name="end_two",
    )(swept_1, low_1, low_end_1, high_end_1, high_1, w_end, w_next, uv_end, z_table, y_table)
    low_2, high_2 = neighbours(low_end_2, high_end_2)
    uv_end, f = pl.pallas_call(
        functools.partial(middle_kernel, group),
        out_shape=(struct((6, 2, *plane)), struct((blocks * group, lanes))),
        in_specs=[hbm, hbm] + [anywhere] * 3 + [vmem] * 5,
        out_specs=(vmem,) * 2,
        scratch_shapes=[held(3, 10), pltpu.VMEM((6, 2, *plane), f32), sems(10)],
        compiler_params=params(16384),
        name="middle",
    )(swept_2, side_2, low_end_2, next_2, high_end_2, uv_end, uv_next, f, z_table, y_table)
    pack, sources = pl.pallas_call(
        functools.partial(end_three_kernel, group, g_group, end_group),
        out_shape=(struct((3, 10, *plane)), struct((blocks * group, lanes))),
        in_specs=[hbm] + [anywhere] * 5 + [vmem] * 6,
        out_specs=(hbm, hbm),
        scratch_shapes=[
            pltpu.VMEM((blocks * group, lanes), f32),
            held(3, 6),
            pltpu.VMEM((3, 4, *plane), f32),
            pltpu.VMEM((6, 2, *plane), f32),
            sems(7),
            sems(8),
        ],
        compiler_params=params(16384),
        name="end_three",
    )(
        side_2, low_2, low_end_2, next_2, high_end_2, high_2, uv_end, f,
        g_moved, later_interval(g_end), z_table, y_table
    )
    inner_1 = [(2, p) for p in range(length - 2)]
    inner_2 = [(1, p) for p in range(length - 8)]
    layout_1 = [(0, None), (1, None)] + inner_1 + [(3, None), (4, None)]
    layout_2 = [(0, p) for p in range(5)] + inner_2 + [(0, p) for p in range(5, 10)]
    layout_0 = [(2, None)] + [(3, p) for p in range(length)] + [(4, None)]
    return (
        sources,
        ((low_1, low_end_1, swept_1, high_end_1, high_1), (tuple(layout_1),)),
        ((pack, swept_2), (tuple(layout_2),)),
        (later_interval(pack), later_interval(swept_2)),
        ((low, fields, high), (tuple(layout_0), tuple(layout_2))),
    )


def per_device(velocity):
    length, size_y, size_z = velocity.shape[3:]
    planes = length // 2
    peers, intervals = lax.axis_size("space"), lax.axis_size("tm")
    devices = peers * intervals
    coarse_x, coarse_y, coarse_z = peers * planes, size_y // 2, size_z // 2
    blocks = coarse_y * coarse_z // lanes
    per_block = devices // blocks
    columns = lanes // per_block
    device = lax.axis_index("space") * intervals + lax.axis_index("tm")
    tm_first = lax.axis_index("tm") == 0
    fields = velocity.reshape(9, length, size_y, size_z)

    x_basis, y_basis, z_basis = basis(coarse_x), basis(coarse_y), basis(coarse_z)
    z_forward = 0.25 * pair_matrix(coarse_z) @ z_basis.T
    z_table = right_table(np.kron(np.eye(2), z_forward))
    y_table = left_table(0.5 * y_basis)
    order = np.arange(coarse_x).reshape(peers, planes).T.reshape(-1)
    x_forward = left_table(x_basis[:, order])
    wanted_x = np.arange(peers)[None, :] * planes + np.arange(-1, planes + 1)[:, None]
    x_backward = left_table(x_basis.T[wanted_x.reshape(-1) % coarse_x])
    z_back = (refine_matrix(coarse_z) @ z_basis.T).T
    z_back_table = right_table(np.kron(np.eye(2), z_back))
    y_back_table = left_table(refine_matrix(coarse_y) @ y_basis.T)
    y_of = np.arange(2)[:, None] * blocks + np.arange(blocks)[None, :]
    waves = wave_squares(coarse_y)[y_of.T][:, :, None] + wave_squares(coarse_z)[None, None, :]
    waves = waves.reshape(devices, columns)
    waves = np.pad(waves, ((0, 0), (0, lanes - columns)))
    mine = lax.dynamic_slice_in_dim(jnp.asarray(waves, f32), device, 1, axis=0)
    total = jnp.asarray(wave_squares(coarse_x), f32)[:, None] + mine
    rates = 1.0 / (1.0 + half_step * coarse_viscosity * (4.0 / (2.0 * 2.0)) * total)

    is_first = tm_first.astype(f32).reshape(1)
    sweep = sweep_split if length >= 12 else sweep_whole
    moved_at = 1
    sources, one, two, carried, zero = sweep(fields, is_first, z_table, y_table, blocks)
    group = round_up(6 * planes, 8)

    both = ("space", "tm")

    def to_columns(value, rows):
        if per_block > 1:
            value = value.reshape(blocks, rows, per_block, columns).swapaxes(1, 2)
        value = value.reshape(devices, rows, columns)
        value = lax.all_to_all(value, both, split_axis=0, concat_axis=0, tiled=True)
        value = jnp.pad(value, ((0, 0), (0, 0), (0, lanes - columns)))
        return value.reshape(devices * rows, lanes)

    def to_planes(value, rows):
        value = value.reshape(devices, rows, lanes)[:, :, :columns]
        value = lax.all_to_all(value, both, split_axis=0, concat_axis=0, tiled=True)
        if per_block > 1:
            value = value.reshape(blocks, per_block, rows, columns).swapaxes(1, 2)
        return value.reshape(blocks, rows, lanes)

    back = round_up(3 * (planes + 2), 8)
    x_table = np.concatenate([x_forward, x_backward], axis=0)
    y_back_table = np.pad(y_back_table, ((0, 0), (0, z_back_table.shape[1] - y_back_table.shape[1])))
    table = np.concatenate([z_back_table, y_back_table], axis=0)
    columned = to_columns(sources, group)
    moved = carried[moved_at]
    columned, moved = lax.optimization_barrier((columned, moved))
    carried = (*carried[:moved_at], moved, *carried[moved_at + 1 :])
    solved_1, solved_2 = pl.pallas_call(
        functools.partial(solve_kernel, peers, intervals, planes, group, back),
        out_shape=(struct((devices * back, lanes)),) * 2,
        in_specs=[vmem, vmem, vmem],
        out_specs=(hbm, hbm),
        scratch_shapes=[
            pltpu.VMEM((devices * back, lanes), f32),
            pltpu.VMEM((devices * back, lanes), f32),
            pltpu.SemaphoreType.DMA((2, devices)),
        ],
        compiler_params=params_but(790),
        name="solve",
    )(columned, rates, x_table)
    spectra_2 = to_planes(solved_2, back)
    solved_1, *carried = lax.optimization_barrier((solved_1, *carried))
    zero = ((*carried, *zero[0]), zero[1])
    spectra_1 = to_planes(solved_1, back)
    outs = corrected(2, spectra_2, table, two, None, is_first)
    outs = corrected(0, later_interval(spectra_2), table, zero, outs, is_first)
    new_velocity, new_rhs = corrected(1, spectra_1, table, one, outs, is_first)
    return (new_velocity[None], new_rhs[None])


def solution(mesh):
    placed = P("tm", None, None, "space", None, None)
    return jax.shard_map(
        per_device,
        mesh=mesh,
        in_specs=(placed,),
        out_specs=(placed, placed),
        check_vma=False,
    )
```
